32 devices in a mesh: groups: 2 (over y), expert: 4 (over z), dp: 4 (over x, core).
Axes of the slice: x: 2, y: 2, z: 4, core: 2. Of those that a mesh axis runs over, the one named last changes fastest.
Arguments:
- tokens: bfloat16 [512, 6144], P(('groups', 'expert'), 'dp'), parts along dimension 0, may hold values from -6 to 6
- expert_ids: int32 [512, 8], P(('groups', 'expert')), parts along dimension 0, may hold values from 0 to 31, all different within a row; in each aligned block of 64 rows (0 to 63, 64 to 127, ...) at most 32 rows name the same one
- scores: float32 [512, 8], P(('groups', 'expert')), parts along dimension 0, may hold values from -8 to 8
- w_gate: bfloat16 [32, 6144, 1024], P('expert', 'dp'), may hold values from -0.078125 to 0.078125
- w_up: bfloat16 [32, 6144, 1024], P('expert', 'dp'), may hold values from -0.078125 to 0.078125
- w_down: bfloat16 [32, 1024, 6144], P('expert', None, 'dp'), may hold values from -0.1875 to 0.1875
Outputs:
- mixed: bfloat16 [512, 6144], P(('groups', 'expert'), 'dp'), parts along dimension 0
The draws below stay inside these ranges and needn't reach their ends.
There are 2 independent parts, one for each index of `groups`. The reference program is written for one: setup_inputs(seed, part) draws one part's arguments, and reference() takes and returns one part's arrays. A program takes and returns all parts, laid end to end along the dimension named above; an argument that names none is the same for every part. Nothing has to cross between parts.
Inputs may be any that keep to these rules, and one draw needn't show every extreme that they name: `expert_ids`: each row names 8 different experts; among the rows of one index of expert (aligned blocks of 64 rows) no expert is named by more than 32 rows, a bound that some block reaches.
All inputs are finite; a program needn't handle non-finite values.
Results may differ from the reference program's by a relative error of at most 0.024.
Values may be sent and summed in bfloat16 or wider, within the bound.
No kernel may reach another device: no remote copies, remote signals or barrier semaphores. Data moves between devices by JAX's collectives and lax.ppermute only.
A program may use at most 128 MiB of HBM per device.

```python
import math
import jax
import jax.numpy as jnp
import numpy as np
from jax import lax

D = 6144
H = 1024
EXPERTS = 32
TOP = 8
TOK_DEV = 64
CAP = 32
TOKENS = 256
N_EXPERT = 4
N_DP = 4


def levels(own_key, dims, split, low, top_value):
    factor_of = 1.0
    for position, blocks in split:
        heights = jax.random.uniform(jax.random.fold_in(jax.random.fold_in(own_key, 6), position), (blocks,), jnp.float32, low / len(split), top_value / len(split))
        factor_of = factor_of * jnp.repeat(jnp.exp(heights), dims[position] // blocks).reshape((-1,) + (1,) * (len(dims) - 1 - position))
    return factor_of


def shared_out(rng, own, number, rows, number_of, top, limit, skew):
    order = jax.random.permutation(rng, number_of)
    packed, usual = load_shares(number_of, rows * top, limit, skew, True), load_shares(number_of, rows * top, limit, skew, False)
    places = jnp.arange(number_of)

    def named(tallies, offset_by):
        used = int((tallies > 0).sum())
        fixed = max(1, used // 4)
        moved = fixed + (places - fixed + offset_by * (used - fixed)) % max(1, number_of - fixed)
        return jnp.zeros((number_of,), jnp.int32).at[order[jnp.where(places < fixed, places, moved)]].set(jnp.asarray(tallies, jnp.int32))

    tallies = jnp.where(number % 4 == 0, named(packed, number // 4), named(usual, number - number // 4 - 1))
    mixed = jax.random.permutation(jax.random.fold_in(own, 3), number_of)
    donor, sink = mixed[0:number_of // 2 * 2:2], mixed[1:number_of // 2 * 2:2]
    room = jnp.minimum(tallies[donor] - 1, limit - tallies[sink]) // 2
    room = jnp.where((donor == order[0]) | (sink == order[0]) | (tallies[sink] == 0), 0, jnp.maximum(room, 0))
    moved = jax.random.randint(jax.random.fold_in(own, 4), (number_of // 2,), 0, 1 << 20) % (room + 1)
    tallies = tallies.at[donor].add(-moved).at[sink].add(moved)
    members = jnp.searchsorted(jnp.cumsum(tallies), jnp.arange(rows * top), side="right").astype(jnp.int32)
    grid = members.reshape(top, rows).T
    grid = grid[jax.random.permutation(jax.random.fold_in(own, 1), rows)]
    offset_by = jax.random.randint(jax.random.fold_in(own, 2), (rows, 1), 0, top)
    return jnp.take_along_axis(grid, (jnp.arange(top)[None, :] + offset_by) % top, axis=1)


def load_shares(count, total, limit, slope, full):
    weights = [(1 << 20) // math.isqrt(rank ** slope) + 1 for rank in range(1, count + 1)]
    largest = limit if full else min(limit, max(-(-total // count), total * weights[0] // sum(weights)))
    least = 1 if total - largest >= count - 1 else 0
    counts, spare = [largest] + [least] * (count - 1), total - largest - least * (count - 1)
    while spare > 0:
        movable = [i for i in range(1, count) if counts[i] < largest] or [i for i in range(1, count) if counts[i] < limit]
        whole, remaining = sum([weights[i] for i in movable]), spare
        for i in movable:
            more = min(limit - counts[i], max(1, remaining * weights[i] // whole), spare)
            counts[i] = counts[i] + more
            spare = spare - more
    return np.array(counts)


def bell_draw(stream_key, shape, deviation, most, split=(), kind=jnp.bfloat16):
    result = deviation * jax.random.normal(stream_key, shape, jnp.float32)
    if split:
        result = result * levels(stream_key, shape, split, -0.22, 0.18)
    return jnp.clip(result, -most, most).astype(kind)


def setup_inputs(seed: int = 0, part: int = 0) -> dict:
    keys = jax.random.split(jax.random.key(seed), 7)
    own_keys = jax.random.split(jax.random.fold_in(keys[6], part), 7)
    tokens = bell_draw(own_keys[0], (TOKENS, D), 1.0, 6.0, ((0, 4), (1, 4)))
    expert_ids_keys = jax.random.split(jax.random.fold_in(own_keys[1], 1), TOKENS // TOK_DEV)
    expert_ids_turns = jax.random.permutation(jax.random.fold_in(own_keys[1], 3), TOKENS // TOK_DEV)
    expert_ids = jax.vmap(lambda own, number: shared_out(jax.random.fold_in(own_keys[1], 2), own, number, TOK_DEV, EXPERTS, TOP, CAP, 2))(expert_ids_keys, expert_ids_turns).reshape((TOKENS, TOP))
    scores = bell_draw(own_keys[2], (TOKENS, TOP), 2.0, 8.0, ((0, 4),), jnp.float32)
    w_gate = bell_draw(keys[3], (EXPERTS, D, H), D ** -0.5, 0.078125, ((0, 4), (1, 4)))
    w_up = bell_draw(keys[4], (EXPERTS, D, H), D ** -0.5, 0.078125, ((0, 4), (1, 4)))
    w_down = bell_draw(keys[5], (EXPERTS, H, D), H ** -0.5, 0.1875, ((0, 4), (2, 4)))
    return dict(tokens=tokens, expert_ids=expert_ids, scores=scores, w_gate=w_gate, w_up=w_up, w_down=w_down)


def block_sum(parts, weight):
    local = D // N_DP
    blocks = jnp.einsum('rbd,bdh->rbh', parts, weight.reshape(N_DP, local, H).astype(jnp.float32))
    rounded = lax.optimization_barrier(blocks.astype(jnp.bfloat16))
    return jnp.sum(rounded.astype(jnp.float32), axis=1)


def reference(tokens, expert_ids, scores, w_gate, w_up, w_down):
    n_blocks = N_EXPERT
    ids = expert_ids.reshape(n_blocks, TOK_DEV * TOP)
    onehot = (ids[:, :, None] == jnp.arange(EXPERTS, dtype=jnp.int32)[None, None, :]).astype(jnp.int32)
    earlier = jnp.cumsum(onehot, axis=1) - onehot
    rank = jnp.sum(earlier * onehot, axis=2)
    block = jnp.arange(n_blocks, dtype=jnp.int32)[:, None]
    slots = ((ids * n_blocks + block) * CAP + rank).reshape(-1).astype(jnp.int32)
    source = jnp.repeat(jnp.arange(TOKENS, dtype=jnp.int32), TOP)
    buffer = jnp.zeros((EXPERTS * n_blocks * CAP, D), jnp.bfloat16).at[slots].set(tokens[source])
    buffer = buffer.reshape(EXPERTS, n_blocks * CAP, D)

    def expert_rows(items):
        rows, gate_w, up_w, down_w = items
        parts = rows.reshape(-1, N_DP, D // N_DP).astype(jnp.float32)
        gate = block_sum(parts, gate_w)
        up = block_sum(parts, up_w)
        hidden = (jax.nn.silu(gate) * up).astype(jnp.bfloat16)
        return jnp.dot(hidden, down_w, preferred_element_type=jnp.float32).astype(jnp.bfloat16)

    outputs = lax.map(expert_rows, (buffer, w_gate, w_up, w_down))
    picked = outputs.reshape(-1, D)[slots].reshape(TOKENS, TOP, D).astype(jnp.float32)
    affinity = jax.nn.sigmoid(scores)
    weights = 2.5 * affinity / jnp.sum(affinity, axis=1, keepdims=True)
    return jnp.einsum('tk,tkd->td', weights, picked).astype(jnp.bfloat16)
```

```python
import functools

import jax
import jax.numpy as jnp
from jax import lax
from jax.experimental import pallas as pl
from jax.experimental.pallas import tpu as pltpu
from jax.sharding import PartitionSpec as P

LANES = 128
VMEM = pl.BlockSpec(memory_space=pltpu.VMEM)
SMEM = pl.BlockSpec(memory_space=pltpu.SMEM)
NOWHERE = -1e6


def bits_of(n):
    return [b for b in range(n.bit_length() - 1)]


def flip(x, axis, k):
    return lax.ppermute(x, axis, [(i, i ^ k) for i in range(lax.axis_size(axis))])


def route_body(n, experts, per_chunk, rows, info, *refs):
    meta, (rank_t, rank, wt, sched) = refs[:n], refs[n:]
    tok, top = meta[0].shape[0], meta[0].shape[1] // 2
    first = info[0].astype(jnp.float32)
    lane = lax.broadcasted_iota(jnp.int32, (tok, LANES), 1).astype(jnp.float32)
    before = (
        lax.broadcasted_iota(jnp.int32, (tok, tok), 0) > lax.broadcasted_iota(jnp.int32, (tok, tok), 1)
    ).astype(jnp.bfloat16)
    seen = jnp.zeros((1, LANES), jnp.float32)
    for s in range(n):
        block = meta[s][...]
        named = jnp.zeros((tok, LANES), jnp.float32)
        weight = jnp.zeros((tok, LANES), jnp.float32)
        for k in range(top):
            hit = jnp.where(block[:, k : k + 1] - first == lane, 1.0, 0.0)
            named = named + hit
            weight = weight + hit * block[:, top + k : top + k + 1]
        named = jnp.where(lane < experts, named, 0.0)
        place = jnp.dot(before, named.astype(jnp.bfloat16), preferred_element_type=jnp.float32) + seen
        rank[s * tok : (s + 1) * tok, :] = jnp.where(named > 0, place, NOWHERE)
        wt[s * tok : (s + 1) * tok, :] = weight
        seen = seen + jnp.sum(named, axis=0, keepdims=True)
    turned = jnp.transpose(rank[...])[: rank_t.shape[0]]
    rank_t[...] = turned
    count = jnp.sum((turned >= 0).astype(jnp.float32), axis=1, keepdims=True)
    shape = (rank_t.shape[0], LANES)
    j = lax.broadcasted_iota(jnp.int32, shape, 1).astype(jnp.float32)
    e = lax.broadcasted_iota(jnp.int32, shape, 0).astype(jnp.float32)
    ahead = ((seen > count) | ((seen == count) & (j < e))) & (j < experts)
    order = jnp.sum(ahead.astype(jnp.float32), axis=1, keepdims=True)
    large = jnp.where((order == j) & (e < experts), 1.0, 0.0)
    small = jnp.where((order == experts - 1 - j) & (e < experts), 1.0, 0.0)
    expert_a = jnp.sum(e * large, axis=0, keepdims=True)
    count_a = jnp.sum(count * large, axis=0, keepdims=True)
    if per_chunk == 2:
        expert_b = jnp.sum(e * small, axis=0, keepdims=True)
        count_b = jnp.sum(count * small, axis=0, keepdims=True)
    else:
        expert_b, count_b = expert_a, jnp.zeros_like(count_a)
        count_a = jnp.full_like(count_a, rows)
    sched[0:1] = expert_a.astype(jnp.int32)
    sched[1:2] = expert_b.astype(jnp.int32)
    sched[2:3] = count_a.astype(jnp.int32)
    sched[3:4] = (count_a + count_b).astype(jnp.int32)
    sched[4:8] = jnp.full((4, LANES), info[1], jnp.int32)


def route(meta, info, experts, per_chunk, rows):
    n, tok = len(meta), meta[0].shape[0]
    padded = -(-experts // 8) * 8
    return pl.pallas_call(
        functools.partial(route_body, n, experts, per_chunk, rows),
        out_shape=(
            jax.ShapeDtypeStruct((padded, n * tok), jnp.float32),
            jax.ShapeDtypeStruct((n * tok, LANES), jnp.float32),
            jax.ShapeDtypeStruct((n * tok, LANES), jnp.float32),
            jax.ShapeDtypeStruct((8, LANES), jnp.int32),
        ),
        in_specs=[SMEM] + [VMEM] * n,
        out_specs=(VMEM,) * 4,
        name="route",
    )(info, *meta)


def gate_up_body(n, chunk, half, sched, *refs):
    tokens, (rank_t, gate_a, gate_b, up_a, up_b, send, keep, feed, rows) = refs[:n], refs[n:]
    step = pl.program_id(0)
    count = rows.shape[0]
    split = sched[2, chunk]

    @pl.when(step == 0)
    def _():
        tok = tokens[0].shape[0]
        for s in range(n):
            feed[s * tok : (s + 1) * tok, :] = tokens[s][...]
        r = lax.broadcasted_iota(jnp.int32, (count, n * tok), 0).astype(jnp.float32)
        a = rank_t[pl.ds(sched[0, chunk], 1), :]
        b = rank_t[pl.ds(sched[1, chunk], 1), :] + split.astype(jnp.float32)
        pick = jnp.where(r == a, 1.0, 0.0) + jnp.where(r == b, 1.0, 0.0)
        rows[...] = jnp.dot(
            pick.astype(jnp.bfloat16), feed[...], preferred_element_type=jnp.float32
        ).astype(jnp.bfloat16)

    x = rows[...]
    width = gate_a.shape[2]
    of_a = lax.broadcasted_iota(jnp.int32, (count, width), 0) < split

    def both(wa, wb):
        left = jnp.dot(x, wa[0], preferred_element_type=jnp.float32)
        right = jnp.dot(x, wb[0], preferred_element_type=jnp.float32)
        return jnp.where(of_a, left, right).astype(jnp.bfloat16)

    gate, up = both(gate_a, gate_b), both(up_a, up_b)

    @pl.when(step < half)
    def _():
        send[0, :, :width] = gate
        send[0, :, width:] = up

    @pl.when(step >= half)
    def _():
        keep[0, :, :width] = gate
        keep[0, :, width:] = up


def gate_up(tokens, rank_t, sched, w_gate, w_up, chunk, rows, n_dp):
    n, (tok, local) = len(tokens), tokens[0].shape
    width = w_gate.shape[2] // n_dp
    half = max(n_dp // 2, 1)

    def weight_spec(row):
        def index(i, sched):
            part = jnp.where(i < half, 2 * i + 1, 2 * (i - half))
            return sched[row, chunk], 0, part ^ sched[4, 0]

        return pl.BlockSpec((1, local, width), index)

    whole = lambda shape: pl.BlockSpec(shape, lambda i, sched: (0, 0))
    out = jax.ShapeDtypeStruct((half, rows, 2 * width), jnp.bfloat16)
    flops = 2 * rows * local * 4 * width * n_dp
    return pl.pallas_call(
        functools.partial(gate_up_body, n, chunk, half),
        out_shape=(out, out),
        grid_spec=pltpu.PrefetchScalarGridSpec(
            num_scalar_prefetch=1,
            grid=(n_dp,),
            in_specs=[whole((tok, local))] * n
            + [whole(rank_t.shape)]
            + [weight_spec(0), weight_spec(1)] * 2,
            out_specs=(
                pl.BlockSpec((1, rows, 2 * width), lambda i, s: (jnp.minimum(i, half - 1), 0, 0)),
                pl.BlockSpec((1, rows, 2 * width), lambda i, s: (jnp.maximum(i - half, 0), 0, 0)),
            ),
            scratch_shapes=[
                pltpu.VMEM((n * tok, local), jnp.bfloat16),
                pltpu.VMEM((rows, local), jnp.bfloat16),
            ],
        ),
        compiler_params=pltpu.CompilerParams(vmem_limit_bytes=32 << 20),
        cost_estimate=pl.CostEstimate(
            flops=flops, bytes_accessed=2 * 4 * local * width * n_dp, transcendentals=0
        ),
        name="gate_up",
    )(sched, *tokens, rank_t, w_gate, w_gate, w_up, w_up)


def down_body(n_dp, n_out, chunk, first, sched, *refs):
    parts, (rank, wt, down_a, down_b), refs = refs[:n_dp], refs[n_dp : n_dp + 4], refs[n_dp + 4 :]
    before = None if first else refs[0]
    outs, (hidden, mix) = refs[0 if first else 1 : -2], refs[-2:]
    rows = hidden.shape[0]
    width = parts[0].shape[-1]
    split = sched[2, chunk]

    @pl.when(pl.program_id(0) == 0)
    def _():
        for l in range(n_dp):
            at = pl.multiple_of((l ^ sched[4, 0]) * width, width)
            hidden[:, pl.ds(at, width)] = parts[l][0]
        lane = lax.broadcasted_iota(jnp.int32, rank.shape, 1)
        column = lambda ref, e: jnp.sum(jnp.where(lane == e, ref[...], 0.0), axis=1, keepdims=True)
        r = lax.broadcasted_iota(jnp.int32, mix.shape, 1).astype(jnp.float32)
        a, b = sched[0, chunk], sched[1, chunk]
        place_b = column(rank, b) + split.astype(jnp.float32)
        mix[...] = (
            jnp.where(r == column(rank, a), column(wt, a), 0.0)
            + jnp.where(r == place_b, column(wt, b), 0.0)
        ).astype(jnp.bfloat16)

    left = jnp.dot(hidden[...], down_a[0], preferred_element_type=jnp.float32)
    right = jnp.dot(hidden[...], down_b[0], preferred_element_type=jnp.float32)
    of_a = lax.broadcasted_iota(jnp.int32, left.shape, 0) < split
    out = jnp.where(of_a, left, right).astype(jnp.bfloat16)
    total = jnp.dot(mix[...], out, preferred_element_type=jnp.float32)
    if not first:
        total = total + before[...]
    tok = total.shape[0] // n_out
    for s in range(n_out):
        outs[s][...] = total[s * tok : (s + 1) * tok].astype(outs[s].dtype)


def down(parts, rank, wt, sched, w_down, total, chunk, last, n_owner):
    n_dp = len(parts)
    _, rows, width = parts[0].shape
    _, hidden, local = w_down.shape
    tokens = rank.shape[0]
    block = 512 if local % 512 == 0 else 256 if local % 256 == 0 else local
    n_out = n_owner if last else 1
    kind = jnp.bfloat16 if last else jnp.float32
    first = total is None

    def weight_spec(row):
        return pl.BlockSpec((1, hidden, block), lambda i, s: (s[row, chunk], 0, i))

    whole = lambda shape: pl.BlockSpec(shape, lambda i, s: (0,) * len(shape))
    column = pl.BlockSpec((tokens, block), lambda i, s: (0, i))
    outs = pl.pallas_call(
        functools.partial(down_body, n_dp, n_out, chunk, first),
        out_shape=(jax.ShapeDtypeStruct((tokens // n_out, local), kind),) * n_out,
        grid_spec=pltpu.PrefetchScalarGridSpec(
            num_scalar_prefetch=1,
            grid=(local // block,),
            in_specs=[whole(parts[0].shape)] * n_dp
            + [whole(rank.shape)] * 2
            + [weight_spec(0), weight_spec(1)]
            + ([] if first else [column]),
            out_specs=(pl.BlockSpec((tokens // n_out, block), lambda i, s: (0, i)),) * n_out,
            scratch_shapes=[
                pltpu.VMEM((rows, hidden), jnp.bfloat16),
                pltpu.VMEM((tokens, rows), jnp.bfloat16),
            ],
        ),
        compiler_params=pltpu.CompilerParams(vmem_limit_bytes=48 << 20),
        cost_estimate=pl.CostEstimate(
            flops=2 * rows * local * (2 * hidden + tokens),
            bytes_accessed=2 * 2 * hidden * local + 8 * tokens * local,
            transcendentals=0,
        ),
        name="down",
    )(sched, *parts, rank, wt, w_down, w_down, *([] if first else [total]))
    return outs if last else outs[0]


def hidden_parts(send, keep, n_dp):
    bits = bits_of(n_dp)
    total = keep.astype(jnp.float32)
    for b in bits:
        if b > 0:
            send = total[1::2].astype(jnp.bfloat16)
            total = total[0::2]
        total = total + flip(send, "dp", 1 << b).astype(jnp.float32)
    width = total.shape[2] // 2
    share = (jax.nn.silu(total[:, :, :width]) * total[:, :, width:]).astype(jnp.bfloat16)
    parts = {0: share}
    for b in reversed(bits):
        for l in list(parts):
            parts[l | 1 << b] = flip(parts[l], "dp", 1 << b)
    return [parts[l] for l in range(n_dp)]


def on_device(tokens, expert_ids, scores, w_gate, w_up, w_down):
    n_owner, n_dp = lax.axis_size("expert"), lax.axis_size("dp")
    tok_rows, top = expert_ids.shape
    experts = w_gate.shape[0]
    capacity = 2 * tok_rows * top // (experts * n_owner)
    per_chunk = 2 if experts % 2 == 0 else 1
    rows = per_chunk * n_owner * capacity

    affinity = jax.nn.sigmoid(scores)
    weights = 2.5 * affinity / jnp.sum(affinity, axis=1, keepdims=True)
    meta = jnp.concatenate([expert_ids.astype(jnp.float32), weights], axis=1)
    metas = [meta] + [flip(meta, "expert", k) for k in range(1, n_owner)]
    feeds = [tokens] + [flip(tokens, "expert", k) for k in range(1, n_owner)]
    info = jnp.stack([lax.axis_index("expert") * experts, lax.axis_index("dp")]).astype(jnp.int32)
    rank_t, rank, wt, sched = route(metas, info, experts, per_chunk, rows)

    chunks = experts // per_chunk
    parts = [
        hidden_parts(*gate_up(feeds, rank_t, sched, w_gate, w_up, c, rows, n_dp), n_dp)
        for c in range(chunks)
    ]
    total = None
    for c in range(chunks):
        total = down(parts[c], rank, wt, sched, w_down, total, c, c == chunks - 1, n_owner)
    mixed = total[0].astype(jnp.float32)
    for k in range(1, n_owner):
        mixed = mixed + flip(total[k], "expert", k).astype(jnp.float32)
    return mixed.astype(jnp.bfloat16)


def solution(mesh):
    in_specs = (
        P(("groups", "expert"), "dp"),
        P(("groups", "expert"), None),
        P(("groups", "expert"), None),
        P("expert", "dp", None),
        P("expert", "dp", None),
        P("expert", None, "dp"),
    )
    out_specs = P(("groups", "expert"), "dp")
    return jax.shard_map(
        on_device, mesh=mesh, in_specs=in_specs, out_specs=out_specs, check_vma=False
    )
```

```python
import functools

import jax
import jax.numpy as jnp
from jax import lax
from jax.experimental import pallas as pl
from jax.experimental.pallas import tpu as pltpu
from jax.sharding import PartitionSpec as P

LANES = 128
VMEM = pl.BlockSpec(memory_space=pltpu.VMEM)
SMEM = pl.BlockSpec(memory_space=pltpu.SMEM)
NOWHERE = -1e6


def bits_of(n):
    return [b for b in range(n.bit_length() - 1)]


def flip(x, axis, k):
    return lax.ppermute(x, axis, [(i, i ^ k) for i in range(lax.axis_size(axis))])


def route_body(n, experts, per_chunk, rows, info, meta, rank_t, rank, wt, sched):
    tok, top = meta.shape[1], meta.shape[2] // 2
    first = info[0].astype(jnp.float32)
    lane = lax.broadcasted_iota(jnp.int32, (tok, LANES), 1).astype(jnp.float32)
    before = (
        lax.broadcasted_iota(jnp.int32, (tok, tok), 0) > lax.broadcasted_iota(jnp.int32, (tok, tok), 1)
    ).astype(jnp.bfloat16)
    seen = jnp.zeros((1, LANES), jnp.float32)
    for s in range(n):
        block = meta[info[2] ^ s]
        affinity = 1.0 / (1.0 + jnp.exp(-block[:, top:]))
        share = 2.5 * affinity / jnp.sum(affinity, axis=1, keepdims=True)
        named = jnp.zeros((tok, LANES), jnp.float32)
        weight = jnp.zeros((tok, LANES), jnp.float32)
        for k in range(top):
            hit = jnp.where(block[:, k : k + 1] - first == lane, 1.0, 0.0)
            named = named + hit
            weight = weight + hit * share[:, k : k + 1]
        named = jnp.where(lane < experts, named, 0.0)
        place = jnp.dot(before, named.astype(jnp.bfloat16), preferred_element_type=jnp.float32) + seen
        rank[s * tok : (s + 1) * tok, :] = jnp.where(named > 0, place, NOWHERE)
        wt[s * tok : (s + 1) * tok, :] = weight
        seen = seen + jnp.sum(named, axis=0, keepdims=True)
    turned = jnp.transpose(rank[...])[: rank_t.shape[0]]
    rank_t[...] = turned
    count = jnp.sum((turned >= 0).astype(jnp.float32), axis=1, keepdims=True)
    shape = (rank_t.shape[0], LANES)
    j = lax.broadcasted_iota(jnp.int32, shape, 1).astype(jnp.float32)
    e = lax.broadcasted_iota(jnp.int32, shape, 0).astype(jnp.float32)
    ahead = ((seen > count) | ((seen == count) & (j < e))) & (j < experts)
    order = jnp.sum(ahead.astype(jnp.float32), axis=1, keepdims=True)
    large = jnp.where((order == j) & (e < experts), 1.0, 0.0)
    small = jnp.where((order == experts - 1 - j) & (e < experts), 1.0, 0.0)
    expert_a = jnp.sum(e * large, axis=0, keepdims=True)
    count_a = jnp.sum(count * large, axis=0, keepdims=True)
    if per_chunk == 2:
        expert_b = jnp.sum(e * small, axis=0, keepdims=True)
        count_b = jnp.sum(count * small, axis=0, keepdims=True)
    else:
        expert_b, count_b = expert_a, jnp.zeros_like(count_a)
        count_a = jnp.full_like(count_a, rows)
    sched[0:1] = expert_a.astype(jnp.int32)
    sched[1:2] = expert_b.astype(jnp.int32)
    sched[2:3] = count_a.astype(jnp.int32)
    sched[3:4] = (count_a + count_b).astype(jnp.int32)
    sched[4:8] = jnp.full((4, LANES), info[1], jnp.int32)


def route(meta, info, experts, per_chunk, rows):
    tokens = meta.shape[0] * meta.shape[1]
    padded = -(-experts // 8) * 8
    return pl.pallas_call(
        functools.partial(route_body, meta.shape[0], experts, per_chunk, rows),
        out_shape=(
            jax.ShapeDtypeStruct((padded, tokens), jnp.float32),
            jax.ShapeDtypeStruct((tokens, LANES), jnp.float32),
            jax.ShapeDtypeStruct((tokens, LANES), jnp.float32),
            jax.ShapeDtypeStruct((8, LANES), jnp.int32),
        ),
        in_specs=[SMEM, VMEM],
        out_specs=(VMEM,) * 4,
        name="route",
    )(info, meta)


def joined(left, right, rows, split):
    most = left.shape[0]
    if right is None:
        return left
    if rows >= 2 * most:
        return jnp.concatenate([left, right], axis=0)
    head = rows - most
    shared = lax.broadcasted_iota(jnp.int32, (most - head, left.shape[1]), 0) + head < split
    middle = jnp.where(shared, left[head:], right[: most - head])
    return jnp.concatenate([left[:head], middle, right[most - head :]], axis=0)


def gate_up_body(n, chunk, half, most, after, sched, *refs):
    tokens, (rank_t, gate_a, gate_b, up_a, up_b), refs = refs[:n], refs[n : n + 5], refs[n + 5 + after :]
    send, keep, feed, rows = refs
    step = pl.program_id(0)
    count = rows.shape[0]
    split = sched[2, chunk]

    @pl.when(step == 0)
    def _():
        tok = tokens[0].shape[0]
        for s in range(n):
            feed[s * tok : (s + 1) * tok, :] = tokens[s][...]
        r = lax.broadcasted_iota(jnp.int32, (count, n * tok), 0).astype(jnp.float32)
        pick = jnp.where(r == rank_t[pl.ds(sched[0, chunk], 1), :], 1.0, 0.0)
        if most < count:
            pick = pick + jnp.where(count - 1 - r == rank_t[pl.ds(sched[1, chunk], 1), :], 1.0, 0.0)
        rows[...] = jnp.dot(
            pick.astype(jnp.bfloat16), feed[...], preferred_element_type=jnp.float32
        ).astype(jnp.bfloat16)

    width = gate_a.shape[2]

    def both(wa, wb):
        left = jnp.dot(rows[:most], wa[0], preferred_element_type=jnp.float32)
        right = None
        if most < count:
            right = jnp.dot(rows[count - most :], wb[0], preferred_element_type=jnp.float32)
        return joined(left, right, count, split).astype(jnp.bfloat16)

    gate, up = both(gate_a, gate_b), both(up_a, up_b)

    @pl.when(step < half)
    def _():
        send[0, :, :width] = gate
        send[0, :, width:] = up

    @pl.when(step >= half)
    def _():
        keep[0, :, :width] = gate
        keep[0, :, width:] = up


def gate_up(tokens, rank_t, sched, w_gate, w_up, chunk, rows, most, n_dp, after):
    n, (tok, local) = len(tokens), tokens[0].shape
    width = w_gate.shape[2] // n_dp
    half = max(n_dp // 2, 1)

    def weight_spec(row):
        def index(i, sched):
            part = jnp.where(i < half, 2 * i + 1, 2 * (i - half))
            return sched[row, chunk], 0, part ^ sched[4, 0]

        return pl.BlockSpec((1, local, width), index)

    whole = lambda shape: pl.BlockSpec(shape, lambda i, sched: (0, 0))
    out = jax.ShapeDtypeStruct((half, rows, 2 * width), jnp.bfloat16)
    return pl.pallas_call(
        functools.partial(gate_up_body, n, chunk, half, most, len(after)),
        out_shape=(out, out),
        grid_spec=pltpu.PrefetchScalarGridSpec(
            num_scalar_prefetch=1,
            grid=(n_dp,),
            in_specs=[whole((tok, local))] * n
            + [whole(rank_t.shape)]
            + [weight_spec(0), weight_spec(1)] * 2
            + [pl.BlockSpec(memory_space=pl.ANY)] * len(after),
            out_specs=(
                pl.BlockSpec((1, rows, 2 * width), lambda i, s: (jnp.minimum(i, half - 1), 0, 0)),
                pl.BlockSpec((1, rows, 2 * width), lambda i, s: (jnp.maximum(i - half, 0), 0, 0)),
            ),
            scratch_shapes=[
                pltpu.VMEM((n * tok, local), jnp.bfloat16),
                pltpu.VMEM((rows, local), jnp.bfloat16),
            ],
        ),
        compiler_params=pltpu.CompilerParams(vmem_limit_bytes=32 << 20),
        cost_estimate=pl.CostEstimate(
            flops=2 * 2 * most * local * 2 * width * n_dp,
            bytes_accessed=2 * 4 * local * width * n_dp,
            transcendentals=0,
        ),
        name="gate_up",
    )(sched, *tokens, rank_t, w_gate, w_gate, w_up, w_up, *after)


def down_body(n_dp, n_out, chunk, first, most, after, sched, *refs):
    parts, (rank, wt, down_a, down_b), refs = refs[:n_dp], refs[n_dp : n_dp + 4], refs[n_dp + 4 :]
    before = None if first else refs[0]
    refs = refs[(0 if first else 1) + after :]
    outs, (hidden, mix) = refs[:-2], refs[-2:]
    rows = hidden.shape[0]
    width = parts[0].shape[-1]
    split = sched[2, chunk]

    @pl.when(pl.program_id(0) == 0)
    def _():
        for l in range(n_dp):
            at = pl.multiple_of((l ^ sched[4, 0]) * width, width)
            hidden[:, pl.ds(at, width)] = parts[l][0]
        lane = lax.broadcasted_iota(jnp.int32, rank.shape, 1)
        column = lambda ref, e: jnp.sum(jnp.where(lane == e, ref[...], 0.0), axis=1, keepdims=True)
        r = lax.broadcasted_iota(jnp.int32, mix.shape, 1).astype(jnp.float32)
        a, b = sched[0, chunk], sched[1, chunk]
        share = jnp.where(r == column(rank, a), column(wt, a), 0.0)
        if most < rows:
            share = share + jnp.where(rows - 1 - r == column(rank, b), column(wt, b), 0.0)
        mix[...] = share.astype(jnp.bfloat16)

    left = jnp.dot(hidden[:most], down_a[0], preferred_element_type=jnp.float32)
    right = None
    if most < rows:
        right = jnp.dot(hidden[rows - most :], down_b[0], preferred_element_type=jnp.float32)
    out = joined(left, right, rows, split).astype(jnp.bfloat16)
    total = jnp.dot(mix[...], out, preferred_element_type=jnp.float32)
    if not first:
        total = total + before[...]
    tok = total.shape[0] // n_out
    for s in range(n_out):
        outs[s][...] = total[s * tok : (s + 1) * tok].astype(outs[s].dtype)


def down(parts, rank, wt, sched, w_down, total, chunk, most, last, n_owner, after):
    n_dp = len(parts)
    _, rows, width = parts[0].shape
    _, hidden, local = w_down.shape
    tokens = rank.shape[0]
    block = 512 if local % 512 == 0 else 256 if local % 256 == 0 else local
    n_out = n_owner if last else 1
    kind = jnp.bfloat16 if last else jnp.float32
    first = total is None

    def weight_spec(row):
        return pl.BlockSpec((1, hidden, block), lambda i, s: (s[row, chunk], 0, i))

    whole = lambda shape: pl.BlockSpec(shape, lambda i, s: (0,) * len(shape))
    column = pl.BlockSpec((tokens, block), lambda i, s: (0, i))
    outs = pl.pallas_call(
        functools.partial(down_body, n_dp, n_out, chunk, first, most, len(after)),
        out_shape=(jax.ShapeDtypeStruct((tokens // n_out, local), kind),) * n_out,
        grid_spec=pltpu.PrefetchScalarGridSpec(
            num_scalar_prefetch=1,
            grid=(local // block,),
            in_specs=[whole(parts[0].shape)] * n_dp
            + [whole(rank.shape)] * 2
            + [weight_spec(0), weight_spec(1)]
            + ([] if first else [column])
            + [pl.BlockSpec(memory_space=pl.ANY)] * len(after),
            out_specs=(pl.BlockSpec((tokens // n_out, block), lambda i, s: (0, i)),) * n_out,
            scratch_shapes=[
                pltpu.VMEM((rows, hidden), jnp.bfloat16),
                pltpu.VMEM((tokens, rows), jnp.bfloat16),
            ],
        ),
        compiler_params=pltpu.CompilerParams(vmem_limit_bytes=48 << 20),
        cost_estimate=pl.CostEstimate(
            flops=2 * local * (2 * most * hidden + rows * tokens),
            bytes_accessed=2 * 2 * hidden * local + 8 * tokens * local,
            transcendentals=0,
        ),
        name="down",
    )(sched, *parts, rank, wt, w_down, w_down, *([] if first else [total]), *after)
    return outs if last else outs[0]


def block_sums(send, keep, n_dp):
    total = keep.astype(jnp.float32)
    for b in bits_of(n_dp):
        if b > 0:
            send = total[1::2].astype(jnp.bfloat16)
            total = total[0::2]
        total = total + flip(send, "dp", 1 << b).astype(jnp.float32)
    width = total.shape[2] // 2
    return (jax.nn.silu(total[:, :, :width]) * total[:, :, width:]).astype(jnp.bfloat16), send


def all_parts(share, n_dp):
    parts = {0: share}
    for b in reversed(bits_of(n_dp)):
        for l in list(parts):
            parts[l | 1 << b] = flip(parts[l], "dp", 1 << b)
    return [parts[l] for l in range(n_dp)]


def on_device(tokens, expert_ids, scores, w_gate, w_up, w_down):
    n_owner, n_dp = lax.axis_size("expert"), lax.axis_size("dp")
    tok_rows, top = expert_ids.shape
    experts = w_gate.shape[0]
    capacity = 2 * tok_rows * top // (experts * n_owner)
    per_chunk = 2 if experts % 2 == 0 else 1
    most = n_owner * capacity
    rows = per_chunk * most
    chunks = experts // per_chunk

    meta = jnp.concatenate([expert_ids.astype(jnp.float32), scores], axis=1)
    metas = lax.all_gather(meta, "expert")
    feeds = [tokens] + [flip(tokens, "expert", k) for k in range(1, n_owner)]
    mine = lax.axis_index("expert")
    info = jnp.stack([mine * experts, lax.axis_index("dp"), mine]).astype(jnp.int32)
    rank_t, rank, wt, sched = route(metas, info, experts, per_chunk, rows)

    shares, sent = [], []
    for c in range(chunks):
        after = ([sent[c - 2]] if c >= 2 else []) + ([shares[c - 3]] if c >= 3 else [])
        send, keep = gate_up(feeds, rank_t, sched, w_gate, w_up, c, rows, most, n_dp, after)
        share, last_sent = block_sums(send, keep, n_dp)
        shares.append(share)
        sent.append(last_sent)
    parts = [all_parts(share, n_dp) for share in shares]
    total = None
    for c in range(chunks):
        after = [sent[-1]] if c == 0 else [shares[-1]] if c == 1 else []
        total = down(parts[c], rank, wt, sched, w_down, total, c, most, c == chunks - 1, n_owner, after)
    mixed = total[0].astype(jnp.float32)
    for k in range(1, n_owner):
        mixed = mixed + flip(total[k], "expert", k).astype(jnp.float32)
    return mixed.astype(jnp.bfloat16)


def solution(mesh):
    in_specs = (
        P(("groups", "expert"), "dp"),
        P(("groups", "expert"), None),
        P(("groups", "expert"), None),
        P("expert", "dp", None),
        P("expert", "dp", None),
        P("expert", None, "dp"),
    )
    out_specs = P(("groups", "expert"), "dp")
    return jax.shard_map(
        on_device, mesh=mesh, in_specs=in_specs, out_specs=out_specs, check_vma=False
    )
```

```python
import functools

import jax
import jax.numpy as jnp
from jax import lax
from jax.experimental import pallas as pl
from jax.experimental.pallas import tpu as pltpu
from jax.sharding import PartitionSpec as P

LANES = 128
VMEM = pl.BlockSpec(memory_space=pltpu.VMEM)
SMEM = pl.BlockSpec(memory_space=pltpu.SMEM)
HERE = pl.BlockSpec(memory_space=pl.ANY)
NOWHERE = -1e6


def bits_of(n):
    return [b for b in range(n.bit_length() - 1)]


def flip(x, axis, k):
    return lax.ppermute(x, axis, [(i, i ^ k) for i in range(lax.axis_size(axis))])


def route_body(n, experts, per_chunk, rows, info, *refs):
    meta, (rank_t, rank, wt, sched) = refs[:n], refs[n:]
    tok, top = meta[0].shape[0], meta[0].shape[1] // 2
    first = info[0].astype(jnp.float32)
    lane = lax.broadcasted_iota(jnp.int32, (tok, LANES), 1).astype(jnp.float32)
    before = (
        lax.broadcasted_iota(jnp.int32, (tok, tok), 0) > lax.broadcasted_iota(jnp.int32, (tok, tok), 1)
    ).astype(jnp.bfloat16)
    seen = jnp.zeros((1, LANES), jnp.float32)
    for s in range(n):
        block = meta[s][...]
        affinity = 1.0 / (1.0 + jnp.exp(-block[:, top:]))
        share = 2.5 * affinity / jnp.sum(affinity, axis=1, keepdims=True)
        named = jnp.zeros((tok, LANES), jnp.float32)
        weight = jnp.zeros((tok, LANES), jnp.float32)
        for k in range(top):
            hit = jnp.where(block[:, k : k + 1] - first == lane, 1.0, 0.0)
            named = named + hit
            weight = weight + hit * share[:, k : k + 1]
        named = jnp.where(lane < experts, named, 0.0)
        place = jnp.dot(before, named.astype(jnp.bfloat16), preferred_element_type=jnp.float32) + seen
        rank[s * tok : (s + 1) * tok, :] = jnp.where(named > 0, place, NOWHERE)
        wt[s * tok : (s + 1) * tok, :] = weight
        seen = seen + jnp.sum(named, axis=0, keepdims=True)
    turned = jnp.transpose(rank[...])[: rank_t.shape[0]]
    rank_t[...] = turned
    count = jnp.sum((turned >= 0).astype(jnp.float32), axis=1, keepdims=True)
    shape = (rank_t.shape[0], LANES)
    j = lax.broadcasted_iota(jnp.int32, shape, 1).astype(jnp.float32)
    e = lax.broadcasted_iota(jnp.int32, shape, 0).astype(jnp.float32)
    ahead = ((seen > count) | ((seen == count) & (j < e))) & (j < experts)
    order = jnp.sum(ahead.astype(jnp.float32), axis=1, keepdims=True)
    large = jnp.where((order == j) & (e < experts), 1.0, 0.0)
    small = jnp.where((order == experts - 1 - j) & (e < experts), 1.0, 0.0)
    expert_a = jnp.sum(e * large, axis=0, keepdims=True)
    count_a = jnp.sum(count * large, axis=0, keepdims=True)
    if per_chunk == 2:
        expert_b = jnp.sum(e * small, axis=0, keepdims=True)
        count_b = jnp.sum(count * small, axis=0, keepdims=True)
    else:
        expert_b, count_b = expert_a, jnp.zeros_like(count_a)
        count_a = jnp.full_like(count_a, rows)
    sched[0:1] = expert_a.astype(jnp.int32)
    sched[1:2] = expert_b.astype(jnp.int32)
    sched[2:3] = count_a.astype(jnp.int32)
    sched[3:4] = (count_a + count_b).astype(jnp.int32)
    sched[4:8] = jnp.full((4, LANES), info[1], jnp.int32)


def route(meta, info, experts, per_chunk, rows):
    tokens = len(meta) * meta[0].shape[0]
    padded = -(-experts // 8) * 8
    return pl.pallas_call(
        functools.partial(route_body, len(meta), experts, per_chunk, rows),
        out_shape=(
            jax.ShapeDtypeStruct((padded, tokens), jnp.float32),
            jax.ShapeDtypeStruct((tokens, LANES), jnp.float32),
            jax.ShapeDtypeStruct((tokens, LANES), jnp.float32),
            jax.ShapeDtypeStruct((8, LANES), jnp.int32),
        ),
        in_specs=[SMEM] + [VMEM] * len(meta),
        out_specs=(VMEM,) * 4,
        name="route",
    )(info, *meta)


def put(out, at, left, right, rows, split):
    most = left.shape[0]
    if right is None:
        out[at] = left
        return
    head = min(rows - most, most)
    out[at[:-2] + (slice(0, head), at[-1])] = left[:head]
    if head < most:
        shared = lax.broadcasted_iota(jnp.int32, (most - head, left.shape[1]), 0) + head < split
        out[at[:-2] + (slice(head, most), at[-1])] = jnp.where(shared, left[head:], right[: most - head])
    out[at[:-2] + (slice(most, rows), at[-1])] = right[most - head :]


def gate_up_body(n, chunk, n_dp, most, after, sched, *refs):
    tokens, (rank_t, w_gate, w_up), refs = refs[:n], refs[n : n + 3], refs[n + 3 + after :]
    send, keep, feed, rows, held, feed_sem, held_sem = refs
    count = rows.shape[0]
    width = send.shape[2] // 2
    split = sched[2, chunk]
    experts = [sched[0, chunk]] + ([sched[1, chunk]] if most < count else [])
    loads = [(w, e) for w in (w_gate, w_up) for e in experts]
    copies = [
        pltpu.make_async_copy(w.at[e], held.at[i], held_sem.at[i]) for i, (w, e) in enumerate(loads)
    ]
    at, feeds = 0, []
    for s in range(n):
        tok = tokens[s].shape[0]
        feeds.append(pltpu.make_async_copy(tokens[s], feed.at[pl.ds(at, tok)], feed_sem.at[s]))
        at += tok
    for copy in feeds:
        copy.start()
    for copy in copies[: len(experts)]:
        copy.start()
    r = lax.broadcasted_iota(jnp.int32, (count, at), 0).astype(jnp.float32)
    pick = jnp.where(r == rank_t[pl.ds(experts[0], 1), :], 1.0, 0.0)
    if most < count:
        pick = pick + jnp.where(count - 1 - r == rank_t[pl.ds(experts[1], 1), :], 1.0, 0.0)
    for copy in feeds:
        copy.wait()
    rows[...] = jnp.dot(
        pick.astype(jnp.bfloat16), feed[...], preferred_element_type=jnp.float32
    ).astype(jnp.bfloat16)
    for m in range(2):
        first = m * len(experts)
        for copy in copies[first : first + len(experts)]:
            copy.wait()
        if m == 0:
            for copy in copies[len(experts) :]:
                copy.start()
        for l in range(n_dp):
            units = pl.ds(pl.multiple_of((l ^ sched[4, 0]) * width, width), width)
            left = jnp.dot(rows[:most], held[first, :, units], preferred_element_type=jnp.float32)
            right = None
            if most < count:
                right = jnp.dot(
                    rows[count - most :], held[first + 1, :, units], preferred_element_type=jnp.float32
                ).astype(jnp.bfloat16)
            to = (l // 2, slice(None), slice(m * width, (m + 1) * width))
            put(send if l % 2 else keep, to, left.astype(jnp.bfloat16), right, count, split)


def gate_up(tokens, rank_t, sched, w_gate, w_up, chunk, rows, most, n_dp, after):
    n, local = len(tokens), tokens[0].shape[1]
    hidden = w_gate.shape[2]
    out = jax.ShapeDtypeStruct((max(n_dp // 2, 1), rows, 2 * hidden // n_dp), jnp.bfloat16)
    mats = 2 * (2 if most < rows else 1)
    return pl.pallas_call(
        functools.partial(gate_up_body, n, chunk, n_dp, most, len(after)),
        out_shape=(out, out),
        in_specs=[SMEM] + [HERE] * n + [VMEM] + [HERE] * (2 + len(after)),
        out_specs=(VMEM, VMEM),
        scratch_shapes=[
            pltpu.VMEM((rank_t.shape[1], local), jnp.bfloat16),
            pltpu.VMEM((rows, local), jnp.bfloat16),
            pltpu.VMEM((mats, local, hidden), jnp.bfloat16),
            pltpu.SemaphoreType.DMA((n,)),
            pltpu.SemaphoreType.DMA((mats,)),
        ],
        compiler_params=pltpu.CompilerParams(vmem_limit_bytes=48 << 20),
        cost_estimate=pl.CostEstimate(
            flops=2 * mats * most * local * hidden,
            bytes_accessed=2 * mats * local * hidden,
            transcendentals=0,
        ),
        name="gate_up",
    )(sched, *tokens, rank_t, w_gate, w_up, *after)


def down_body(n_dp, n_out, chunk, first, most, after, sched, *refs):
    parts, (rank, wt, w_down), refs = refs[:n_dp], refs[n_dp : n_dp + 3], refs[n_dp + 3 :]
    before = None if first else refs[0]
    refs = refs[(0 if first else 1) + after :]
    outs, (hidden, mix, out, held, held_sem) = refs[:-5], refs[-5:]
    rows = hidden.shape[0]
    width = parts[0].shape[-1]
    split = sched[2, chunk]
    experts = [sched[0, chunk]] + ([sched[1, chunk]] if most < rows else [])
    copies = [
        pltpu.make_async_copy(w_down.at[e], held.at[i], held_sem.at[i]) for i, e in enumerate(experts)
    ]
    for copy in copies:
        copy.start()
    for l in range(n_dp):
        at = pl.multiple_of((l ^ sched[4, 0]) * width, width)
        hidden[:, pl.ds(at, width)] = parts[l][0]
    lane = lax.broadcasted_iota(jnp.int32, rank.shape, 1)
    column = lambda ref, e: jnp.sum(jnp.where(lane == e, ref[...], 0.0), axis=1, keepdims=True)
    r = lax.broadcasted_iota(jnp.int32, mix.shape, 1).astype(jnp.float32)
    share = jnp.where(r == column(rank, experts[0]), column(wt, experts[0]), 0.0)
    if most < rows:
        share = share + jnp.where(rows - 1 - r == column(rank, experts[1]), column(wt, experts[1]), 0.0)
    mix[...] = share.astype(jnp.bfloat16)
    for copy in copies:
        copy.wait()
    local = out.shape[1]
    block = 512 if local % 512 == 0 else 256 if local % 256 == 0 else local
    for i in range(local // block):
        cols = slice(i * block, (i + 1) * block)
        left = jnp.dot(hidden[:most], held[0, :, cols], preferred_element_type=jnp.float32)
        right = None
        if most < rows:
            right = jnp.dot(hidden[rows - most :], held[1, :, cols], preferred_element_type=jnp.float32)
            right = right.astype(jnp.bfloat16)
        put(out, (slice(None), cols), left.astype(jnp.bfloat16), right, rows, split)
        total = jnp.dot(mix[...], out[:, cols], preferred_element_type=jnp.float32)
        if not first:
            total = total + before[:, cols]
        tok = total.shape[0] // n_out
        for s in range(n_out):
            outs[s][:, cols] = total[s * tok : (s + 1) * tok].astype(outs[s].dtype)


def down(parts, rank, wt, sched, w_down, total, chunk, most, last, n_owner, after):
    n_dp = len(parts)
    _, rows, width = parts[0].shape
    _, hidden, local = w_down.shape
    tokens = rank.shape[0]
    n_out = n_owner if last else 1
    kind = jnp.bfloat16 if last else jnp.float32
    first = total is None
    mats = 2 if most < rows else 1
    outs = pl.pallas_call(
        functools.partial(down_body, n_dp, n_out, chunk, first, most, len(after)),
        out_shape=(jax.ShapeDtypeStruct((tokens // n_out, local), kind),) * n_out,
        in_specs=[SMEM]
        + [VMEM] * (n_dp + 2)
        + [HERE]
        + ([] if first else [VMEM])
        + [HERE] * len(after),
        out_specs=(VMEM,) * n_out,
        scratch_shapes=[
            pltpu.VMEM((rows, hidden), jnp.bfloat16),
            pltpu.VMEM((tokens, rows), jnp.bfloat16),
            pltpu.VMEM((rows, local), jnp.bfloat16),
            pltpu.VMEM((mats, hidden, local), jnp.bfloat16),
            pltpu.SemaphoreType.DMA((mats,)),
        ],
        compiler_params=pltpu.CompilerParams(vmem_limit_bytes=48 << 20),
        cost_estimate=pl.CostEstimate(
            flops=2 * local * (2 * most * hidden + rows * tokens),
            bytes_accessed=2 * mats * hidden * local + 8 * tokens * local,
            transcendentals=0,
        ),
        name="down",
    )(sched, *parts, rank, wt, w_down, *([] if first else [total]), *after)
    return outs if last else outs[0]


def finish_body(total, late, *refs):
    gate_up = total[...] + late[...].astype(jnp.float32)
    width = gate_up.shape[2] // 2
    gate, up = gate_up[:, :, :width], gate_up[:, :, width:]
    refs[-1][...] = (gate / (1.0 + jnp.exp(-gate)) * up).astype(jnp.bfloat16)


def partial_sums(send, keep, n_dp):
    total = keep.astype(jnp.float32)
    late = jnp.zeros(total.shape, jnp.bfloat16)
    for b in bits_of(n_dp):
        if b > 0:
            total = total + late.astype(jnp.float32)
            send = total[1::2].astype(jnp.bfloat16)
            total = total[0::2]
        late = flip(send, "dp", 1 << b)
    return total, late, send


def finish(total, late, after):
    return pl.pallas_call(
        finish_body,
        out_shape=jax.ShapeDtypeStruct(total.shape[:2] + (total.shape[2] // 2,), jnp.bfloat16),
        in_specs=[VMEM] * 2 + [HERE] * len(after),
        out_specs=VMEM,
        cost_estimate=pl.CostEstimate(flops=0, bytes_accessed=1 << 20, transcendentals=total.size // 2),
        name="finish",
    )(total, late, *after)


def all_parts(share, n_dp):
    parts = {0: share}
    for b in reversed(bits_of(n_dp)):
        for l in list(parts):
            parts[l | 1 << b] = flip(parts[l], "dp", 1 << b)
    return [parts[l] for l in range(n_dp)]


def on_device(tokens, expert_ids, scores, w_gate, w_up, w_down):
    n_owner, n_dp = lax.axis_size("expert"), lax.axis_size("dp")
    tok_rows, top = expert_ids.shape
    experts = w_gate.shape[0]
    capacity = 2 * tok_rows * top // (experts * n_owner)
    per_chunk = 2 if experts % 2 == 0 else 1
    most = n_owner * capacity
    rows = per_chunk * most
    chunks = experts // per_chunk

    meta = jnp.concatenate([expert_ids.astype(jnp.float32), scores], axis=1)
    feeds = gathered(tokens, "expert")
    metas = [meta] + [
        lax.ppermute(meta, "expert", [(i, (i - k) % n_owner) for i in range(n_owner)])
        for k in gathered_order(n_owner)[1:]
    ]
    info = jnp.stack([lax.axis_index("expert") * experts, lax.axis_index("dp")]).astype(jnp.int32)
    rank_t, rank, wt, sched = route(metas, info, experts, per_chunk, rows)

    shares, sent, parts, total = [], [], [], None
    add = lambda c, after: down(
        parts[c], rank, wt, sched, w_down, total, c, most, c == chunks - 1, n_owner, after
    )
    for c in range(chunks):
        after = ([sent[c - 2]] if c >= 2 else []) + ([shares[c - 3]] if c >= 3 else [])
        send, keep = gate_up(feeds, rank_t, sched, w_gate, w_up, c, rows, most, n_dp, after)
        mine, late, last_sent = partial_sums(send, keep, n_dp)
        sent.append(last_sent)
        if c == chunks - 1 and c > 0:
            total = add(0, [last_sent])
        shares.append(finish(mine, late, [] if total is None else [total]))
        parts.append(all_parts(shares[-1], n_dp))
    for c in range(1 if chunks > 1 else 0, chunks):
        total = add(c, [shares[-1]])
    return returned(total, "expert")


def gathered_order(n):
    near = [d for s in range(1, n // 2) for d in (-s, s)]
    return [0] + near + ([n // 2] if n > 1 else [])


def gathered(x, axis):
    n = lax.axis_size(axis)
    up, down_ = [(i, (i + 1) % n) for i in range(n)], [(i, (i - 1) % n) for i in range(n)]
    below = above = x
    found = [x]
    for _ in range(1, n // 2):
        below, above = lax.ppermute(below, axis, up), lax.ppermute(above, axis, down_)
        found += [below, above]
    if n > 1:
        half = x.shape[0] // 2
        found += [lax.ppermute(below[:half], axis, up), lax.ppermute(above[half:], axis, down_)]
    return found


def returned(partials, axis):
    n = lax.axis_size(axis)
    order = gathered_order(n)
    mixed = partials[0].astype(jnp.float32)
    for k, partial in zip(order[1:], partials[1:]):
        there = lax.ppermute(partial, axis, [(i, (i + k) % n) for i in range(n)])
        mixed = mixed + there.astype(jnp.float32)
    return mixed.astype(jnp.bfloat16)


def solution(mesh):
    in_specs = (
        P(("groups", "expert"), "dp"),
        P(("groups", "expert"), None),
        P(("groups", "expert"), None),
        P("expert", "dp", None),
        P("expert", "dp", None),
        P("expert", None, "dp"),
    )
    out_specs = P(("groups", "expert"), "dp")
    return jax.shard_map(
        on_device, mesh=mesh, in_specs=in_specs, out_specs=out_specs, check_vma=False
    )
```

```python
import functools

import jax
import jax.numpy as jnp
from jax import lax
from jax.experimental import pallas as pl
from jax.experimental.pallas import tpu as pltpu
from jax.sharding import PartitionSpec as P

LANES = 128
VMEM = pl.BlockSpec(memory_space=pltpu.VMEM)
SMEM = pl.BlockSpec(memory_space=pltpu.SMEM)
HERE = pl.BlockSpec(memory_space=pl.ANY)
NOWHERE = -1e6


def bits_of(n):
    return [b for b in range(n.bit_length() - 1)]


def flip(x, axis, k):
    return lax.ppermute(x, axis, [(i, i ^ k) for i in range(lax.axis_size(axis))])


def route_body(n, experts, per_chunk, rows, info, *refs):
    meta, (rank_t, rank, wt, sched) = refs[:n], refs[n:]
    tok, top = meta[0].shape[0], meta[0].shape[1] // 2
    first = info[0].astype(jnp.float32)
    lane = lax.broadcasted_iota(jnp.int32, (tok, LANES), 1).astype(jnp.float32)
    before = (
        lax.broadcasted_iota(jnp.int32, (tok, tok), 0) > lax.broadcasted_iota(jnp.int32, (tok, tok), 1)
    ).astype(jnp.bfloat16)
    seen = jnp.zeros((1, LANES), jnp.float32)
    for s in range(n):
        block = meta[s][...]
        affinity = 1.0 / (1.0 + jnp.exp(-block[:, top:]))
        share = 2.5 * affinity / jnp.sum(affinity, axis=1, keepdims=True)
        named = jnp.zeros((tok, LANES), jnp.float32)
        weight = jnp.zeros((tok, LANES), jnp.float32)
        for k in range(top):
            hit = jnp.where(block[:, k : k + 1] - first == lane, 1.0, 0.0)
            named = named + hit
            weight = weight + hit * share[:, k : k + 1]
        named = jnp.where(lane < experts, named, 0.0)
        place = jnp.dot(before, named.astype(jnp.bfloat16), preferred_element_type=jnp.float32) + seen
        rank[s * tok : (s + 1) * tok, :] = jnp.where(named > 0, place, NOWHERE)
        wt[s * tok : (s + 1) * tok, :] = weight
        seen = seen + jnp.sum(named, axis=0, keepdims=True)
    turned = jnp.transpose(rank[...])[: rank_t.shape[0]]
    rank_t[...] = turned
    count = jnp.sum((turned >= 0).astype(jnp.float32), axis=1, keepdims=True)
    shape = (rank_t.shape[0], LANES)
    j = lax.broadcasted_iota(jnp.int32, shape, 1).astype(jnp.float32)
    e = lax.broadcasted_iota(jnp.int32, shape, 0).astype(jnp.float32)
    ahead = ((seen > count) | ((seen == count) & (j < e))) & (j < experts)
    order = jnp.sum(ahead.astype(jnp.float32), axis=1, keepdims=True)
    large = jnp.where((order == j) & (e < experts), 1.0, 0.0)
    small = jnp.where((order == experts - 1 - j) & (e < experts), 1.0, 0.0)
    expert_a = jnp.sum(e * large, axis=0, keepdims=True)
    count_a = jnp.sum(count * large, axis=0, keepdims=True)
    if per_chunk == 2:
        expert_b = jnp.sum(e * small, axis=0, keepdims=True)
        count_b = jnp.sum(count * small, axis=0, keepdims=True)
    else:
        expert_b, count_b = expert_a, jnp.zeros_like(count_a)
        count_a = jnp.full_like(count_a, rows)
    sched[0:1] = expert_a.astype(jnp.int32)
    sched[1:2] = expert_b.astype(jnp.int32)
    sched[2:3] = count_a.astype(jnp.int32)
    sched[3:4] = (count_a + count_b).astype(jnp.int32)
    sched[4:8] = jnp.full((4, LANES), info[1], jnp.int32)


def route(meta, info, experts, per_chunk, rows):
    tokens = len(meta) * meta[0].shape[0]
    padded = -(-experts // 8) * 8
    return pl.pallas_call(
        functools.partial(route_body, len(meta), experts, per_chunk, rows),
        out_shape=(
            jax.ShapeDtypeStruct((padded, tokens), jnp.float32),
            jax.ShapeDtypeStruct((tokens, LANES), jnp.float32),
            jax.ShapeDtypeStruct((tokens, LANES), jnp.float32),
            jax.ShapeDtypeStruct((8, LANES), jnp.int32),
        ),
        in_specs=[SMEM] + [VMEM] * len(meta),
        out_specs=(VMEM,) * 4,
        name="route",
    )(info, *meta)


def put(out, at, left, right, rows, split):
    most = left.shape[0]
    if right is None:
        out[at] = left
        return
    head = min(rows - most, most)
    out[at[:-2] + (slice(0, head), at[-1])] = left[:head]
    if head < most:
        shared = lax.broadcasted_iota(jnp.int32, (most - head, left.shape[1]), 0) + head < split
        out[at[:-2] + (slice(head, most), at[-1])] = jnp.where(shared, left[head:], right[: most - head])
    out[at[:-2] + (slice(most, rows), at[-1])] = right[most - head :]


def turned_dot(w, x):
    turned = lax.dot_general(w, x, (((0,), (1,)), ((), ())), preferred_element_type=jnp.float32)
    return jnp.transpose(turned).astype(jnp.bfloat16)


def gate_up_body(n, chunk, n_dp, most, after, sched, *refs):
    tokens, (rank_t, w_gate, w_up), refs = refs[:n], refs[n : n + 3], refs[n + 3 + after :]
    send, keep, feed, rows, held, feed_sem, held_sem = refs
    count = rows.shape[0]
    width = send.shape[2] // 2
    split = sched[2, chunk]
    experts = [sched[0, chunk]] + ([sched[1, chunk]] if most < count else [])
    loads = [(w, e) for w in (w_gate, w_up) for e in experts]
    copies = [
        pltpu.make_async_copy(w.at[e], held.at[i], held_sem.at[i]) for i, (w, e) in enumerate(loads)
    ]
    at, feeds = 0, []
    for s in range(n):
        tok = tokens[s].shape[0]
        feeds.append(pltpu.make_async_copy(tokens[s], feed.at[pl.ds(at, tok)], feed_sem.at[s]))
        at += tok
    for copy in feeds:
        copy.start()
    for copy in copies[: len(experts)]:
        copy.start()
    r = lax.broadcasted_iota(jnp.int32, (count, at), 0).astype(jnp.float32)
    pick = jnp.where(r == rank_t[pl.ds(experts[0], 1), :], 1.0, 0.0)
    if most < count:
        pick = pick + jnp.where(count - 1 - r == rank_t[pl.ds(experts[1], 1), :], 1.0, 0.0)
    for copy in feeds:
        copy.wait()
    rows[...] = jnp.dot(
        pick.astype(jnp.bfloat16), feed[...], preferred_element_type=jnp.float32
    ).astype(jnp.bfloat16)
    for m in range(2):
        first = m * len(experts)
        for copy in copies[first : first + len(experts)]:
            copy.wait()
        if m == 0:
            for copy in copies[len(experts) :]:
                copy.start()
        for l in range(n_dp):
            units = pl.ds(pl.multiple_of((l ^ sched[4, 0]) * width, width), width)
            left = turned_dot(held[first, :, units], rows[:most])
            right = turned_dot(held[first + 1, :, units], rows[count - most :]) if most < count else None
            to = (l // 2, slice(None), slice(m * width, (m + 1) * width))
            put(send if l % 2 else keep, to, left, right, count, split)


def gate_up(tokens, rank_t, sched, w_gate, w_up, chunk, rows, most, n_dp, after):
    n, local = len(tokens), tokens[0].shape[1]
    hidden = w_gate.shape[2]
    out = jax.ShapeDtypeStruct((max(n_dp // 2, 1), rows, 2 * hidden // n_dp), jnp.bfloat16)
    mats = 2 * (2 if most < rows else 1)
    return pl.pallas_call(
        functools.partial(gate_up_body, n, chunk, n_dp, most, len(after)),
        out_shape=(out, out),
        in_specs=[SMEM] + [HERE] * n + [VMEM] + [HERE] * (2 + len(after)),
        out_specs=(VMEM, VMEM),
        scratch_shapes=[
            pltpu.VMEM((rank_t.shape[1], local), jnp.bfloat16),
            pltpu.VMEM((rows, local), jnp.bfloat16),
            pltpu.VMEM((mats, local, hidden), jnp.bfloat16),
            pltpu.SemaphoreType.DMA((n,)),
            pltpu.SemaphoreType.DMA((mats,)),
        ],
        compiler_params=pltpu.CompilerParams(vmem_limit_bytes=40 << 20),
        cost_estimate=pl.CostEstimate(
            flops=2 * mats * most * local * hidden,
            bytes_accessed=2 * mats * local * hidden,
            transcendentals=0,
        ),
        name="gate_up",
    )(sched, *tokens, rank_t, w_gate, w_up, *after)


def down_body(n_dp, n_out, chunk, first, most, after, sched, *refs):
    parts, (rank, wt, w_down), refs = refs[:n_dp], refs[n_dp : n_dp + 3], refs[n_dp + 3 :]
    before = None if first else refs[0]
    refs = refs[(0 if first else 1) + after :]
    outs, (hidden, mix, out, held, held_sem) = refs[:-5], refs[-5:]
    rows = hidden.shape[0]
    width = parts[0].shape[-1]
    split = sched[2, chunk]
    experts = [sched[0, chunk]] + ([sched[1, chunk]] if most < rows else [])
    copies = [
        pltpu.make_async_copy(w_down.at[e], held.at[i], held_sem.at[i]) for i, e in enumerate(experts)
    ]
    for copy in copies:
        copy.start()
    for l in range(n_dp):
        at = pl.multiple_of((l ^ sched[4, 0]) * width, width)
        hidden[:, pl.ds(at, width)] = parts[l][0]
    lane = lax.broadcasted_iota(jnp.int32, rank.shape, 1)
    column = lambda ref, e: jnp.sum(jnp.where(lane == e, ref[...], 0.0), axis=1, keepdims=True)
    r = lax.broadcasted_iota(jnp.int32, mix.shape, 1).astype(jnp.float32)
    share = jnp.where(r == column(rank, experts[0]), column(wt, experts[0]), 0.0)
    if most < rows:
        share = share + jnp.where(rows - 1 - r == column(rank, experts[1]), column(wt, experts[1]), 0.0)
    mix[...] = share.astype(jnp.bfloat16)
    for copy in copies:
        copy.wait()
    local = out.shape[1]
    block = 512 if local % 512 == 0 else 256 if local % 256 == 0 else local
    for i in range(local // block):
        cols = slice(i * block, (i + 1) * block)
        left = turned_dot(held[0, :, cols], hidden[:most])
        right = turned_dot(held[1, :, cols], hidden[rows - most :]) if most < rows else None
        put(out, (slice(None), cols), left, right, rows, split)
        total = jnp.dot(mix[...], out[:, cols], preferred_element_type=jnp.float32)
        if not first:
            total = total + before[:, cols]
        tok = total.shape[0] // n_out
        for s in range(n_out):
            outs[s][:, cols] = total[s * tok : (s + 1) * tok].astype(outs[s].dtype)


def down(parts, rank, wt, sched, w_down, total, chunk, most, last, n_owner, after):
    n_dp = len(parts)
    _, rows, width = parts[0].shape
    _, hidden, local = w_down.shape
    tokens = rank.shape[0]
    n_out = n_owner if last else 1
    kind = jnp.bfloat16 if last else jnp.float32
    first = total is None
    mats = 2 if most < rows else 1
    outs = pl.pallas_call(
        functools.partial(down_body, n_dp, n_out, chunk, first, most, len(after)),
        out_shape=(jax.ShapeDtypeStruct((tokens // n_out, local), kind),) * n_out,
        in_specs=[SMEM]
        + [VMEM] * (n_dp + 2)
        + [HERE]
        + ([] if first else [VMEM])
        + [HERE] * len(after),
        out_specs=(VMEM,) * n_out,
        scratch_shapes=[
            pltpu.VMEM((rows, hidden), jnp.bfloat16),
            pltpu.VMEM((tokens, rows), jnp.bfloat16),
            pltpu.VMEM((rows, local), jnp.bfloat16),
            pltpu.VMEM((mats, hidden, local), jnp.bfloat16),
            pltpu.SemaphoreType.DMA((mats,)),
        ],
        compiler_params=pltpu.CompilerParams(vmem_limit_bytes=40 << 20),
        cost_estimate=pl.CostEstimate(
            flops=2 * local * (2 * most * hidden + rows * tokens),
            bytes_accessed=2 * mats * hidden * local + 8 * tokens * local,
            transcendentals=0,
        ),
        name="down",
    )(sched, *parts, rank, wt, w_down, *([] if first else [total]), *after)
    return outs if last else outs[0]


def partial_sums(send, keep, n_dp):
    total = keep.astype(jnp.float32)
    late = jnp.zeros(total.shape, jnp.bfloat16)
    for b in bits_of(n_dp):
        if b > 0:
            total = total + late.astype(jnp.float32)
            send = total[1::2].astype(jnp.bfloat16)
            total = total[0::2]
        late = flip(send, "dp", 1 << b)
    return total, late, send


def finish(total, late, after):
    if after:
        late, *_ = lax.optimization_barrier((late, *after))
    gate_up = total + late.astype(jnp.float32)
    width = gate_up.shape[2] // 2
    return (jax.nn.silu(gate_up[:, :, :width]) * gate_up[:, :, width:]).astype(jnp.bfloat16)


def all_parts(share, n_dp):
    parts = {0: share}
    for b in reversed(bits_of(n_dp)):
        for l in list(parts):
            parts[l | 1 << b] = flip(parts[l], "dp", 1 << b)
    return [parts[l] for l in range(n_dp)]


def on_device(tokens, expert_ids, scores, w_gate, w_up, w_down):
    n_owner, n_dp = lax.axis_size("expert"), lax.axis_size("dp")
    tok_rows, top = expert_ids.shape
    experts = w_gate.shape[0]
    capacity = 2 * tok_rows * top // (experts * n_owner)
    per_chunk = 2 if experts % 2 == 0 else 1
    most = n_owner * capacity
    rows = per_chunk * most
    chunks = experts // per_chunk

    meta = jnp.concatenate([expert_ids.astype(jnp.float32), scores], axis=1)
    feeds = gathered(tokens, "expert")
    metas = [meta] + [
        lax.ppermute(meta, "expert", [(i, (i - k) % n_owner) for i in range(n_owner)])
        for k in gathered_order(n_owner)[1:]
    ]
    info = jnp.stack([lax.axis_index("expert") * experts, lax.axis_index("dp")]).astype(jnp.int32)
    rank_t, rank, wt, sched = route(metas, info, experts, per_chunk, rows)

    shares, sent, parts, total = [], [], [], None
    add = lambda c, after: down(
        parts[c], rank, wt, sched, w_down, total, c, most, c == chunks - 1, n_owner, after
    )
    for c in range(chunks):
        after = ([sent[c - 2]] if c >= 2 else []) + ([shares[c - 3]] if c >= 3 else [])
        send, keep = gate_up(feeds, rank_t, sched, w_gate, w_up, c, rows, most, n_dp, after)
        mine, late, last_sent = partial_sums(send, keep, n_dp)
        sent.append(last_sent)
        if c == chunks - 1 and c > 0:
            total = add(0, [last_sent])
        shares.append(finish(mine, late, [] if total is None else [total]))
        parts.append(all_parts(shares[-1], n_dp))
    for c in range(1 if chunks > 1 else 0, chunks):
        total = add(c, [shares[-1]])
    return returned(total, "expert")


def gathered_order(n):
    near = [d for s in range(1, n // 2) for d in (-s, s)]
    return [0] + near + ([n // 2] if n > 1 else [])


def gathered(x, axis):
    n = lax.axis_size(axis)
    up, down_ = [(i, (i + 1) % n) for i in range(n)], [(i, (i - 1) % n) for i in range(n)]
    below = above = x
    found = [x]
    for _ in range(1, n // 2):
        below, above = lax.ppermute(below, axis, up), lax.ppermute(above, axis, down_)
        found += [below, above]
    if n > 1:
        half = x.shape[0] // 2
        found += [lax.ppermute(below[:half], axis, up), lax.ppermute(above[half:], axis, down_)]
    return found


def returned(partials, axis):
    n = lax.axis_size(axis)
    order = gathered_order(n)
    mixed = partials[0].astype(jnp.float32)
    for k, partial in zip(order[1:], partials[1:]):
        there = lax.ppermute(partial, axis, [(i, (i + k) % n) for i in range(n)])
        mixed = mixed + there.astype(jnp.float32)
    return mixed.astype(jnp.bfloat16)


def solution(mesh):
    in_specs = (
        P(("groups", "expert"), "dp"),
        P(("groups", "expert"), None),
        P(("groups", "expert"), None),
        P("expert", "dp", None),
        P("expert", "dp", None),
        P("expert", None, "dp"),
    )
    out_specs = P(("groups", "expert"), "dp")
    return jax.shard_map(
        on_device, mesh=mesh, in_specs=in_specs, out_specs=out_specs, check_vma=False
    )
```

```python
import functools

import jax
import jax.numpy as jnp
from jax import lax
from jax.experimental import pallas as pl
from jax.experimental.pallas import tpu as pltpu
from jax.sharding import PartitionSpec as P

LANES = 128
VMEM = pl.BlockSpec(memory_space=pltpu.VMEM)
SMEM = pl.BlockSpec(memory_space=pltpu.SMEM)
HERE = pl.BlockSpec(memory_space=pl.ANY)
FAR = pl.BlockSpec(memory_space=pltpu.HBM)
NOWHERE = -1e6


def bits_of(n):
    return [b for b in range(n.bit_length() - 1)]


def flip(x, axis, k):
    return lax.ppermute(x, axis, [(i, i ^ k) for i in range(lax.axis_size(axis))])


def route_body(n, experts, per_chunk, rows, info, *refs):
    meta, (rank, wt, sched) = refs[:n], refs[n:]
    tok, top = meta[0].shape[1], meta[0].shape[0] // 2
    padded = rank.shape[0]
    first = info[0].astype(jnp.float32)
    e = lax.broadcasted_iota(jnp.int32, (padded, tok), 0).astype(jnp.float32)
    before = (
        lax.broadcasted_iota(jnp.int32, (tok, tok), 0) < lax.broadcasted_iota(jnp.int32, (tok, tok), 1)
    ).astype(jnp.bfloat16)
    count = jnp.zeros((padded, 1), jnp.float32)
    for s in range(n):
        ids, scores = meta[s][:top], meta[s][top:]
        affinity = 1.0 / (1.0 + jnp.exp(-scores))
        share = 2.5 * affinity / jnp.sum(affinity, axis=0, keepdims=True)
        named = jnp.zeros((padded, tok), jnp.float32)
        weight = jnp.zeros((padded, tok), jnp.float32)
        for k in range(top):
            hit = jnp.where(ids[k : k + 1] - first == e, 1.0, 0.0)
            named = named + hit
            weight = weight + hit * share[k : k + 1]
        named = jnp.where(e < experts, named, 0.0)
        place = jnp.dot(named.astype(jnp.bfloat16), before, preferred_element_type=jnp.float32) + count
        rank[:, s * tok : (s + 1) * tok] = jnp.where(named > 0, place, NOWHERE)
        wt[:, s * tok : (s + 1) * tok] = weight
        count = count + jnp.sum(named, axis=1, keepdims=True)
    shape = (padded, LANES)
    j = lax.broadcasted_iota(jnp.int32, shape, 1).astype(jnp.float32)
    e = lax.broadcasted_iota(jnp.int32, shape, 0).astype(jnp.float32)
    other = jnp.sum(jnp.where(e == j, count, 0.0), axis=0, keepdims=True)
    ahead = ((other > count) | ((other == count) & (j < e))) & (j < experts)
    order = jnp.sum(ahead.astype(jnp.float32), axis=1, keepdims=True)
    large = jnp.where((order == j) & (e < experts), 1.0, 0.0)
    small = jnp.where((order == experts - 1 - j) & (e < experts), 1.0, 0.0)
    expert_a = jnp.sum(e * large, axis=0, keepdims=True)
    count_a = jnp.sum(count * large, axis=0, keepdims=True)
    if per_chunk == 2:
        expert_b = jnp.sum(e * small, axis=0, keepdims=True)
    else:
        expert_b = expert_a
        count_a = jnp.full_like(count_a, rows)
    sched[0:1] = expert_a.astype(jnp.int32)
    sched[1:2] = expert_b.astype(jnp.int32)
    sched[2:3] = count_a.astype(jnp.int32)
    sched[3:8] = jnp.full((5, LANES), info[1], jnp.int32)


def route(meta, info, experts, per_chunk, rows):
    tokens = len(meta) * meta[0].shape[1]
    padded = -(-experts // 8) * 8
    return pl.pallas_call(
        functools.partial(route_body, len(meta), experts, per_chunk, rows),
        out_shape=(
            jax.ShapeDtypeStruct((padded, tokens), jnp.float32),
            jax.ShapeDtypeStruct((padded, tokens), jnp.float32),
            jax.ShapeDtypeStruct((8, LANES), jnp.int32),
        ),
        in_specs=[SMEM] + [VMEM] * len(meta),
        out_specs=(VMEM,) * 3,
        name="route",
    )(info, *meta)


def put(out, at, sides, rows, split):
    left, right = sides[0], sides[-1]
    most = left.shape[0]
    if len(sides) == 1:
        out[at] = left
        return
    head = min(rows - most, most)
    out[at[:-2] + (slice(0, head), at[-1])] = left[:head]
    if head < most:
        shared = lax.broadcasted_iota(jnp.int32, (most - head, left.shape[1]), 0) + head < split
        out[at[:-2] + (slice(head, most), at[-1])] = jnp.where(shared, left[head:], right[: most - head])
    out[at[:-2] + (slice(most, rows), at[-1])] = right[most - head :]


def gate_up_body(n, chunk, n_dp, most, after, sched_in, *refs):
    tokens, (rank_in, w_gate, w_up), refs = refs[:n], refs[n : n + 3], refs[n + 3 + after :]
    send, keep, sched, rank, feed, rows, held, small_sem, feed_sem, held_sem = refs
    count = rows.shape[0]
    width = send.shape[2] // 2
    order = pltpu.make_async_copy(sched_in, sched, small_sem.at[0])
    ranks = pltpu.make_async_copy(rank_in, rank, small_sem.at[1])
    order.start()
    ranks.start()
    at, feeds = 0, []
    for s in range(n):
        tok = tokens[s].shape[0]
        feeds.append(pltpu.make_async_copy(tokens[s], feed.at[pl.ds(at, tok)], feed_sem.at[s]))
        at += tok
    for copy in feeds:
        copy.start()
    order.wait()
    split = sched[2, chunk]
    experts = [sched[0, chunk]] + ([sched[1, chunk]] if most < count else [])
    pieces = list(range(1, n_dp, 2)) + list(range(0, n_dp, 2))
    copies = {}
    for l in pieces:
        units = pl.ds(pl.multiple_of((l ^ sched[3, 0]) * width, width), width)
        for m, w in enumerate((w_gate, w_up)):
            for x, e in enumerate(experts):
                i = m * len(experts) + x
                copies[l, m, x] = pltpu.make_async_copy(
                    w.at[e, :, units], held.at[i, :, pl.ds(l * width, width)], held_sem.at[l, i]
                )
                copies[l, m, x].start()
    ranks.wait()
    r = lax.broadcasted_iota(jnp.int32, (count, at), 0).astype(jnp.float32)
    pick = jnp.where(r == rank[pl.ds(experts[0], 1), :], 1.0, 0.0)
    if most < count:
        pick = pick + jnp.where(count - 1 - r == rank[pl.ds(experts[1], 1), :], 1.0, 0.0)
    for copy in feeds:
        copy.wait()
    rows[...] = jnp.dot(
        pick.astype(jnp.bfloat16), feed[...], preferred_element_type=jnp.float32
    ).astype(jnp.bfloat16)
    for l in pieces:
        units = slice(l * width, (l + 1) * width)
        for m in range(2):
            sides = []
            for x, part in enumerate((rows[:most], rows[count - most :])[: len(experts)]):
                copies[l, m, x].wait()
                sides.append(
                    jnp.dot(
                        part, held[m * len(experts) + x, :, units], preferred_element_type=jnp.float32
                    ).astype(jnp.bfloat16)
                )
            to = (l // 2, slice(None), slice(m * width, (m + 1) * width))
            put(send if l % 2 else keep, to, sides, count, split)


def gate_up(tokens, rank, sched, w_gate, w_up, chunk, rows, most, n_dp, after):
    n, local = len(tokens), tokens[0].shape[1]
    hidden = w_gate.shape[2]
    out = jax.ShapeDtypeStruct((max(n_dp // 2, 1), rows, 2 * hidden // n_dp), jnp.bfloat16)
    mats = 2 * (2 if most < rows else 1)
    return pl.pallas_call(
        functools.partial(gate_up_body, n, chunk, n_dp, most, len(after)),
        out_shape=(out, out),
        in_specs=[FAR, FAR] + [HERE] * (n - 1) + [FAR] * 3 + [HERE] * len(after),
        out_specs=(VMEM, VMEM),
        scratch_shapes=[
            pltpu.SMEM(sched.shape, jnp.int32),
            pltpu.VMEM(rank.shape, jnp.float32),
            pltpu.VMEM((rank.shape[1], local), jnp.bfloat16),
            pltpu.VMEM((rows, local), jnp.bfloat16),
            pltpu.VMEM((mats, local, hidden), jnp.bfloat16),
            pltpu.SemaphoreType.DMA((2,)),
            pltpu.SemaphoreType.DMA((n,)),
            pltpu.SemaphoreType.DMA((n_dp, mats)),
        ],
        compiler_params=pltpu.CompilerParams(vmem_limit_bytes=40 << 20),
        cost_estimate=pl.CostEstimate(
            flops=8 * mats * most * local * hidden,
            bytes_accessed=2 * mats * local * hidden,
            transcendentals=0,
        ),
        name="gate_up",
    )(sched, *tokens, rank, w_gate, w_up, *after)


def down_body(n_dp, cuts, chunk, first, most, after, sched_in, *refs):
    parts, (rank_in, wt_in, w_down), refs = refs[:n_dp], refs[n_dp : n_dp + 3], refs[n_dp + 3 :]
    before = None if first else refs[0]
    refs = refs[(0 if first else 1) + after :]
    outs, refs = refs[: len(cuts)], refs[len(cuts) :]
    sched, rank, wt, hidden, mix, out, held, small_sem, held_sem = refs
    rows = hidden.shape[0]
    width = parts[0].shape[-1]
    local = out.shape[1]
    smalls = [
        pltpu.make_async_copy(source, to, small_sem.at[i])
        for i, (source, to) in enumerate(((sched_in, sched), (rank_in, rank), (wt_in, wt)))
    ]
    for copy in smalls:
        copy.start()
    smalls[0].wait()
    split = sched[2, chunk]
    experts = [sched[0, chunk]] + ([sched[1, chunk]] if most < rows else [])
    block = 512 if local % 512 == 0 else 256 if local % 256 == 0 else local
    copies = {}
    for i in range(local // block):
        for x, e in enumerate(experts):
            cols = pl.ds(i * block, block)
            copies[i, x] = pltpu.make_async_copy(
                w_down.at[e, :, cols], held.at[x, :, cols], held_sem.at[i, x]
            )
            copies[i, x].start()
    for l in range(n_dp):
        at = pl.multiple_of((l ^ sched[3, 0]) * width, width)
        hidden[:, pl.ds(at, width)] = parts[l][0]
    smalls[1].wait()
    smalls[2].wait()
    r = lax.broadcasted_iota(jnp.int32, mix.shape, 0).astype(jnp.float32)
    row = lambda ref, e: ref[pl.ds(e, 1), :]
    share = jnp.where(r == row(rank, experts[0]), row(wt, experts[0]), 0.0)
    if most < rows:
        share = share + jnp.where(rows - 1 - r == row(rank, experts[1]), row(wt, experts[1]), 0.0)
    mix[...] = share.astype(jnp.bfloat16)
    for i in range(local // block):
        cols = slice(i * block, (i + 1) * block)
        sides = []
        for x, part in enumerate((hidden[:most], hidden[rows - most :])[: len(experts)]):
            copies[i, x].wait()
            sides.append(
                jnp.dot(part, held[x, :, cols], preferred_element_type=jnp.float32).astype(jnp.bfloat16)
            )
        put(out, (slice(None), cols), sides, rows, split)
        total = lax.dot_general(
            mix[...], out[:, cols], (((0,), (0,)), ((), ())), preferred_element_type=jnp.float32
        )
        if not first:
            total = total + before[:, cols]
        at = 0
        for to, cut in zip(outs, cuts):
            to[:, cols] = total[at : at + cut].astype(to.dtype)
            at += cut


def down(parts, rank, wt, sched, w_down, total, chunk, most, cuts, after):
    n_dp = len(parts)
    _, rows, width = parts[0].shape
    _, hidden, local = w_down.shape
    tokens = rank.shape[1]
    first, last = total is None, len(cuts) > 1
    kind = jnp.bfloat16 if last else jnp.float32
    mats = 2 if most < rows else 1
    outs = pl.pallas_call(
        functools.partial(down_body, n_dp, cuts, chunk, first, most, len(after)),
        out_shape=tuple(jax.ShapeDtypeStruct((cut, local), kind) for cut in cuts),
        in_specs=[FAR]
        + [VMEM] * n_dp
        + [FAR] * 3
        + ([] if first else [VMEM])
        + [HERE] * len(after),
        out_specs=(VMEM,) * len(cuts),
        scratch_shapes=[
            pltpu.SMEM(sched.shape, jnp.int32),
            pltpu.VMEM(rank.shape, jnp.float32),
            pltpu.VMEM(rank.shape, jnp.float32),
            pltpu.VMEM((rows, hidden), jnp.bfloat16),
            pltpu.VMEM((rows, tokens), jnp.bfloat16),
            pltpu.VMEM((rows, local), jnp.bfloat16),
            pltpu.VMEM((mats, hidden, local), jnp.bfloat16),
            pltpu.SemaphoreType.DMA((3,)),
            pltpu.SemaphoreType.DMA((local // 256 + 1, mats)),
        ],
        compiler_params=pltpu.CompilerParams(vmem_limit_bytes=40 << 20),
        cost_estimate=pl.CostEstimate(
            flops=8 * local * (mats * most * hidden + rows * tokens),
            bytes_accessed=2 * mats * hidden * local + 8 * tokens * local,
            transcendentals=0,
        ),
        name="down",
    )(sched, *parts, rank, wt, w_down, *([] if first else [total]), *after)
    return outs if last else outs[0]


def partial_sums(send, keep, n_dp):
    total = keep.astype(jnp.float32)
    late = jnp.zeros(total.shape, jnp.bfloat16)
    for b in bits_of(n_dp):
        if b > 0:
            total = total + late.astype(jnp.float32)
            send = total[1::2].astype(jnp.bfloat16)
            total = total[0::2]
        late = flip(send, "dp", 1 << b)
    return total, late, send


def finish(total, late, after):
    if after:
        late, *_ = lax.optimization_barrier((late, *after))
    gate_up = total + late.astype(jnp.float32)
    width = gate_up.shape[2] // 2
    return (jax.nn.silu(gate_up[:, :, :width]) * gate_up[:, :, width:]).astype(jnp.bfloat16)


def all_parts(share, n_dp):
    parts = {0: share}
    for b in reversed(bits_of(n_dp)):
        for l in list(parts):
            parts[l | 1 << b] = flip(parts[l], "dp", 1 << b)
    return [parts[l] for l in range(n_dp)]


def on_device(tokens, expert_ids, scores, w_gate, w_up, w_down):
    n_owner, n_dp = lax.axis_size("expert"), lax.axis_size("dp")
    tok_rows, top = expert_ids.shape
    experts = w_gate.shape[0]
    capacity = 2 * tok_rows * top // (experts * n_owner)
    per_chunk = 2 if experts % 2 == 0 else 1
    most = n_owner * capacity
    rows = per_chunk * most
    chunks = experts // per_chunk

    meta = jnp.concatenate([expert_ids.T.astype(jnp.float32), scores.T], axis=0)
    feeds = gathered(tokens, "expert")
    metas = [meta] + [
        lax.ppermute(meta, "expert", [(i, (i - k) % n_owner) for i in range(n_owner)])
        for k in gathered_order(n_owner)[1:]
    ]
    info = jnp.stack([lax.axis_index("expert") * experts, lax.axis_index("dp")]).astype(jnp.int32)
    rank, wt, sched = route(metas, info, experts, per_chunk, rows)

    shares, sent, parts, total = [], [], [], None
    cuts = [feed.shape[0] for feed in feeds]

    def add(c, after):
        return down(
            parts[c], rank, wt, sched, w_down, total, c, most,
            cuts if c == chunks - 1 else [sum(cuts)], after,
        )

    for c in range(chunks):
        after = ([sent[c - 1]] if c >= 1 else []) + ([shares[c - 2]] if c >= 2 else [])
        send, keep = gate_up(feeds, rank, sched, w_gate, w_up, c, rows, most, n_dp, after)
        mine, late, last_sent = partial_sums(send, keep, n_dp)
        sent.append(last_sent)
        if c == chunks - 1 and c > 0:
            total = add(0, [last_sent, shares[-1]])
        shares.append(finish(mine, late, [] if total is None else [total]))
        parts.append(all_parts(shares[-1], n_dp))
    for c in range(1 if chunks > 1 else 0, chunks):
        total = add(c, [shares[-1]] if c == 1 else [])
    return returned(total, "expert") if n_owner > 1 else total[0].astype(jnp.bfloat16)


def gathered_order(n):
    near = [d for s in range(1, n // 2) for d in (-s, s)]
    return [0] + near + ([n // 2] if n > 1 else [])


def gathered(x, axis):
    n = lax.axis_size(axis)
    up, down_ = [(i, (i + 1) % n) for i in range(n)], [(i, (i - 1) % n) for i in range(n)]
    below = above = x
    found = [x]
    for _ in range(1, n // 2):
        below, above = lax.ppermute(below, axis, up), lax.ppermute(above, axis, down_)
        found += [below, above]
    if n > 1:
        half = x.shape[0] // 2
        found += [lax.ppermute(below[:half], axis, up), lax.ppermute(above[half:], axis, down_)]
    return found


def returned(partials, axis):
    n = lax.axis_size(axis)
    up, down_ = [(i, (i + 1) % n) for i in range(n)], [(i, (i - 1) % n) for i in range(n)]
    wide = lambda x: x.astype(jnp.float32)
    near = {0: partials[0]}
    for k, partial in zip(gathered_order(n)[1:-1], partials[1:-2]):
        near[k] = partial
    half = partials[-1].shape[0]
    low, high = lax.ppermute(partials[-2], axis, down_), lax.ppermute(partials[-1], axis, up)
    halves = True
    for s in range(n // 2 - 1, 0, -1):
        a, b = wide(near[-s]), wide(near[s])
        if halves:
            a = jnp.concatenate([a[:half] + wide(low), a[half:]], axis=0)
            b = jnp.concatenate([b[:half], b[half:] + wide(high)], axis=0)
        else:
            a, b = a + wide(low), b + wide(high)
        low = lax.ppermute(a.astype(jnp.bfloat16), axis, down_)
        high = lax.ppermute(b.astype(jnp.bfloat16), axis, up)
        halves = False
    if halves:
        back = jnp.concatenate([wide(low), wide(high)], axis=0)
    else:
        back = wide(low) + wide(high)
    return (wide(near[0]) + back).astype(jnp.bfloat16)


def solution(mesh):
    in_specs = (
        P(("groups", "expert"), "dp"),
        P(("groups", "expert"), None),
        P(("groups", "expert"), None),
        P("expert", "dp", None),
        P("expert", "dp", None),
        P("expert", None, "dp"),
    )
    out_specs = P(("groups", "expert"), "dp")
    return jax.shard_map(
        on_device, mesh=mesh, in_specs=in_specs, out_specs=out_specs, check_vma=False
    )
```

```python
import functools

import jax
import jax.numpy as jnp
from jax import lax
from jax.experimental import pallas as pl
from jax.experimental.pallas import tpu as pltpu
from jax.sharding import PartitionSpec as P

LANES = 128
VMEM = pl.BlockSpec(memory_space=pltpu.VMEM)
SMEM = pl.BlockSpec(memory_space=pltpu.SMEM)
HERE = pl.BlockSpec(memory_space=pl.ANY)
FAR = pl.BlockSpec(memory_space=pltpu.HBM)
NOWHERE = -1e6


def bits_of(n):
    return [b for b in range(n.bit_length() - 1)]


def flip(x, axis, k):
    return lax.ppermute(x, axis, [(i, i ^ k) for i in range(lax.axis_size(axis))])


def route_body(n, experts, per_chunk, rows, info, *refs):
    meta, (rank, wt, sched) = refs[:n], refs[n:]
    tok, top = meta[0].shape[1], meta[0].shape[0] // 2
    padded = rank.shape[0]
    first = info[0].astype(jnp.float32)
    e = lax.broadcasted_iota(jnp.int32, (padded, tok), 0).astype(jnp.float32)
    before = (
        lax.broadcasted_iota(jnp.int32, (tok, tok), 0) < lax.broadcasted_iota(jnp.int32, (tok, tok), 1)
    ).astype(jnp.bfloat16)
    count = jnp.zeros((padded, 1), jnp.float32)
    for s in range(n):
        ids, scores = meta[s][:top], meta[s][top:]
        affinity = 1.0 / (1.0 + jnp.exp(-scores))
        share = 2.5 * affinity / jnp.sum(affinity, axis=0, keepdims=True)
        named = jnp.zeros((padded, tok), jnp.float32)
        weight = jnp.zeros((padded, tok), jnp.float32)
        for k in range(top):
            hit = jnp.where(ids[k : k + 1] - first == e, 1.0, 0.0)
            named = named + hit
            weight = weight + hit * share[k : k + 1]
        named = jnp.where(e < experts, named, 0.0)
        place = jnp.dot(named.astype(jnp.bfloat16), before, preferred_element_type=jnp.float32) + count
        rank[:, s * tok : (s + 1) * tok] = jnp.where(named > 0, place, NOWHERE)
        wt[:, s * tok : (s + 1) * tok] = weight
        count = count + jnp.sum(named, axis=1, keepdims=True)
    shape = (padded, LANES)
    j = lax.broadcasted_iota(jnp.int32, shape, 1).astype(jnp.float32)
    e = lax.broadcasted_iota(jnp.int32, shape, 0).astype(jnp.float32)
    other = jnp.sum(jnp.where(e == j, count, 0.0), axis=0, keepdims=True)
    ahead = ((other > count) | ((other == count) & (j < e))) & (j < experts)
    order = jnp.sum(ahead.astype(jnp.float32), axis=1, keepdims=True)
    large = jnp.where((order == j) & (e < experts), 1.0, 0.0)
    small = jnp.where((order == experts - 1 - j) & (e < experts), 1.0, 0.0)
    expert_a = jnp.sum(e * large, axis=0, keepdims=True)
    count_a = jnp.sum(count * large, axis=0, keepdims=True)
    if per_chunk == 2:
        expert_b = jnp.sum(e * small, axis=0, keepdims=True)
    else:
        expert_b = expert_a
        count_a = jnp.full_like(count_a, rows)
    sched[0:1] = expert_a.astype(jnp.int32)
    sched[1:2] = expert_b.astype(jnp.int32)
    sched[2:3] = count_a.astype(jnp.int32)
    sched[3:8] = jnp.full((5, LANES), info[1], jnp.int32)


def route(meta, info, experts, per_chunk, rows):
    tokens = len(meta) * meta[0].shape[1]
    padded = -(-experts // 8) * 8
    return pl.pallas_call(
        functools.partial(route_body, len(meta), experts, per_chunk, rows),
        out_shape=(
            jax.ShapeDtypeStruct((padded, tokens), jnp.float32),
            jax.ShapeDtypeStruct((padded, tokens), jnp.float32),
            jax.ShapeDtypeStruct((8, LANES), jnp.int32),
        ),
        in_specs=[SMEM] + [VMEM] * len(meta),
        out_specs=(VMEM,) * 3,
        compiler_params=pltpu.CompilerParams(vmem_limit_bytes=40 << 20),
        name="route",
    )(info, *meta)


def put(out, at, sides, rows, split):
    left, right = sides[0], sides[-1]
    most = left.shape[0]
    if len(sides) == 1:
        out[at] = left
        return
    head = min(rows - most, most)
    out[at[:-2] + (slice(0, head), at[-1])] = left[:head]
    if head < most:
        shared = lax.broadcasted_iota(jnp.int32, (most - head, left.shape[1]), 0) + head < split
        out[at[:-2] + (slice(head, most), at[-1])] = jnp.where(shared, left[head:], right[: most - head])
    out[at[:-2] + (slice(most, rows), at[-1])] = right[most - head :]


def gate_up_body(n, chunk, n_dp, most, after, sched_in, *refs):
    tokens, (rank_in, w_gate, w_up), refs = refs[:n], refs[n : n + 3], refs[n + 3 + after :]
    send, keep, sched, rank, feed, rows, held, small_sem, feed_sem, held_sem = refs
    count = rows.shape[0]
    width = send.shape[2] // 2
    order = pltpu.make_async_copy(sched_in, sched, small_sem.at[0])
    ranks = pltpu.make_async_copy(rank_in, rank, small_sem.at[1])
    order.start()
    ranks.start()
    at, feeds = 0, []
    for s in range(n):
        tok = tokens[s].shape[0]
        feeds.append(pltpu.make_async_copy(tokens[s], feed.at[pl.ds(at, tok)], feed_sem.at[s]))
        at += tok
    for copy in feeds:
        copy.start()
    order.wait()
    split = sched[2, chunk]
    experts = [sched[0, chunk]] + ([sched[1, chunk]] if most < count else [])
    pieces = list(range(1, n_dp, 2)) + list(range(0, n_dp, 2))
    copies = {}
    for l in pieces:
        units = pl.ds(pl.multiple_of((l ^ sched[3, 0]) * width, width), width)
        for m, w in enumerate((w_gate, w_up)):
            for x, e in enumerate(experts):
                i = m * len(experts) + x
                copies[l, m, x] = pltpu.make_async_copy(
                    w.at[e, :, units], held.at[i, :, pl.ds(l * width, width)], held_sem.at[l, i]
                )

    def fetch(l):
        for m in range(2):
            for x in range(len(experts)):
                copies[l, m, x].start()

    fetch(pieces[0])
    ranks.wait()
    r = lax.broadcasted_iota(jnp.int32, (count, at), 0).astype(jnp.float32)
    pick = jnp.where(r == rank[pl.ds(experts[0], 1), :], 1.0, 0.0)
    if most < count:
        pick = pick + jnp.where(count - 1 - r == rank[pl.ds(experts[1], 1), :], 1.0, 0.0)
    for copy in feeds:
        copy.wait()
    rows[...] = jnp.dot(
        pick.astype(jnp.bfloat16), feed[...], preferred_element_type=jnp.float32
    ).astype(jnp.bfloat16)
    for l, ahead in zip(pieces, pieces[1:] + [None]):
        units = slice(l * width, (l + 1) * width)
        if ahead is not None:
            fetch(ahead)
        for m in range(2):
            sides = []
            for x, part in enumerate((rows[:most], rows[count - most :])[: len(experts)]):
                copies[l, m, x].wait()
                sides.append(
                    jnp.dot(
                        part, held[m * len(experts) + x, :, units], preferred_element_type=jnp.float32
                    ).astype(jnp.bfloat16)
                )
            to = (l // 2, slice(None), slice(m * width, (m + 1) * width))
            put(send if l % 2 else keep, to, sides, count, split)


def gate_up(tokens, rank, sched, w_gate, w_up, chunk, rows, most, n_dp, after):
    n, local = len(tokens), tokens[0].shape[1]
    hidden = w_gate.shape[2]
    out = jax.ShapeDtypeStruct((max(n_dp // 2, 1), rows, 2 * hidden // n_dp), jnp.bfloat16)
    mats = 2 * (2 if most < rows else 1)
    return pl.pallas_call(
        functools.partial(gate_up_body, n, chunk, n_dp, most, len(after)),
        out_shape=(out, out),
        in_specs=[FAR, FAR] + [HERE] * (n - 1) + [FAR] * 3 + [HERE] * len(after),
        out_specs=(VMEM, VMEM),
        scratch_shapes=[
            pltpu.SMEM(sched.shape, jnp.int32),
            pltpu.VMEM(rank.shape, jnp.float32),
            pltpu.VMEM((rank.shape[1], local), jnp.bfloat16),
            pltpu.VMEM((rows, local), jnp.bfloat16),
            pltpu.VMEM((mats, local, hidden), jnp.bfloat16),
            pltpu.SemaphoreType.DMA((2,)),
            pltpu.SemaphoreType.DMA((n,)),
            pltpu.SemaphoreType.DMA((n_dp, mats)),
        ],
        compiler_params=pltpu.CompilerParams(vmem_limit_bytes=40 << 20),
        cost_estimate=pl.CostEstimate(
            flops=8 * mats * most * local * hidden,
            bytes_accessed=2 * mats * local * hidden,
            transcendentals=0,
        ),
        name="gate_up",
    )(sched, *tokens, rank, w_gate, w_up, *after)


def down_body(n_dp, cuts, chunk, first, most, after, sched_in, *refs):
    parts, (rank_in, wt_in, w_down), refs = refs[:n_dp], refs[n_dp : n_dp + 3], refs[n_dp + 3 :]
    before = None if first else refs[0]
    refs = refs[(0 if first else 1) + after :]
    outs, refs = refs[: len(cuts)], refs[len(cuts) :]
    sched, rank, wt, hidden, mix, out, held, small_sem, held_sem = refs
    rows = hidden.shape[0]
    width = parts[0].shape[-1]
    local = out.shape[1]
    smalls = [
        pltpu.make_async_copy(source, to, small_sem.at[i])
        for i, (source, to) in enumerate(((sched_in, sched), (rank_in, rank), (wt_in, wt)))
    ]
    for copy in smalls:
        copy.start()
    smalls[0].wait()
    split = sched[2, chunk]
    experts = [sched[0, chunk]] + ([sched[1, chunk]] if most < rows else [])
    block = 512 if local % 512 == 0 else 256 if local % 256 == 0 else local
    copies = {}
    for i in range(local // block):
        for x, e in enumerate(experts):
            cols = pl.ds(i * block, block)
            copies[i, x] = pltpu.make_async_copy(
                w_down.at[e, :, cols], held.at[x, :, cols], held_sem.at[i, x]
            )
            copies[i, x].start()
    for l in range(n_dp):
        at = pl.multiple_of((l ^ sched[3, 0]) * width, width)
        hidden[:, pl.ds(at, width)] = parts[l][0]
    smalls[1].wait()
    smalls[2].wait()
    r = lax.broadcasted_iota(jnp.int32, mix.shape, 0).astype(jnp.float32)
    row = lambda ref, e: ref[pl.ds(e, 1), :]
    share = jnp.where(r == row(rank, experts[0]), row(wt, experts[0]), 0.0)
    if most < rows:
        share = share + jnp.where(rows - 1 - r == row(rank, experts[1]), row(wt, experts[1]), 0.0)
    mix[...] = share.astype(jnp.bfloat16)
    for i in range(local // block):
        cols = slice(i * block, (i + 1) * block)
        sides = []
        for x, part in enumerate((hidden[:most], hidden[rows - most :])[: len(experts)]):
            copies[i, x].wait()
            sides.append(
                jnp.dot(part, held[x, :, cols], preferred_element_type=jnp.float32).astype(jnp.bfloat16)
            )
        put(out, (slice(None), cols), sides, rows, split)
        total = lax.dot_general(
            mix[...], out[:, cols], (((0,), (0,)), ((), ())), preferred_element_type=jnp.float32
        )
        if not first:
            total = total + before[:, cols]
        at = 0
        for to, cut in zip(outs, cuts):
            to[:, cols] = total[at : at + cut].astype(to.dtype)
            at += cut


def down(parts, rank, wt, sched, w_down, total, chunk, most, cuts, after):
    n_dp = len(parts)
    _, rows, width = parts[0].shape
    _, hidden, local = w_down.shape
    tokens = rank.shape[1]
    first, last = total is None, len(cuts) > 1
    kind = jnp.bfloat16 if last else jnp.float32
    mats = 2 if most < rows else 1
    outs = pl.pallas_call(
        functools.partial(down_body, n_dp, cuts, chunk, first, most, len(after)),
        out_shape=tuple(jax.ShapeDtypeStruct((cut, local), kind) for cut in cuts),
        in_specs=[FAR]
        + [VMEM] * n_dp
        + [FAR] * 3
        + ([] if first else [VMEM])
        + [HERE] * len(after),
        out_specs=(VMEM,) * len(cuts),
        scratch_shapes=[
            pltpu.SMEM(sched.shape, jnp.int32),
            pltpu.VMEM(rank.shape, jnp.float32),
            pltpu.VMEM(rank.shape, jnp.float32),
            pltpu.VMEM((rows, hidden), jnp.bfloat16),
            pltpu.VMEM((rows, tokens), jnp.bfloat16),
            pltpu.VMEM((rows, local), jnp.bfloat16),
            pltpu.VMEM((mats, hidden, local), jnp.bfloat16),
            pltpu.SemaphoreType.DMA((3,)),
            pltpu.SemaphoreType.DMA((local // 256 + 1, mats)),
        ],
        compiler_params=pltpu.CompilerParams(vmem_limit_bytes=40 << 20),
        cost_estimate=pl.CostEstimate(
            flops=8 * local * (mats * most * hidden + rows * tokens),
            bytes_accessed=2 * mats * hidden * local + 8 * tokens * local,
            transcendentals=0,
        ),
        name="down",
    )(sched, *parts, rank, wt, w_down, *([] if first else [total]), *after)
    return outs if last else outs[0]


def partial_sums(send, keep, n_dp):
    total = keep.astype(jnp.float32)
    late = jnp.zeros(total.shape, jnp.bfloat16)
    for b in bits_of(n_dp):
        if b > 0:
            total = total + late.astype(jnp.float32)
            send = total[1::2].astype(jnp.bfloat16)
            total = total[0::2]
        late = flip(send, "dp", 1 << b)
    return total, late, send


def finish(total, late, after):
    if after:
        late, *_ = lax.optimization_barrier((late, *after))
    gate_up = total + late.astype(jnp.float32)
    width = gate_up.shape[2] // 2
    return (jax.nn.silu(gate_up[:, :, :width]) * gate_up[:, :, width:]).astype(jnp.bfloat16)


def all_parts(share, n_dp):
    parts = {0: share}
    for b in reversed(bits_of(n_dp)):
        for l in list(parts):
            parts[l | 1 << b] = flip(parts[l], "dp", 1 << b)
    return [parts[l] for l in range(n_dp)]


def on_device(tokens, expert_ids, scores, w_gate, w_up, w_down):
    n_owner, n_dp = lax.axis_size("expert"), lax.axis_size("dp")
    tok_rows, top = expert_ids.shape
    experts = w_gate.shape[0]
    capacity = 2 * tok_rows * top // (experts * n_owner)
    per_chunk = 2 if experts % 2 == 0 else 1
    most = n_owner * capacity
    rows = per_chunk * most
    chunks = experts // per_chunk

    meta = jnp.concatenate([expert_ids.T.astype(jnp.float32), scores.T], axis=0)
    feeds = gathered(tokens, "expert")
    metas = [meta] + [
        lax.ppermute(meta, "expert", [(i, (i - k) % n_owner) for i in range(n_owner)])
        for k in gathered_order(n_owner)[1:]
    ]
    info = jnp.stack([lax.axis_index("expert") * experts, lax.axis_index("dp")]).astype(jnp.int32)
    rank, wt, sched = route(metas, info, experts, per_chunk, rows)

    shares, sent, parts, total = [], [], [], None
    cuts = [feed.shape[0] for feed in feeds]

    def add(c, after):
        return down(
            parts[c], rank, wt, sched, w_down, total, c, most,
            cuts if c == chunks - 1 else [sum(cuts)], after,
        )

    for c in range(chunks):
        after = ([sent[c - 1]] if c >= 1 else []) + ([shares[c - 2]] if c >= 2 else [])
        send, keep = gate_up(feeds, rank, sched, w_gate, w_up, c, rows, most, n_dp, after)
        mine, late, last_sent = partial_sums(send, keep, n_dp)
        sent.append(last_sent)
        if c > 0:
            parts.append(all_parts(lax.optimization_barrier((shares[-1], last_sent))[0], n_dp))
        early = range(min(2, c)) if c == chunks - 1 else []
        for d in early:
            total = add(d, [last_sent, shares[-1]])
        shares.append(finish(mine, late, [total] if early else []))
    parts.append(all_parts(shares[-1], n_dp))
    for c in range(len(early), chunks):
        total = add(c, [shares[-1]] if c < chunks - 1 else [])
    return returned(total, "expert") if n_owner > 1 else total[0].astype(jnp.bfloat16)


def gathered_order(n):
    near = [d for s in range(1, n // 2) for d in (-s, s)]
    return [0] + near + ([n // 2] if n > 1 else [])


def gathered(x, axis):
    n = lax.axis_size(axis)
    up, down_ = [(i, (i + 1) % n) for i in range(n)], [(i, (i - 1) % n) for i in range(n)]
    below = above = x
    found = [x]
    for _ in range(1, n // 2):
        below, above = lax.ppermute(below, axis, up), lax.ppermute(above, axis, down_)
        found += [below, above]
    if n > 1:
        half = x.shape[0] // 2
        found += [lax.ppermute(below[:half], axis, up), lax.ppermute(above[half:], axis, down_)]
    return found


def returned(partials, axis):
    n = lax.axis_size(axis)
    up, down_ = [(i, (i + 1) % n) for i in range(n)], [(i, (i - 1) % n) for i in range(n)]
    wide = lambda x: x.astype(jnp.float32)
    near = {0: partials[0]}
    for k, partial in zip(gathered_order(n)[1:-1], partials[1:-2]):
        near[k] = partial
    half = partials[-1].shape[0]
    low, high = lax.ppermute(partials[-2], axis, down_), lax.ppermute(partials[-1], axis, up)
    halves = True
    for s in range(n // 2 - 1, 0, -1):
        a, b = wide(near[-s]), wide(near[s])
        if halves:
            a = jnp.concatenate([a[:half] + wide(low), a[half:]], axis=0)
            b = jnp.concatenate([b[:half], b[half:] + wide(high)], axis=0)
        else:
            a, b = a + wide(low), b + wide(high)
        low = lax.ppermute(a.astype(jnp.bfloat16), axis, down_)
        high = lax.ppermute(b.astype(jnp.bfloat16), axis, up)
        halves = False
    if halves:
        back = jnp.concatenate([wide(low), wide(high)], axis=0)
    else:
        back = wide(low) + wide(high)
    return (wide(near[0]) + back).astype(jnp.bfloat16)


def solution(mesh):
    in_specs = (
        P(("groups", "expert"), "dp"),
        P(("groups", "expert"), None),
        P(("groups", "expert"), None),
        P("expert", "dp", None),
        P("expert", "dp", None),
        P("expert", None, "dp"),
    )
    out_specs = P(("groups", "expert"), "dp")
    return jax.shard_map(
        on_device, mesh=mesh, in_specs=in_specs, out_specs=out_specs, check_vma=False
    )
```

```python
import functools

import jax
import jax.numpy as jnp
from jax import lax
from jax.experimental import pallas as pl
from jax.experimental.pallas import tpu as pltpu
from jax.sharding import PartitionSpec as P

LANES = 128
VMEM = pl.BlockSpec(memory_space=pltpu.VMEM)
SMEM = pl.BlockSpec(memory_space=pltpu.SMEM)
HERE = pl.BlockSpec(memory_space=pl.ANY)
FAR = pl.BlockSpec(memory_space=pltpu.HBM)
NOWHERE = -1e6


def bits_of(n):
    return [b for b in range(n.bit_length() - 1)]


def flip(x, axis, k):
    return lax.ppermute(x, axis, [(i, i ^ k) for i in range(lax.axis_size(axis))])


def route_body(n, experts, info, *refs):
    meta, (rank, wt) = refs[:n], refs[n:]
    tok, top = meta[0].shape[1], meta[0].shape[0] // 2
    padded = rank.shape[0]
    first = info[0].astype(jnp.float32)
    e = lax.broadcasted_iota(jnp.int32, (padded, tok), 0).astype(jnp.float32)
    before = (
        lax.broadcasted_iota(jnp.int32, (tok, tok), 0) < lax.broadcasted_iota(jnp.int32, (tok, tok), 1)
    ).astype(jnp.bfloat16)
    count = jnp.zeros((padded, 1), jnp.float32)
    for s in range(n):
        ids, scores = meta[s][:top], meta[s][top:]
        affinity = 1.0 / (1.0 + jnp.exp(-scores))
        share = 2.5 * affinity / jnp.sum(affinity, axis=0, keepdims=True)
        named = jnp.zeros((padded, tok), jnp.float32)
        weight = jnp.zeros((padded, tok), jnp.float32)
        for k in range(top):
            hit = jnp.where(ids[k : k + 1] - first == e, 1.0, 0.0)
            named = named + hit
            weight = weight + hit * share[k : k + 1]
        named = jnp.where(e < experts, named, 0.0)
        place = jnp.dot(named.astype(jnp.bfloat16), before, preferred_element_type=jnp.float32) + count
        rank[:, s * tok : (s + 1) * tok] = jnp.where(named > 0, place, NOWHERE)
        wt[:, s * tok : (s + 1) * tok] = weight
        count = count + jnp.sum(named, axis=1, keepdims=True)


def route(meta, info, experts):
    tokens = len(meta) * meta[0].shape[1]
    table = jax.ShapeDtypeStruct((-(-experts // 8) * 8, tokens), jnp.float32)
    return pl.pallas_call(
        functools.partial(route_body, len(meta), experts),
        out_shape=(table, table),
        in_specs=[SMEM] + [VMEM] * len(meta),
        out_specs=(VMEM, VMEM),
        compiler_params=pltpu.CompilerParams(vmem_limit_bytes=40 << 20),
        name="route",
    )(info, *meta)


def gate_up_body(n, experts, n_dp, after, info, *refs):
    tokens, (rank_in, w_gate, w_up), refs = refs[:n], refs[n : n + 3], refs[n + 3 + after :]
    send, keep, rank, feed, rows, held, rank_sem, feed_sem, held_sem = refs
    most = rows.shape[0] // len(experts)
    width = send.shape[2] // 2
    pieces = list(range(1, n_dp, 2)) + list(range(0, n_dp, 2))
    mats = [(m, x) for m in range(2) for x in range(len(experts))]

    def copy(l, m, x):
        units = pl.ds(pl.multiple_of((l ^ info[1]) * width, width), width)
        i = m * len(experts) + x
        return pltpu.make_async_copy(
            (w_gate, w_up)[m].at[experts[x], :, units],
            held.at[i, :, pl.ds(l * width, width)],
            held_sem.at[l, i],
        )

    ranks = pltpu.make_async_copy(rank_in, rank, rank_sem.at[0])
    ranks.start()
    at, feeds = 0, []
    for s in range(n):
        tok = tokens[s].shape[0]
        feeds.append(pltpu.make_async_copy(tokens[s], feed.at[pl.ds(at, tok)], feed_sem.at[s]))
        at += tok
    for part in feeds:
        part.start()
    for m, x in mats:
        copy(pieces[0], m, x).start()
    ranks.wait()
    r = lax.broadcasted_iota(jnp.int32, (most, at), 0).astype(jnp.float32)
    pick = jnp.concatenate(
        [jnp.where(r == rank[e : e + 1, :], 1.0, 0.0).astype(jnp.bfloat16) for e in experts], axis=0
    )
    for part in feeds:
        part.wait()
    rows[...] = jnp.dot(pick, feed[...], preferred_element_type=jnp.float32).astype(jnp.bfloat16)
    for l, ahead in zip(pieces, pieces[1:] + [None]):
        if ahead is not None:
            for m, x in mats:
                copy(ahead, m, x).start()
        to = send if l % 2 else keep
        for m, x in mats:
            copy(l, m, x).wait()
            mine = slice(x * most, (x + 1) * most)
            to[l // 2, mine, m * width : (m + 1) * width] = jnp.dot(
                rows[mine],
                held[m * len(experts) + x, :, l * width : (l + 1) * width],
                preferred_element_type=jnp.float32,
            ).astype(jnp.bfloat16)


def gate_up(tokens, rank, info, w_gate, w_up, experts, most, n_dp, after):
    n, local = len(tokens), tokens[0].shape[1]
    hidden = w_gate.shape[2]
    rows, mats = most * len(experts), 2 * len(experts)
    out = jax.ShapeDtypeStruct((max(n_dp // 2, 1), rows, 2 * hidden // n_dp), jnp.bfloat16)
    return pl.pallas_call(
        functools.partial(gate_up_body, n, experts, n_dp, len(after)),
        out_shape=(out, out),
        in_specs=[SMEM] + [HERE] * (n + 3 + len(after)),
        out_specs=(VMEM, VMEM),
        scratch_shapes=[
            pltpu.VMEM(rank.shape, jnp.float32),
            pltpu.VMEM((rank.shape[1], local), jnp.bfloat16),
            pltpu.VMEM((rows, local), jnp.bfloat16),
            pltpu.VMEM((mats, local, hidden), jnp.bfloat16),
            pltpu.SemaphoreType.DMA((1,)),
            pltpu.SemaphoreType.DMA((n,)),
            pltpu.SemaphoreType.DMA((n_dp, mats)),
        ],
        compiler_params=pltpu.CompilerParams(vmem_limit_bytes=40 << 20),
        cost_estimate=pl.CostEstimate(
            flops=8 * mats * most * local * hidden,
            bytes_accessed=2 * mats * local * hidden,
            transcendentals=0,
        ),
        name="gate_up",
    )(info, *tokens, rank, w_gate, w_up, *after)


def down_body(n_part, cuts, experts, first, after, info, *refs):
    parts, (rank, wt, w_down), refs = refs[:n_part], refs[n_part : n_part + 3], refs[n_part + 3 :]
    before = None if first else refs[0]
    refs = refs[(0 if first else 1) + after :]
    outs, (hidden, mix, out, held, held_sem) = refs[: len(cuts)], refs[len(cuts) :]
    most = hidden.shape[0] // len(experts)
    width = parts[0].shape[-1]
    local = out.shape[1]
    block = 512 if local % 512 == 0 else 256 if local % 256 == 0 else local
    copies = {}
    for i in range(local // block):
        for x, e in enumerate(experts):
            cols = pl.ds(i * block, block)
            copies[i, x] = pltpu.make_async_copy(
                w_down.at[e, :, cols], held.at[x, :, cols], held_sem.at[i, x]
            )
            copies[i, x].start()
    for p, part in enumerate(parts):
        for j in range(part.shape[0]):
            at = pl.multiple_of(((2 * j + p) ^ info[1]) * width, width)
            hidden[:, pl.ds(at, width)] = part[j]
    r = lax.broadcasted_iota(jnp.int32, (most, mix.shape[1]), 0).astype(jnp.float32)
    for x, e in enumerate(experts):
        mix[x * most : (x + 1) * most, :] = jnp.where(
            r == rank[e : e + 1, :], wt[e : e + 1, :], 0.0
        ).astype(jnp.bfloat16)
    for i in range(local // block):
        cols = slice(i * block, (i + 1) * block)
        for x in range(len(experts)):
            mine = slice(x * most, (x + 1) * most)
            copies[i, x].wait()
            out[mine, cols] = jnp.dot(
                hidden[mine], held[x, :, cols], preferred_element_type=jnp.float32
            ).astype(jnp.bfloat16)
        total = lax.dot_general(
            mix[...], out[:, cols], (((0,), (0,)), ((), ())), preferred_element_type=jnp.float32
        )
        if not first:
            total = total + before[:, cols]
        at = 0
        for to, cut in zip(outs, cuts):
            to[:, cols] = total[at : at + cut].astype(to.dtype)
            at += cut


def down(parts, rank, wt, info, w_down, total, experts, cuts, after):
    rows = parts[0].shape[1]
    _, hidden, local = w_down.shape
    tokens = rank.shape[1]
    first, last = total is None, len(cuts) > 1
    kind = jnp.bfloat16 if last else jnp.float32
    mats = len(experts)
    outs = pl.pallas_call(
        functools.partial(down_body, len(parts), cuts, experts, first, len(after)),
        out_shape=tuple(jax.ShapeDtypeStruct((cut, local), kind) for cut in cuts),
        in_specs=[SMEM]
        + [VMEM] * (len(parts) + 2)
        + [HERE]
        + ([] if first else [VMEM])
        + [HERE] * len(after),
        out_specs=(VMEM,) * len(cuts),
        scratch_shapes=[
            pltpu.VMEM((rows, hidden), jnp.bfloat16),
            pltpu.VMEM((rows, tokens), jnp.bfloat16),
            pltpu.VMEM((rows, local), jnp.bfloat16),
            pltpu.VMEM((mats, hidden, local), jnp.bfloat16),
            pltpu.SemaphoreType.DMA((local // 256 + 1, mats)),
        ],
        compiler_params=pltpu.CompilerParams(vmem_limit_bytes=40 << 20),
        cost_estimate=pl.CostEstimate(
            flops=8 * local * rows * (hidden + tokens),
            bytes_accessed=2 * mats * hidden * local + 8 * tokens * local,
            transcendentals=0,
        ),
        name="down",
    )(info, *parts, rank, wt, w_down, *([] if first else [total]), *after)
    return outs if last else outs[0]


def chip_sums(send, keep, n_dp):
    total = keep.astype(jnp.float32)
    late = jnp.zeros(total.shape, jnp.float32)
    for b in bits_of(n_dp):
        if b > 0:
            total = total + late
            send = total.astype(jnp.bfloat16)
        late = flip(send, "dp", 1 << b).astype(jnp.float32)
        if b > 0:
            pairs = (late.shape[0] >> b, 2, 1 << (b - 1)) + late.shape[1:]
            late = jnp.flip(late.reshape(pairs), axis=1).reshape(late.shape)
    return total, late, send


def finish(total, late, after):
    if after:
        late, *_ = lax.optimization_barrier((late, *after))
    gate_up = total + late
    width = gate_up.shape[2] // 2
    return (jax.nn.silu(gate_up[:, :, :width]) * gate_up[:, :, width:]).astype(jnp.bfloat16)


def all_parts(mine, n_dp):
    return [mine, flip(mine, "dp", 1)] if n_dp > 1 else [mine]


def on_device(tokens, expert_ids, scores, w_gate, w_up, w_down):
    n_owner, n_dp = lax.axis_size("expert"), lax.axis_size("dp")
    tok_rows, top = expert_ids.shape
    experts = w_gate.shape[0]
    capacity = 2 * tok_rows * top // (experts * n_owner)
    per_chunk = 2 if experts % 2 == 0 else 1
    most = n_owner * capacity
    chunks = experts // per_chunk

    meta = jnp.concatenate([expert_ids.T.astype(jnp.float32), scores.T], axis=0)
    feeds = gathered(tokens, "expert")
    metas = [meta] + [
        lax.ppermute(meta, "expert", [(i, (i - k) % n_owner) for i in range(n_owner)])
        for k in gathered_order(n_owner)[1:]
    ]
    info = jnp.stack([lax.axis_index("expert") * experts, lax.axis_index("dp")]).astype(jnp.int32)
    rank, wt = route(metas, info, experts)

    cuts = [feed.shape[0] for feed in feeds]
    of = lambda c: list(range(c * per_chunk, (c + 1) * per_chunk))
    shares, sent, parts, total = [], [], [], None

    def add(c, after):
        outs = cuts if c == chunks - 1 else [sum(cuts)]
        return down(parts[c], rank, wt, info, w_down, total, of(c), outs, after)

    for c in range(chunks):
        after = ([sent[c - 1]] if c >= 1 else []) + ([shares[c - 2]] if c >= 2 else [])
        send, keep = gate_up(feeds, rank, info, w_gate, w_up, of(c), most, n_dp, after)
        if c > 0:
            send = lax.optimization_barrier((send, shares[-1]))[0]
        mine, late, last_sent = chip_sums(send, keep, n_dp)
        sent.append(last_sent)
        if c > 0:
            parts.append(all_parts(lax.optimization_barrier((shares[-1], last_sent))[0], n_dp))
        early = range(c) if c == chunks - 1 else []
        for d in early:
            total = add(d, [last_sent, shares[-1]] if d == 0 else [])
        shares.append(finish(mine, late, [total] if early else []))
    parts.append(all_parts(shares[-1], n_dp))
    total = add(chunks - 1, [])
    return returned(total, "expert") if n_owner > 1 else total[0].astype(jnp.bfloat16)


def gathered_order(n):
    near = [d for s in range(1, n // 2) for d in (-s, s)]
    return [0] + near + ([n // 2] if n > 1 else [])


def gathered(x, axis):
    n = lax.axis_size(axis)
    up, down_ = [(i, (i + 1) % n) for i in range(n)], [(i, (i - 1) % n) for i in range(n)]
    below = above = x
    found = [x]
    for _ in range(1, n // 2):
        below, above = lax.ppermute(below, axis, up), lax.ppermute(above, axis, down_)
        found += [below, above]
    if n > 1:
        half = x.shape[0] // 2
        found += [lax.ppermute(below[:half], axis, up), lax.ppermute(above[half:], axis, down_)]
    return found


def returned(partials, axis):
    n = lax.axis_size(axis)
    up, down_ = [(i, (i + 1) % n) for i in range(n)], [(i, (i - 1) % n) for i in range(n)]
    wide = lambda x: x.astype(jnp.float32)
    near = {0: partials[0]}
    for k, partial in zip(gathered_order(n)[1:-1], partials[1:-2]):
        near[k] = partial
    half = partials[-1].shape[0]
    low, high = lax.ppermute(partials[-2], axis, down_), lax.ppermute(partials[-1], axis, up)
    halves = True
    for s in range(n // 2 - 1, 0, -1):
        a, b = wide(near[-s]), wide(near[s])
        if halves:
            a = jnp.concatenate([a[:half] + wide(low), a[half:]], axis=0)
            b = jnp.concatenate([b[:half], b[half:] + wide(high)], axis=0)
        else:
            a, b = a + wide(low), b + wide(high)
        low = lax.ppermute(a.astype(jnp.bfloat16), axis, down_)
        high = lax.ppermute(b.astype(jnp.bfloat16), axis, up)
        halves = False
    if halves:
        back = jnp.concatenate([wide(low), wide(high)], axis=0)
    else:
        back = wide(low) + wide(high)
    return (wide(near[0]) + back).astype(jnp.bfloat16)


def solution(mesh):
    in_specs = (
        P(("groups", "expert"), "dp"),
        P(("groups", "expert"), None),
        P(("groups", "expert"), None),
        P("expert", "dp", None),
        P("expert", "dp", None),
        P("expert", None, "dp"),
    )
    out_specs = P(("groups", "expert"), "dp")
    return jax.shard_map(
        on_device, mesh=mesh, in_specs=in_specs, out_specs=out_specs, check_vma=False
    )
```

```python
import functools

import jax
import jax.numpy as jnp
from jax import lax
from jax.experimental import pallas as pl
from jax.experimental.pallas import tpu as pltpu
from jax.sharding import PartitionSpec as P

LANES = 128
VMEM = pl.BlockSpec(memory_space=pltpu.VMEM)
SMEM = pl.BlockSpec(memory_space=pltpu.SMEM)
HERE = pl.BlockSpec(memory_space=pl.ANY)
FAR = pl.BlockSpec(memory_space=pltpu.HBM)
NOWHERE = -1e6


def bits_of(n):
    return [b for b in range(n.bit_length() - 1)]


def flip(x, axis, k):
    return lax.ppermute(x, axis, [(i, i ^ k) for i in range(lax.axis_size(axis))])


def route_body(n, experts, info, *refs):
    meta, (rank, wt) = refs[:n], refs[n:]
    tok, top = meta[0].shape[1], meta[0].shape[0] // 2
    padded = rank.shape[0]
    first = info[0].astype(jnp.float32)
    e = lax.broadcasted_iota(jnp.int32, (padded, tok), 0).astype(jnp.float32)
    before = (
        lax.broadcasted_iota(jnp.int32, (tok, tok), 0) < lax.broadcasted_iota(jnp.int32, (tok, tok), 1)
    ).astype(jnp.bfloat16)
    count = jnp.zeros((padded, 1), jnp.float32)
    for s in range(n):
        ids, scores = meta[s][:top], meta[s][top:]
        affinity = 1.0 / (1.0 + jnp.exp(-scores))
        share = 2.5 * affinity / jnp.sum(affinity, axis=0, keepdims=True)
        named = jnp.zeros((padded, tok), jnp.float32)
        weight = jnp.zeros((padded, tok), jnp.float32)
        for k in range(top):
            hit = jnp.where(ids[k : k + 1] - first == e, 1.0, 0.0)
            named = named + hit
            weight = weight + hit * share[k : k + 1]
        named = jnp.where(e < experts, named, 0.0)
        place = jnp.dot(named.astype(jnp.bfloat16), before, preferred_element_type=jnp.float32) + count
        rank[:, s * tok : (s + 1) * tok] = jnp.where(named > 0, place, NOWHERE)
        wt[:, s * tok : (s + 1) * tok] = weight
        count = count + jnp.sum(named, axis=1, keepdims=True)


def route(meta, info, experts):
    tokens = len(meta) * meta[0].shape[1]
    table = jax.ShapeDtypeStruct((-(-experts // 8) * 8, tokens), jnp.float32)
    return pl.pallas_call(
        functools.partial(route_body, len(meta), experts),
        out_shape=(table, table),
        in_specs=[SMEM] + [VMEM] * len(meta),
        out_specs=(VMEM, VMEM),
        compiler_params=pltpu.CompilerParams(vmem_limit_bytes=40 << 20),
        name="route",
    )(info, *meta)


def fetches(w_gate, w_up, experts, units, to, sem):
    return [
        pltpu.make_async_copy(w.at[e, :, units], to.at[i], sem.at[i])
        for i, (w, e) in enumerate((w, e) for w in (w_gate, w_up) for e in experts)
    ]


def units_of(l, info, width):
    return pl.ds(pl.multiple_of((l ^ info[1]) * width, width), width)


def products(rows, weights, to, j):
    most = rows.shape[0] * 2 // weights.shape[0]
    width = weights.shape[2]
    for i in range(weights.shape[0]):
        m, x = divmod(i, weights.shape[0] // 2)
        mine = slice(x * most, (x + 1) * most)
        to[j, mine, m * width : (m + 1) * width] = jnp.dot(
            rows[mine], weights[i], preferred_element_type=jnp.float32
        ).astype(jnp.bfloat16)


def shares_body(n, experts, shares, ahead, after, info, *refs):
    sources, refs = refs[: n + 1] if n else refs[:1], refs[n + 1 if n else 1 :]
    (given, w_gate, w_up), refs = refs[:3], refs[3 + after :]
    to, refs = refs[0], refs[1:]
    width = given.shape[2]
    rows = sources[0]
    if n:
        rows, refs = refs[0], refs[1:]
    if ahead is not None:
        handed, refs = refs[0], refs[1:]
    held, held_sem, handed_sem, refs = refs[0], refs[1], refs[2], refs[3:]
    rest = [
        fetches(w_gate, w_up, experts, units_of(l, info, width), held.at[j], held_sem.at[j])
        for j, l in enumerate(shares[1:])
    ]
    on = []
    if ahead is not None:
        on = fetches(w_gate, w_up, ahead[0], units_of(ahead[1], info, width), handed, handed_sem)
    if n:
        feed, feed_sem = refs
        at, feeds = 0, []
        for s in range(n):
            tok = sources[s].shape[0]
            feeds.append(pltpu.make_async_copy(sources[s], feed.at[pl.ds(at, tok)], feed_sem.at[s]))
            at += tok
        for copy in feeds:
            copy.start()
    for copies in rest + [on]:
        for copy in copies:
            copy.start()
    if n:
        rank = sources[n]
        most = rows.shape[0] // len(experts)
        r = lax.broadcasted_iota(jnp.int32, (most, at), 0).astype(jnp.float32)
        pick = jnp.concatenate(
            [jnp.where(r == rank[e : e + 1, :], 1.0, 0.0).astype(jnp.bfloat16) for e in experts], axis=0
        )
        for copy in feeds:
            copy.wait()
        rows[...] = jnp.dot(pick, feed[...], preferred_element_type=jnp.float32).astype(jnp.bfloat16)
    products(rows, given, to, 0)
    for j, copies in enumerate(rest):
        for copy in copies:
            copy.wait()
        products(rows, held.at[j], to, j + 1)
    for copy in on:
        copy.wait()


def some_shares(sources, info, given, w_gate, w_up, experts, most, shares, ahead, after):
    n = len(sources) - 1
    mats, local, width = given.shape
    rows = most * len(experts)
    pieces = max(len(shares) - 1, 1)
    out = [jax.ShapeDtypeStruct((len(shares), rows, 2 * width), jnp.bfloat16)]
    if n:
        out.append(jax.ShapeDtypeStruct((rows, local), jnp.bfloat16))
    if ahead is not None:
        out.append(jax.ShapeDtypeStruct(given.shape, jnp.bfloat16))
    scratch = [
        pltpu.VMEM((pieces, mats, local, width), jnp.bfloat16),
        pltpu.SemaphoreType.DMA((pieces, mats)),
        pltpu.SemaphoreType.DMA((mats,)),
    ]
    if n:
        scratch += [
            pltpu.VMEM((sources[-1].shape[1], local), jnp.bfloat16),
            pltpu.SemaphoreType.DMA((n,)),
        ]
    return pl.pallas_call(
        functools.partial(shares_body, n, experts, shares, ahead, len(after)),
        out_shape=tuple(out),
        in_specs=[SMEM] + [HERE] * n + [VMEM] * 2 + [HERE] * (2 + len(after)),
        out_specs=(VMEM,) * len(out),
        scratch_shapes=scratch,
        compiler_params=pltpu.CompilerParams(vmem_limit_bytes=40 << 20),
        cost_estimate=pl.CostEstimate(flops=1, bytes_accessed=1, transcendentals=0),
        name="send_shares" if n else "keep_shares",
    )(info, *sources, given, w_gate, w_up, *after)


def stage_body(experts, share, info, tokens, w_gate, w_up, copied, handed, sem, handed_sem):
    width = handed.shape[2]
    own = pltpu.make_async_copy(tokens, copied, sem.at[0])
    own.start()
    copies = fetches(w_gate, w_up, experts, units_of(share, info, width), handed, handed_sem)
    for copy in copies:
        copy.start()
    own.wait()
    for copy in copies:
        copy.wait()


def stage(tokens, info, w_gate, w_up, experts, share, n_dp):
    _, local, hidden = w_gate.shape
    mats = 2 * len(experts)
    return pl.pallas_call(
        functools.partial(stage_body, experts, share),
        out_shape=(
            jax.ShapeDtypeStruct(tokens.shape, tokens.dtype),
            jax.ShapeDtypeStruct((mats, local, hidden // n_dp), jnp.bfloat16),
        ),
        in_specs=[SMEM] + [HERE] * 3,
        out_specs=(VMEM, VMEM),
        scratch_shapes=[pltpu.SemaphoreType.DMA((1,)), pltpu.SemaphoreType.DMA((mats,))],
        compiler_params=pltpu.CompilerParams(vmem_limit_bytes=40 << 20),
        cost_estimate=pl.CostEstimate(flops=1, bytes_accessed=1, transcendentals=0),
        name="stage",
    )(info, tokens, w_gate, w_up)


def down_body(lanes, cuts, experts, first, after, info, *refs):
    n_part = len(lanes)
    parts, (rank, wt, w_down), refs = refs[:n_part], refs[n_part : n_part + 3], refs[n_part + 3 :]
    before = None if first else refs[0]
    refs = refs[(0 if first else 1) + after :]
    outs, (hidden, mix, out, held, held_sem) = refs[: len(cuts)], refs[len(cuts) :]
    most = hidden.shape[0] // len(experts)
    width = parts[0].shape[-1]
    local = out.shape[1]
    block = 512 if local % 512 == 0 else 256 if local % 256 == 0 else local
    copies = {}
    for i in range(local // block):
        for x, e in enumerate(experts):
            cols = pl.ds(i * block, block)
            copies[i, x] = pltpu.make_async_copy(
                w_down.at[e, :, cols], held.at[x, :, cols], held_sem.at[i, x]
            )
            copies[i, x].start()
    for part, (at, shares) in zip(parts, lanes):
        for j, l in enumerate(shares):
            hidden[:, units_of(l, info, width)] = part[j, :, at : at + width]
    r = lax.broadcasted_iota(jnp.int32, (most, mix.shape[1]), 0).astype(jnp.float32)
    for x, e in enumerate(experts):
        mix[x * most : (x + 1) * most, :] = jnp.where(
            r == rank[e : e + 1, :], wt[e : e + 1, :], 0.0
        ).astype(jnp.bfloat16)
    for i in range(local // block):
        cols = slice(i * block, (i + 1) * block)
        for x in range(len(experts)):
            mine = slice(x * most, (x + 1) * most)
            copies[i, x].wait()
            out[mine, cols] = jnp.dot(
                hidden[mine], held[x, :, cols], preferred_element_type=jnp.float32
            ).astype(jnp.bfloat16)
        total = lax.dot_general(
            mix[...], out[:, cols], (((0,), (0,)), ((), ())), preferred_element_type=jnp.float32
        )
        if not first:
            total = total + before[:, cols]
        at = 0
        for to, cut in zip(outs, cuts):
            to[:, cols] = total[at : at + cut].astype(to.dtype)
            at += cut


def down(parts, rank, wt, info, w_down, total, experts, cuts, after):
    parts, lanes = [part for part, *_ in parts], [tuple(where) for _, *where in parts]
    rows = parts[0].shape[1]
    _, hidden, local = w_down.shape
    tokens = rank.shape[1]
    first, last = total is None, len(cuts) > 1
    kind = jnp.bfloat16 if last else jnp.float32
    mats = len(experts)
    outs = pl.pallas_call(
        functools.partial(down_body, lanes, cuts, experts, first, len(after)),
        out_shape=tuple(jax.ShapeDtypeStruct((cut, local), kind) for cut in cuts),
        in_specs=[SMEM]
        + [VMEM] * (len(parts) + 2)
        + [HERE]
        + ([] if first else [VMEM])
        + [HERE] * len(after),
        out_specs=(VMEM,) * len(cuts),
        scratch_shapes=[
            pltpu.VMEM((rows, hidden), jnp.bfloat16),
            pltpu.VMEM((rows, tokens), jnp.bfloat16),
            pltpu.VMEM((rows, local), jnp.bfloat16),
            pltpu.VMEM((mats, hidden, local), jnp.bfloat16),
            pltpu.SemaphoreType.DMA((local // 256 + 1, mats)),
        ],
        compiler_params=pltpu.CompilerParams(vmem_limit_bytes=40 << 20),
        cost_estimate=pl.CostEstimate(
            flops=8 * local * rows * (hidden + tokens),
            bytes_accessed=2 * mats * hidden * local + 8 * tokens * local,
            transcendentals=0,
        ),
        name="down",
    )(info, *parts, rank, wt, w_down, *([] if first else [total]), *after)
    return outs if last else outs[0]


def finish(total, late, after):
    if after:
        late, *_ = lax.optimization_barrier((late, *after))
    gate_up = total + late.astype(jnp.float32)
    width = gate_up.shape[2] // 2
    return (jax.nn.silu(gate_up[:, :, :width]) * gate_up[:, :, width:]).astype(jnp.bfloat16)


def chip_sums(send, keep, bits):
    total = keep.astype(jnp.float32) + flip(send, "dp", 1).astype(jnp.float32)
    for b in bits[1:-1]:
        total = total[0::2] + flip(total[1::2].astype(jnp.bfloat16), "dp", 1 << b).astype(jnp.float32)
    return total[0::2], total[1::2].astype(jnp.bfloat16)


def everyone_s(share, other, at, bits):
    width = share.shape[2]
    top = 1 << bits[-1]
    parts = [(share, 0, [0]), (other, at, [top])]
    held, whose = jnp.concatenate([share, other[:, :, at : at + width]], axis=0), [0, top]
    for b in reversed(bits[:-1]):
        theirs = flip(held, "dp", 1 << b)
        parts.append((theirs, 0, [l | 1 << b for l in whose]))
        if b > 0:
            held, whose = jnp.concatenate([held, theirs], axis=0), whose + parts[-1][2]
    return parts


def on_device(tokens, expert_ids, scores, w_gate, w_up, w_down):
    n_owner, n_dp = lax.axis_size("expert"), lax.axis_size("dp")
    tok_rows, top = expert_ids.shape
    experts = w_gate.shape[0]
    capacity = 2 * tok_rows * top // (experts * n_owner)
    per_chunk = 2 if experts % 2 == 0 else 1
    most = n_owner * capacity
    chunks = experts // per_chunk

    meta = jnp.concatenate([expert_ids.T.astype(jnp.float32), scores.T], axis=0)
    feeds = gathered(tokens, "expert")
    metas = [meta] + [
        lax.ppermute(meta, "expert", [(i, (i - k) % n_owner) for i in range(n_owner)])
        for k in gathered_order(n_owner)[1:]
    ]
    info = jnp.stack([lax.axis_index("expert") * experts, lax.axis_index("dp")]).astype(jnp.int32)
    rank, wt = route(metas, info, experts)

    cuts = [feed.shape[0] for feed in feeds]
    of = lambda c: list(range(c * per_chunk, (c + 1) * per_chunk))
    bits = bits_of(n_dp)
    cross = 1 << bits[-1]
    odd, even = list(range(1, n_dp, 2)), list(range(0, n_dp, 2))
    feeds[0], given = stage(tokens, info, w_gate, w_up, of(0), odd[0], n_dp)
    sent, parts, total = [], [], None
    share = kept = late = None

    def add(c, after):
        outs = cuts if c == chunks - 1 else [sum(cuts)]
        return down(parts[c], rank, wt, info, w_down, total, of(c), outs, after)

    for c in range(chunks):
        last = c == chunks - 1
        send, rows, given = some_shares(
            [*feeds, rank], info, given, w_gate, w_up, of(c), most, odd, (of(c), 0), sent[-1:]
        )
        keep, *given = some_shares(
            [rows], info, given, w_gate, w_up, of(c), most, even, None if last else (of(c + 1), odd[0]), []
        )
        given = given[0] if given else None
        before, behind = kept, late
        kept, out = chip_sums(send, keep, bits)
        width = out.shape[2]
        if c > 0:
            share = finish(before, behind[:, :, :width], [])
            out = jnp.concatenate([out, share], axis=2)
        sent.append(out)
        late = flip(out, "dp", cross)
        if c > 0:
            parts.append(everyone_s(share, late, width, bits))
        if last:
            for d in range(min(c - 1, 2)):
                total = add(d, [out] if d == 0 else [])
    share = finish(kept, late[:, :, :width], [] if total is None else [total])
    other = flip(share, "dp", cross)
    for c in range(max(min(chunks - 2, 2), 0), chunks - 1):
        total = add(c, [share])
    if total is not None:
        other = lax.optimization_barrier((other, total))[0]
    parts.append(everyone_s(share, other, 0, bits))
    total = add(chunks - 1, [])
    return returned(total, "expert") if n_owner > 1 else total[0].astype(jnp.bfloat16)


def gathered_order(n):
    near = [d for s in range(1, n // 2) for d in (-s, s)]
    return [0] + near + ([n // 2] if n > 1 else [])


def gathered(x, axis):
    n = lax.axis_size(axis)
    up, down_ = [(i, (i + 1) % n) for i in range(n)], [(i, (i - 1) % n) for i in range(n)]
    below = above = x
    found = [x]
    for _ in range(1, n // 2):
        below, above = lax.ppermute(below, axis, up), lax.ppermute(above, axis, down_)
        found += [below, above]
    if n > 1:
        half = x.shape[0] // 2
        found += [lax.ppermute(below[:half], axis, up), lax.ppermute(above[half:], axis, down_)]
    return found


def returned(partials, axis):
    n = lax.axis_size(axis)
    up, down_ = [(i, (i + 1) % n) for i in range(n)], [(i, (i - 1) % n) for i in range(n)]
    wide = lambda x: x.astype(jnp.float32)
    near = {0: partials[0]}
    for k, partial in zip(gathered_order(n)[1:-1], partials[1:-2]):
        near[k] = partial
    half = partials[-1].shape[0]
    low, high = lax.ppermute(partials[-2], axis, down_), lax.ppermute(partials[-1], axis, up)
    halves = True
    for s in range(n // 2 - 1, 0, -1):
        a, b = wide(near[-s]), wide(near[s])
        if halves:
            a = jnp.concatenate([a[:half] + wide(low), a[half:]], axis=0)
            b = jnp.concatenate([b[:half], b[half:] + wide(high)], axis=0)
        else:
            a, b = a + wide(low), b + wide(high)
        low = lax.ppermute(a.astype(jnp.bfloat16), axis, down_)
        high = lax.ppermute(b.astype(jnp.bfloat16), axis, up)
        halves = False
    if halves:
        back = jnp.concatenate([wide(low), wide(high)], axis=0)
    else:
        back = wide(low) + wide(high)
    return (wide(near[0]) + back).astype(jnp.bfloat16)


def solution(mesh):
    in_specs = (
        P(("groups", "expert"), "dp"),
        P(("groups", "expert"), None),
        P(("groups", "expert"), None),
        P("expert", "dp", None),
        P("expert", "dp", None),
        P("expert", None, "dp"),
    )
    out_specs = P(("groups", "expert"), "dp")
    return jax.shard_map(
        on_device, mesh=mesh, in_specs=in_specs, out_specs=out_specs, check_vma=False
    )
```

```python
import functools

import jax
import jax.numpy as jnp
from jax import lax
from jax.experimental import pallas as pl
from jax.experimental.pallas import tpu as pltpu
from jax.sharding import PartitionSpec as P

LANES = 128
VMEM = pl.BlockSpec(memory_space=pltpu.VMEM)
SMEM = pl.BlockSpec(memory_space=pltpu.SMEM)
HERE = pl.BlockSpec(memory_space=pl.ANY)
FAR = pl.BlockSpec(memory_space=pltpu.HBM)
NOWHERE = -1e6


def bits_of(n):
    return [b for b in range(n.bit_length() - 1)]


def flip(x, axis, k):
    return lax.ppermute(x, axis, [(i, i ^ k) for i in range(lax.axis_size(axis))])


def route_body(n, experts, info, *refs):
    meta, (rank, wt) = refs[:n], refs[n:]
    tok, top = meta[0].shape[1], meta[0].shape[0] // 2
    padded = rank.shape[0]
    first = info[0].astype(jnp.float32)
    e = lax.broadcasted_iota(jnp.int32, (padded, tok), 0).astype(jnp.float32)
    before = (
        lax.broadcasted_iota(jnp.int32, (tok, tok), 0) < lax.broadcasted_iota(jnp.int32, (tok, tok), 1)
    ).astype(jnp.bfloat16)
    count = jnp.zeros((padded, 1), jnp.float32)
    for s in range(n):
        ids, scores = meta[s][:top], meta[s][top:]
        affinity = 1.0 / (1.0 + jnp.exp(-scores))
        share = 2.5 * affinity / jnp.sum(affinity, axis=0, keepdims=True)
        named = jnp.zeros((padded, tok), jnp.float32)
        weight = jnp.zeros((padded, tok), jnp.float32)
        for k in range(top):
            hit = jnp.where(ids[k : k + 1] - first == e, 1.0, 0.0)
            named = named + hit
            weight = weight + hit * share[k : k + 1]
        named = jnp.where(e < experts, named, 0.0)
        place = jnp.dot(named.astype(jnp.bfloat16), before, preferred_element_type=jnp.float32) + count
        rank[:, s * tok : (s + 1) * tok] = jnp.where(named > 0, place, NOWHERE)
        wt[:, s * tok : (s + 1) * tok] = weight
        count = count + jnp.sum(named, axis=1, keepdims=True)


def route(meta, info, experts):
    tokens = len(meta) * meta[0].shape[1]
    table = jax.ShapeDtypeStruct((-(-experts // 8) * 8, tokens), jnp.float32)
    return pl.pallas_call(
        functools.partial(route_body, len(meta), experts),
        out_shape=(table, table),
        in_specs=[SMEM] + [VMEM] * len(meta),
        out_specs=(VMEM, VMEM),
        compiler_params=pltpu.CompilerParams(vmem_limit_bytes=40 << 20),
        name="route",
    )(info, *meta)


def backwards(l, n):
    bits = bits_of(n)
    return sum((((l >> b) & 1) << (len(bits) - 1 - b) for b in bits), 0 * l)


def units_of(l, info, n, width):
    return pl.ds(pl.multiple_of((backwards(l, n) ^ info[2]) * width, width), width)


def fetches(w, experts, side, info, to, sem):
    half = to.shape[2]
    units = pl.ds(pl.multiple_of(((info[1] & 1) ^ side) * half, half), half)
    return [pltpu.make_async_copy(w.at[e, :, units], to.at[x], sem.at[x]) for x, e in enumerate(experts)]


def products(rows, weights, to, m, info):
    most = rows.shape[0] // weights.shape[0]
    shares, width = to.shape[0], to.shape[2] // 2
    for x in range(weights.shape[0]):
        mine = slice(x * most, (x + 1) * most)
        part = jnp.dot(rows[mine], weights[x], preferred_element_type=jnp.float32).astype(jnp.bfloat16)
        for q in range(shares):
            j = backwards(q, shares) ^ (info[1] >> 1)
            to[j, mine, m * width : (m + 1) * width] = part[:, q * width : (q + 1) * width]


def half_body(n, experts, side, ahead, after, info, *refs):
    sources, refs = refs[: max(n + 1, 1)], refs[max(n + 1, 1) :]
    (given, w_gate, w_up), refs = refs[:3], refs[3 + after :]
    to, refs = refs[0], refs[1:]
    rows = sources[0]
    if n:
        rows, refs = refs[0], refs[1:]
    if ahead is not None:
        handed, refs = refs[0], refs[1:]
    (held, held_sem, handed_sem), refs = refs[:3], refs[3:]
    if n:
        feed, feed_sem = refs
        at, feeds = 0, []
        for s in range(n):
            tok = sources[s].shape[0]
            feeds.append(pltpu.make_async_copy(sources[s], feed.at[pl.ds(at, tok)], feed_sem.at[s]))
            at += tok
        for copy in feeds:
            copy.start()
    rest = fetches(w_up, experts, side, info, held, held_sem)
    on = []
    if ahead is not None:
        on = fetches(w_gate, ahead[0], ahead[1], info, handed, handed_sem)
    for copy in rest + on:
        copy.start()
    if n:
        rank = sources[n]
        most = rows.shape[0] // len(experts)
        r = lax.broadcasted_iota(jnp.int32, (most, at), 0).astype(jnp.float32)
        pick = jnp.concatenate(
            [jnp.where(r == rank[e : e + 1, :], 1.0, 0.0).astype(jnp.bfloat16) for e in experts], axis=0
        )
        for copy in feeds:
            copy.wait()
        rows[...] = jnp.dot(pick, feed[...], preferred_element_type=jnp.float32).astype(jnp.bfloat16)
    products(rows, given, to, 0, info)
    for copy in rest:
        copy.wait()
    products(rows, held, to, 1, info)
    for copy in on:
        copy.wait()


def half_units(sources, info, given, w_gate, w_up, experts, most, n_dp, side, ahead, after):
    n = len(sources) - 1
    _, local, half = given.shape
    rows = most * len(experts)
    out = [jax.ShapeDtypeStruct((n_dp // 2, rows, 4 * half // n_dp), jnp.bfloat16)]
    if n:
        out.append(jax.ShapeDtypeStruct((rows, local), jnp.bfloat16))
    if ahead is not None:
        out.append(jax.ShapeDtypeStruct(given.shape, jnp.bfloat16))
    scratch = [
        pltpu.VMEM(given.shape, jnp.bfloat16),
        pltpu.SemaphoreType.DMA((len(experts),)),
        pltpu.SemaphoreType.DMA((len(experts),)),
    ]
    if n:
        scratch += [
            pltpu.VMEM((sources[-1].shape[1], local), jnp.bfloat16),
            pltpu.SemaphoreType.DMA((n,)),
        ]
    return pl.pallas_call(
        functools.partial(half_body, n, experts, side, ahead, len(after)),
        out_shape=tuple(out),
        in_specs=[SMEM] + [HERE] * n + [VMEM] * 2 + [HERE] * (2 + len(after)),
        out_specs=(VMEM,) * len(out),
        scratch_shapes=scratch,
        compiler_params=pltpu.CompilerParams(vmem_limit_bytes=40 << 20),
        cost_estimate=pl.CostEstimate(flops=1, bytes_accessed=1, transcendentals=0),
        name="send_half" if n else "keep_half",
    )(info, *sources, given, w_gate, w_up, *after)


def stage_body(experts, side, info, w_gate, handed, sem):
    copies = fetches(w_gate, experts, side, info, handed, sem)
    for copy in copies:
        copy.start()
    for copy in copies:
        copy.wait()


def stage(info, w_gate, experts, side):
    _, local, hidden = w_gate.shape
    return pl.pallas_call(
        functools.partial(stage_body, experts, side),
        out_shape=jax.ShapeDtypeStruct((len(experts), local, hidden // 2), jnp.bfloat16),
        in_specs=[SMEM, HERE],
        out_specs=VMEM,
        scratch_shapes=[pltpu.SemaphoreType.DMA((len(experts),))],
        compiler_params=pltpu.CompilerParams(vmem_limit_bytes=40 << 20),
        cost_estimate=pl.CostEstimate(flops=1, bytes_accessed=1, transcendentals=0),
        name="stage",
    )(info, w_gate)


def block_of(local):
    return 512 if local % 512 == 0 else 256 if local % 256 == 0 else local


def down_body(lanes, cuts, experts, first, after, info, *refs):
    n_part = len(lanes)
    parts, (rank, wt, w_down), refs = refs[:n_part], refs[n_part : n_part + 3], refs[n_part + 3 :]
    before = None if first else refs[0]
    refs = refs[(0 if first else 1) + after :]
    outs, (hidden, mix, out, held, held_sem) = refs[: len(cuts)], refs[len(cuts) :]
    most = hidden.shape[0] // len(experts)
    width = parts[0].shape[-1]
    n_dp = hidden.shape[1] // width
    local = out.shape[1]
    block = block_of(local)
    copies = {}
    for i in range(local // block):
        for x, e in enumerate(experts):
            cols = pl.ds(i * block, block)
            copies[i, x] = pltpu.make_async_copy(
                w_down.at[e, :, cols], held.at[x, :, cols], held_sem.at[i, x]
            )
            copies[i, x].start()
    for part, (at, shares) in zip(parts, lanes):
        for j, l in enumerate(shares):
            hidden[:, units_of(l, info, n_dp, width)] = part[j, :, at : at + width]
    r = lax.broadcasted_iota(jnp.int32, (most, mix.shape[1]), 0).astype(jnp.float32)
    for x, e in enumerate(experts):
        mix[x * most : (x + 1) * most, :] = jnp.where(
            r == rank[e : e + 1, :], wt[e : e + 1, :], 0.0
        ).astype(jnp.bfloat16)
    for i in range(local // block):
        cols = slice(i * block, (i + 1) * block)
        for x in range(len(experts)):
            mine = slice(x * most, (x + 1) * most)
            copies[i, x].wait()
            out[mine, cols] = jnp.dot(
                hidden[mine], held[x, :, cols], preferred_element_type=jnp.float32
            ).astype(jnp.bfloat16)
        total = lax.dot_general(
            mix[...], out[:, cols], (((0,), (0,)), ((), ())), preferred_element_type=jnp.float32
        )
        if not first:
            total = total + before[:, cols]
        at, left = 0, i * block
        for k, (cut, wide) in enumerate(cuts):
            if 0 <= left < wide:
                outs[k][:, left : left + block] = total[at : at + cut].astype(outs[k].dtype)
            at += cut
            if at == total.shape[0]:
                at, left = 0, left - wide


def down(parts, rank, wt, info, w_down, total, experts, cuts, after):
    parts, lanes = [part for part, *_ in parts], [tuple(where) for _, *where in parts]
    rows = parts[0].shape[1]
    _, hidden, local = w_down.shape
    tokens = rank.shape[1]
    first, last = total is None, len(cuts) > 1
    kind = jnp.bfloat16 if last else jnp.float32
    mats = len(experts)
    outs = pl.pallas_call(
        functools.partial(down_body, lanes, cuts, experts, first, len(after)),
        out_shape=tuple(jax.ShapeDtypeStruct(cut, kind) for cut in cuts),
        in_specs=[SMEM]
        + [VMEM] * (len(parts) + 2)
        + [HERE]
        + ([] if first else [VMEM])
        + [HERE] * len(after),
        out_specs=(VMEM,) * len(cuts),
        scratch_shapes=[
            pltpu.VMEM((rows, hidden), jnp.bfloat16),
            pltpu.VMEM((rows, tokens), jnp.bfloat16),
            pltpu.VMEM((rows, local), jnp.bfloat16),
            pltpu.VMEM((mats, hidden, local), jnp.bfloat16),
            pltpu.SemaphoreType.DMA((local // 256 + 1, mats)),
        ],
        compiler_params=pltpu.CompilerParams(vmem_limit_bytes=40 << 20),
        cost_estimate=pl.CostEstimate(
            flops=8 * local * rows * (hidden + tokens),
            bytes_accessed=2 * mats * hidden * local + 8 * tokens * local,
            transcendentals=0,
        ),
        name="down",
    )(info, *parts, rank, wt, w_down, *([] if first else [total]), *after)
    return outs if last else outs[0]


def finish(total, late, after):
    if after:
        late, *_ = lax.optimization_barrier((late, *after))
    gate_up = total + late.astype(jnp.float32)
    width = gate_up.shape[2] // 2
    return (jax.nn.silu(gate_up[:, :, :width]) * gate_up[:, :, width:]).astype(jnp.bfloat16)


def chip_sums(send, keep, bits):
    total = keep.astype(jnp.float32) + flip(send, "dp", 1).astype(jnp.float32)
    for b in bits[1:-1]:
        total = total[0::2] + flip(total[1::2].astype(jnp.bfloat16), "dp", 1 << b).astype(jnp.float32)
    return total[0::2], total[1::2].astype(jnp.bfloat16)


def everyone_s(share, other, at, bits):
    width = share.shape[2]
    top = 1 << bits[-1]
    parts = [(share, 0, [0]), (other, at, [top])]
    held, whose = jnp.concatenate([share, other[:, :, at : at + width]], axis=0), [0, top]
    for b in reversed(bits[:-1]):
        theirs = flip(held, "dp", 1 << b)
        parts.append((theirs, 0, [l | 1 << b for l in whose]))
        if b > 0:
            held, whose = jnp.concatenate([held, theirs], axis=0), whose + parts[-1][2]
    return parts


def on_device(tokens, expert_ids, scores, w_gate, w_up, w_down):
    n_owner, n_dp = lax.axis_size("expert"), lax.axis_size("dp")
    tok_rows, top = expert_ids.shape
    experts = w_gate.shape[0]
    capacity = 2 * tok_rows * top // (experts * n_owner)
    per_chunk = 2 if experts % 2 == 0 else 1
    most = n_owner * capacity
    chunks = experts // per_chunk

    meta = jnp.concatenate([expert_ids.T.astype(jnp.float32), scores.T], axis=0)
    metas = [meta] + [
        lax.ppermute(meta, "expert", [(i, (i - k) % n_owner) for i in range(n_owner)])
        for k in gathered_order(n_owner)[1:]
    ]
    me = lax.axis_index("dp").astype(jnp.int32)
    first = lax.axis_index("expert").astype(jnp.int32) * experts
    info = jnp.stack([first, me, backwards(me, n_dp)])
    of = lambda c: list(range(c * per_chunk, (c + 1) * per_chunk))
    given = stage(info, w_gate, of(0), 1)
    feeds = gathered(tokens, "expert", (given, *metas[1:]))
    rank, wt = route(metas, info, experts)

    tall, wide = [feed.shape[0] for feed in feeds], tokens.shape[1]
    narrow = wide // block_of(wide) // 2 * block_of(wide)
    final = [(cut, wide - narrow) for cut in tall] + ([(cut, narrow) for cut in tall] if narrow else [])
    bits = bits_of(n_dp)
    cross = 1 << bits[-1]
    sent, parts, total = [], [], None
    share = kept = late = None

    def add(c, after):
        outs = final if c == chunks - 1 else [(sum(tall), wide)]
        return down(parts[c], rank, wt, info, w_down, total, of(c), outs, after)

    for c in range(chunks):
        last = c == chunks - 1
        send, rows, given = half_units(
            [*feeds, rank], info, given, w_gate, w_up, of(c), most, n_dp, 1, (of(c), 0), sent[-1:]
        )
        ahead = None if last else (of(c + 1), 1)
        keep, *given = half_units(
            [rows], info, given, w_gate, w_up, of(c), most, n_dp, 0, ahead, []
        )
        given = given[0] if given else None
        before, behind = kept, late
        kept, out = chip_sums(send, keep, bits)
        width = out.shape[2]
        if c > 0:
            share = finish(before, behind[:, :, :width], [])
            out = jnp.concatenate([out, share], axis=2)
        sent.append(out)
        late = flip(out, "dp", cross)
        if c > 0:
            parts.append(everyone_s(share, late, width, bits))
        if last:
            for d in range(min(c - 1, 2)):
                total = add(d, [out] if d == 0 else [])
    share = finish(kept, late[:, :, :width], [] if total is None else [total])
    other = flip(share, "dp", cross)
    for c in range(max(min(chunks - 2, 2), 0), chunks - 1):
        total = add(c, [share])
    if total is not None:
        other = lax.optimization_barrier((other, total))[0]
    parts.append(everyone_s(share, other, 0, bits))
    total = add(chunks - 1, [])
    mixed = [returned(total[k : k + len(tall)], "expert") for k in range(0, len(total), len(tall))]
    return jnp.concatenate(mixed, axis=1).astype(jnp.bfloat16)


def gathered_order(n):
    near = [d for s in range(1, n // 2) for d in (-s, s)]
    return [0] + near + ([n // 2] if n > 1 else [])


def gathered(x, axis, beside):
    n = lax.axis_size(axis)
    up, down_ = [(i, (i + 1) % n) for i in range(n)], [(i, (i - 1) % n) for i in range(n)]
    below = above = x
    found = [x]
    for _ in range(1, n // 2):
        below, above = lax.ppermute(below, axis, up), lax.ppermute(above, axis, down_)
        found += [below, above]
    if n > 1:
        half = x.shape[0] // 2
        below, above, *_ = lax.optimization_barrier((below, above, *beside))
        found += [lax.ppermute(below[:half], axis, up), lax.ppermute(above[half:], axis, down_)]
    return found


def returned(partials, axis):
    n = lax.axis_size(axis)
    up, down_ = [(i, (i + 1) % n) for i in range(n)], [(i, (i - 1) % n) for i in range(n)]
    wide = lambda x: x.astype(jnp.float32)
    near = {0: partials[0]}
    if n == 1:
        return wide(near[0])
    for k, partial in zip(gathered_order(n)[1:-1], partials[1:-2]):
        near[k] = partial
    half = partials[-1].shape[0]
    low, high = lax.ppermute(partials[-2], axis, down_), lax.ppermute(partials[-1], axis, up)
    halves = True
    for s in range(n // 2 - 1, 0, -1):
        a, b = wide(near[-s]), wide(near[s])
        if halves:
            a = jnp.concatenate([a[:half] + wide(low), a[half:]], axis=0)
            b = jnp.concatenate([b[:half], b[half:] + wide(high)], axis=0)
        else:
            a, b = a + wide(low), b + wide(high)
        low = lax.ppermute(a.astype(jnp.bfloat16), axis, down_)
        high = lax.ppermute(b.astype(jnp.bfloat16), axis, up)
        halves = False
    if halves:
        back = jnp.concatenate([wide(low), wide(high)], axis=0)
    else:
        back = wide(low) + wide(high)
    return wide(near[0]) + back


def solution(mesh):
    in_specs = (
        P(("groups", "expert"), "dp"),
        P(("groups", "expert"), None),
        P(("groups", "expert"), None),
        P("expert", "dp", None),
        P("expert", "dp", None),
        P("expert", None, "dp"),
    )
    out_specs = P(("groups", "expert"), "dp")
    return jax.shard_map(
        on_device, mesh=mesh, in_specs=in_specs, out_specs=out_specs, check_vma=False
    )
```

```python
import functools

import jax
import jax.numpy as jnp
from jax import lax
from jax.experimental import pallas as pl
from jax.experimental.pallas import tpu as pltpu
from jax.sharding import PartitionSpec as P

LANES = 128
VMEM = pl.BlockSpec(memory_space=pltpu.VMEM)
SMEM = pl.BlockSpec(memory_space=pltpu.SMEM)
HERE = pl.BlockSpec(memory_space=pl.ANY)
FAR = pl.BlockSpec(memory_space=pltpu.HBM)
NOWHERE = -1e6


def bits_of(n):
    return [b for b in range(n.bit_length() - 1)]


def flip(x, axis, k):
    return lax.ppermute(x, axis, [(i, i ^ k) for i in range(lax.axis_size(axis))])


def route_body(n, experts, info, *refs):
    meta, (rank, wt) = refs[:n], refs[n:]
    tok, top = meta[0].shape[1], meta[0].shape[0] // 2
    padded = rank.shape[0]
    first = info[0].astype(jnp.float32)
    e = lax.broadcasted_iota(jnp.int32, (padded, tok), 0).astype(jnp.float32)
    before = (
        lax.broadcasted_iota(jnp.int32, (tok, tok), 0) < lax.broadcasted_iota(jnp.int32, (tok, tok), 1)
    ).astype(jnp.bfloat16)
    count = jnp.zeros((padded, 1), jnp.float32)
    for s in range(n):
        ids, scores = meta[s][:top], meta[s][top:]
        affinity = 1.0 / (1.0 + jnp.exp(-scores))
        share = 2.5 * affinity / jnp.sum(affinity, axis=0, keepdims=True)
        named = jnp.zeros((padded, tok), jnp.float32)
        weight = jnp.zeros((padded, tok), jnp.float32)
        for k in range(top):
            hit = jnp.where(ids[k : k + 1] - first == e, 1.0, 0.0)
            named = named + hit
            weight = weight + hit * share[k : k + 1]
        named = jnp.where(e < experts, named, 0.0)
        place = jnp.dot(named.astype(jnp.bfloat16), before, preferred_element_type=jnp.float32) + count
        rank[:, s * tok : (s + 1) * tok] = jnp.where(named > 0, place, NOWHERE)
        wt[:, s * tok : (s + 1) * tok] = weight
        count = count + jnp.sum(named, axis=1, keepdims=True)


def route(meta, info, experts):
    tokens = len(meta) * meta[0].shape[1]
    table = jax.ShapeDtypeStruct((-(-experts // 8) * 8, tokens), jnp.float32)
    return pl.pallas_call(
        functools.partial(route_body, len(meta), experts),
        out_shape=(table, table),
        in_specs=[SMEM] + [VMEM] * len(meta),
        out_specs=(VMEM, VMEM),
        compiler_params=pltpu.CompilerParams(vmem_limit_bytes=40 << 20),
        name="route",
    )(info, *meta)


def backwards(l, n):
    bits = bits_of(n)
    return sum((((l >> b) & 1) << (len(bits) - 1 - b) for b in bits), 0 * l)


def units_of(l, info, n, width):
    return pl.ds(pl.multiple_of((backwards(l, n) ^ info[2]) * width, width), width)


def set_shape(need, weights):
    (_, depth, wide), (experts, side) = weights[0].shape, need
    return (len(experts), depth, wide) if side is None else (2, len(experts), depth, wide // 2)


def set_copies(need, weights, info, to, sem):
    experts, side = need
    if side is None:
        return [pltpu.make_async_copy(weights[0].at[e], to.at[x], sem.at[x]) for x, e in enumerate(experts)]
    half = to.shape[-1]
    units = pl.ds(pl.multiple_of(((info[1] & 1) ^ side) * half, half), half)
    return [
        pltpu.make_async_copy(w.at[e, :, units], to.at[m, x], sem.at[m * len(experts) + x])
        for m, w in enumerate(weights)
        for x, e in enumerate(experts)
    ]


def call(body, name, info, inputs, weights, ahead, after, outs, scratch, limit=24):
    n_in, n_out = len(inputs), len(outs)
    outs = list(outs)
    weights = [] if ahead is None else weights[2:] if ahead[1] is None else weights[:2]
    if ahead is not None:
        outs.append(jax.ShapeDtypeStruct(set_shape(ahead, weights), jnp.bfloat16))
        scratch = scratch + [pltpu.SemaphoreType.DMA((2 * len(ahead[0]),))]

    def whole(info, *refs):
        own, far = refs[:n_in], refs[n_in : n_in + len(weights)]
        rest = refs[n_in + len(weights) + len(after) :]
        results, rest = rest[: len(outs)], rest[len(outs) :]
        on = []
        if ahead is not None:
            on = set_copies(ahead, far, info, results[-1], rest[-1])
            rest = rest[:-1]
        body(info, own, results[:n_out], rest, lambda: [copy.start() for copy in on])
        for copy in on:
            copy.wait()

    return pl.pallas_call(
        whole,
        out_shape=tuple(outs),
        in_specs=[SMEM] + [spec for _, spec in inputs] + [HERE] * (len(weights) + len(after)),
        out_specs=(VMEM,) * len(outs),
        scratch_shapes=scratch,
        compiler_params=pltpu.CompilerParams(vmem_limit_bytes=limit << 20),
        cost_estimate=pl.CostEstimate(flops=1, bytes_accessed=1, transcendentals=0),
        name=name,
    )(info, *[x for x, _ in inputs], *weights, *after)


def stage(info, weights, need, after):
    body = lambda info, own, outs, rest, fetch: fetch()
    return call(body, "stage", info, [], weights, need, after, [], [], 40)[0]


def products(rows, given, to, info):
    most = rows.shape[0] // given.shape[1]
    shares, width = to.shape[0], to.shape[2] // 2
    for m in range(2):
        for x in range(given.shape[1]):
            mine = slice(x * most, (x + 1) * most)
            part = jnp.dot(rows[mine], given[m, x], preferred_element_type=jnp.float32)
            part = part.astype(jnp.bfloat16)
            for q in range(shares):
                j = backwards(q, shares) ^ (info[1] >> 1)
                to[j, mine, m * width : (m + 1) * width] = part[:, q * width : (q + 1) * width]


def send_body(experts, info, own, outs, rest, fetch):
    sources, rank, given = own[:-2], own[-2], own[-1]
    (to, rows), (feed, feed_sem) = outs, rest
    at, feeds = 0, []
    for s, source in enumerate(sources):
        tok = source.shape[0]
        feeds.append(pltpu.make_async_copy(source, feed.at[pl.ds(at, tok)], feed_sem.at[s]))
        at += tok
    for copy in feeds:
        copy.start()
    fetch()
    most = rows.shape[0] // len(experts)
    r = lax.broadcasted_iota(jnp.int32, (most, at), 0).astype(jnp.float32)
    pick = jnp.concatenate(
        [jnp.where(r == rank[e : e + 1, :], 1.0, 0.0).astype(jnp.bfloat16) for e in experts], axis=0
    )
    for copy in feeds:
        copy.wait()
    rows[...] = jnp.dot(pick, feed[...], preferred_element_type=jnp.float32).astype(jnp.bfloat16)
    products(rows, given, to, info)


def keep_body(info, own, outs, rest, fetch):
    fetch()
    rows, given = own
    products(rows, given, outs[0], info)


def part_shape(given, most, n_dp):
    _, experts, _, half = given.shape
    return jax.ShapeDtypeStruct((n_dp // 2, most * experts, 4 * half // n_dp), jnp.bfloat16)


def send_half(feeds, rank, info, given, weights, experts, most, n_dp, ahead, after):
    local = given.shape[2]
    rows = jax.ShapeDtypeStruct((most * len(experts), local), jnp.bfloat16)
    scratch = [
        pltpu.VMEM((rank.shape[1], local), jnp.bfloat16),
        pltpu.SemaphoreType.DMA((len(feeds),)),
    ]
    inputs = [(feed, HERE) for feed in feeds] + [(rank, VMEM), (given, VMEM)]
    outs = [part_shape(given, most, n_dp), rows]
    body = functools.partial(send_body, experts)
    return call(body, "send_half", info, inputs, weights, ahead, after, outs, scratch)


def keep_half(rows, info, given, weights, most, n_dp, ahead):
    inputs = [(rows, VMEM), (given, VMEM)]
    outs = [part_shape(given, most, n_dp)]
    return call(keep_body, "keep_half", info, inputs, weights, ahead, [], outs, [])


def down_body(lanes, experts, first, info, own, outs, rest, fetch):
    fetch()
    parts, (rank, wt, given) = own[: len(lanes)], own[len(lanes) : len(lanes) + 3]
    before = None if first else own[-1]
    hidden, mix, out = rest
    most = hidden.shape[0] // len(experts)
    width = parts[0].shape[-1]
    n_dp = hidden.shape[1] // width
    for part, (at, shares) in zip(parts, lanes):
        for j, l in enumerate(shares):
            hidden[:, units_of(l, info, n_dp, width)] = part[j, :, at : at + width]
    r = lax.broadcasted_iota(jnp.int32, (most, mix.shape[1]), 0).astype(jnp.float32)
    for x, e in enumerate(experts):
        mix[x * most : (x + 1) * most, :] = jnp.where(
            r == rank[e : e + 1, :], wt[e : e + 1, :], 0.0
        ).astype(jnp.bfloat16)
    local = out.shape[1]
    block = 512 if local % 512 == 0 else 256 if local % 256 == 0 else local
    for i in range(local // block):
        cols = slice(i * block, (i + 1) * block)
        for x in range(len(experts)):
            mine = slice(x * most, (x + 1) * most)
            out[mine, cols] = jnp.dot(
                hidden[mine], given[x, :, cols], preferred_element_type=jnp.float32
            ).astype(jnp.bfloat16)
        total = lax.dot_general(
            mix[...], out[:, cols], (((0,), (0,)), ((), ())), preferred_element_type=jnp.float32
        )
        if not first:
            total = total + before[:, cols]
        at = 0
        for to in outs:
            to[:, cols] = total[at : at + to.shape[0]].astype(to.dtype)
            at += to.shape[0]


def down(parts, rank, wt, info, given, weights, total, experts, cuts, ahead, after):
    parts, lanes = [part for part, *_ in parts], [tuple(where) for _, *where in parts]
    rows = parts[0].shape[1]
    _, hidden, local = given.shape
    kind = jnp.bfloat16 if len(cuts) > 1 else jnp.float32
    before = [] if total is None else [total]
    outs = [jax.ShapeDtypeStruct((cut, local), kind) for cut in cuts]
    scratch = [
        pltpu.VMEM((rows, hidden), jnp.bfloat16),
        pltpu.VMEM((rows, rank.shape[1]), jnp.bfloat16),
        pltpu.VMEM((rows, local), jnp.bfloat16),
    ]
    inputs = [(x, VMEM) for x in (*parts, rank, wt, given, *before)]
    body = functools.partial(down_body, lanes, experts, total is None)
    return call(body, "down", info, inputs, weights, ahead, after, outs, scratch)


def finish(total, late, after):
    if after:
        late, *_ = lax.optimization_barrier((late, *after))
    gate_up = total + late.astype(jnp.float32)
    width = gate_up.shape[2] // 2
    return (jax.nn.silu(gate_up[:, :, :width]) * gate_up[:, :, width:]).astype(jnp.bfloat16)


def chip_sums(send, keep, bits):
    total = keep.astype(jnp.float32) + flip(send, "dp", 1).astype(jnp.float32)
    for b in bits[1:-1]:
        total = total[0::2] + flip(total[1::2].astype(jnp.bfloat16), "dp", 1 << b).astype(jnp.float32)
    return total[0::2], total[1::2].astype(jnp.bfloat16)


def everyone_s(share, other, at, bits):
    width = share.shape[2]
    top = 1 << bits[-1]
    parts = [(share, 0, [0]), (other, at, [top])]
    held, whose = jnp.concatenate([share, other[:, :, at : at + width]], axis=0), [0, top]
    for b in reversed(bits[:-1]):
        theirs = flip(held, "dp", 1 << b)
        parts.append((theirs, 0, [l | 1 << b for l in whose]))
        if b > 0:
            held, whose = jnp.concatenate([held, theirs], axis=0), whose + parts[-1][2]
    return parts


def on_device(tokens, expert_ids, scores, w_gate, w_up, w_down):
    n_owner, n_dp = lax.axis_size("expert"), lax.axis_size("dp")
    tok_rows, top = expert_ids.shape
    experts = w_gate.shape[0]
    capacity = 2 * tok_rows * top // (experts * n_owner)
    per_chunk = 2 if experts % 2 == 0 else 1
    most = n_owner * capacity
    chunks = experts // per_chunk

    meta = jnp.concatenate([expert_ids.T.astype(jnp.float32), scores.T], axis=0)
    me = lax.axis_index("dp").astype(jnp.int32)
    first = lax.axis_index("expert").astype(jnp.int32) * experts
    info = jnp.stack([first, me, backwards(me, n_dp)])
    of = lambda c: list(range(c * per_chunk, (c + 1) * per_chunk))
    weights = (w_gate, w_up, w_down)
    needs = [(of(c), side) for c in range(chunks) for side in (1, 0)] + [(of(c), None) for c in range(chunks)]
    given = {0: stage(info, weights, needs[0], [])}

    def fetched(k, outs):
        if k + 2 < len(needs):
            *outs, given[k + 2] = outs
        return outs

    ahead = lambda k: needs[k + 2] if k + 2 < len(needs) else None

    meta = lax.optimization_barrier((meta, given[0]))[0]
    metas = [meta] + [
        lax.ppermute(meta, "expert", [(i, (i - k) % n_owner) for i in range(n_owner)])
        for k in gathered_order(n_owner)[1:]
    ]
    feeds, halfway = gathered(tokens, "expert", metas)
    given[1] = stage(info, weights, needs[1], halfway)
    rank, wt = route(metas, info, experts)

    tall, wide = [feed.shape[0] for feed in feeds], tokens.shape[1]
    bits = bits_of(n_dp)
    cross = 1 << bits[-1]
    sent, parts, total = [], [], None
    share = kept = late = None

    def add(c, after):
        k, cuts = 2 * chunks + c, tall if c == chunks - 1 else [sum(tall)]
        outs = down(parts[c], rank, wt, info, given[k], weights, total, of(c), cuts, ahead(k), after)
        outs = fetched(k, outs)
        return outs if c == chunks - 1 else outs[0]

    for c in range(chunks):
        last = c == chunks - 1
        k = 2 * c
        send, rows = fetched(
            k, send_half(feeds, rank, info, given[k], weights, of(c), most, n_dp, ahead(k), sent[-1:] or [given[1]])
        )
        k = 2 * c + 1
        (keep,) = fetched(k, keep_half(rows, info, given[k], weights, most, n_dp, ahead(k)))
        before, behind = kept, late
        kept, out = chip_sums(send, keep, bits)
        width = out.shape[2]
        if c > 0:
            share = finish(before, behind[:, :, :width], [])
            out = jnp.concatenate([out, share], axis=2)
        sent.append(out)
        late = flip(out, "dp", cross)
        if c > 0:
            parts.append(everyone_s(share, late, width, bits))
        if last:
            for d in range(min(c - 1, 2)):
                total = add(d, [out] if d == 0 else [])
    share = finish(kept, late[:, :, :width], [] if total is None else [total])
    other = flip(share, "dp", cross)
    for c in range(max(min(chunks - 2, 2), 0), chunks - 1):
        total = add(c, [share])
    if total is not None:
        other = lax.optimization_barrier((other, total))[0]
    parts.append(everyone_s(share, other, 0, bits))
    total = add(chunks - 1, [])
    return returned(total, "expert").astype(jnp.bfloat16)


def gathered_order(n):
    near = [d for s in range(1, n // 2) for d in (-s, s)]
    return [0] + near + ([n // 2] if n > 1 else [])


def gathered(x, axis, beside):
    n = lax.axis_size(axis)
    up, down_ = [(i, (i + 1) % n) for i in range(n)], [(i, (i - 1) % n) for i in range(n)]
    below = above = x
    found, halfway = [x], []
    for _ in range(1, n // 2):
        below, above = lax.ppermute(below, axis, up), lax.ppermute(above, axis, down_)
        found += [below, above]
    if n > 1:
        half = x.shape[0] // 2
        below, above, *_ = lax.optimization_barrier((below, above, *beside))
        halfway = [below]
        found += [lax.ppermute(below[:half], axis, up), lax.ppermute(above[half:], axis, down_)]
    return found, halfway


def returned(partials, axis):
    n = lax.axis_size(axis)
    up, down_ = [(i, (i + 1) % n) for i in range(n)], [(i, (i - 1) % n) for i in range(n)]
    wide = lambda x: x.astype(jnp.float32)
    near = {0: partials[0]}
    if n == 1:
        return wide(near[0])
    for k, partial in zip(gathered_order(n)[1:-1], partials[1:-2]):
        near[k] = partial
    half = partials[-1].shape[0]
    low, high = lax.ppermute(partials[-2], axis, down_), lax.ppermute(partials[-1], axis, up)
    halves = True
    for s in range(n // 2 - 1, 0, -1):
        a, b = wide(near[-s]), wide(near[s])
        if halves:
            a = jnp.concatenate([a[:half] + wide(low), a[half:]], axis=0)
            b = jnp.concatenate([b[:half], b[half:] + wide(high)], axis=0)
        else:
            a, b = a + wide(low), b + wide(high)
        low = lax.ppermute(a.astype(jnp.bfloat16), axis, down_)
        high = lax.ppermute(b.astype(jnp.bfloat16), axis, up)
        halves = False
    if halves:
        back = jnp.concatenate([wide(low), wide(high)], axis=0)
    else:
        back = wide(low) + wide(high)
    return wide(near[0]) + back


def solution(mesh):
    in_specs = (
        P(("groups", "expert"), "dp"),
        P(("groups", "expert"), None),
        P(("groups", "expert"), None),
        P("expert", "dp", None),
        P("expert", "dp", None),
        P("expert", None, "dp"),
    )
    out_specs = P(("groups", "expert"), "dp")
    return jax.shard_map(
        on_device, mesh=mesh, in_specs=in_specs, out_specs=out_specs, check_vma=False
    )
```

```python
import functools

import jax
import jax.numpy as jnp
from jax import lax
from jax.experimental import pallas as pl
from jax.experimental.pallas import tpu as pltpu
from jax.sharding import PartitionSpec as P

LANES = 128
VMEM = pl.BlockSpec(memory_space=pltpu.VMEM)
SMEM = pl.BlockSpec(memory_space=pltpu.SMEM)
HERE = pl.BlockSpec(memory_space=pl.ANY)
FAR = pl.BlockSpec(memory_space=pltpu.HBM)
NOWHERE = -1e6


def bits_of(n):
    return [b for b in range(n.bit_length() - 1)]


def flip(x, axis, k):
    return lax.ppermute(x, axis, [(i, i ^ k) for i in range(lax.axis_size(axis))])


def route_body(n, experts, info, *refs):
    meta, (rank, wt) = refs[:n], refs[n:]
    tok, top = meta[0].shape[1], meta[0].shape[0] // 2
    padded = rank.shape[0]
    first = info[0].astype(jnp.float32)
    e = lax.broadcasted_iota(jnp.int32, (padded, tok), 0).astype(jnp.float32)
    before = (
        lax.broadcasted_iota(jnp.int32, (tok, tok), 0) < lax.broadcasted_iota(jnp.int32, (tok, tok), 1)
    ).astype(jnp.bfloat16)
    count = jnp.zeros((padded, 1), jnp.float32)
    for s in range(n):
        ids, scores = meta[s][:top], meta[s][top:]
        affinity = 1.0 / (1.0 + jnp.exp(-scores))
        share = 2.5 * affinity / jnp.sum(affinity, axis=0, keepdims=True)
        named = jnp.zeros((padded, tok), jnp.float32)
        weight = jnp.zeros((padded, tok), jnp.float32)
        for k in range(top):
            hit = jnp.where(ids[k : k + 1] - first == e, 1.0, 0.0)
            named = named + hit
            weight = weight + hit * share[k : k + 1]
        named = jnp.where(e < experts, named, 0.0)
        place = jnp.dot(named.astype(jnp.bfloat16), before, preferred_element_type=jnp.float32) + count
        rank[:, s * tok : (s + 1) * tok] = jnp.where(named > 0, place, NOWHERE)
        wt[:, s * tok : (s + 1) * tok] = weight
        count = count + jnp.sum(named, axis=1, keepdims=True)


def route(meta, info, experts):
    tokens = len(meta) * meta[0].shape[1]
    table = jax.ShapeDtypeStruct((-(-experts // 8) * 8, tokens), jnp.float32)
    return pl.pallas_call(
        functools.partial(route_body, len(meta), experts),
        out_shape=(table, table),
        in_specs=[SMEM] + [VMEM] * len(meta),
        out_specs=(VMEM, VMEM),
        compiler_params=pltpu.CompilerParams(vmem_limit_bytes=40 << 20),
        name="route",
    )(info, *meta)


def backwards(l, n):
    bits = bits_of(n)
    return sum((((l >> b) & 1) << (len(bits) - 1 - b) for b in bits), 0 * l)


def units_of(l, info, n, width):
    return pl.ds(pl.multiple_of((backwards(l, n) ^ info[2]) * width, width), width)


def set_shape(need, weights):
    (_, depth, wide), (experts, side) = weights[0].shape, need
    return (len(experts), depth, wide) if side is None else (2, len(experts), depth, wide // 2)


def set_copies(need, weights, info, to, sem):
    experts, side = need
    if side is None:
        return [pltpu.make_async_copy(weights[0].at[e], to.at[x], sem.at[x]) for x, e in enumerate(experts)]
    half = to.shape[-1]
    units = pl.ds(pl.multiple_of(((info[1] & 1) ^ side) * half, half), half)
    return [
        pltpu.make_async_copy(w.at[e, :, units], to.at[m, x], sem.at[m * len(experts) + x])
        for m, w in enumerate(weights)
        for x, e in enumerate(experts)
    ]


def call(body, name, info, inputs, weights, ahead, after, outs, scratch, limit=24):
    n_in, n_out = len(inputs), len(outs)
    outs = list(outs)
    weights = [] if ahead is None else weights[2:] if ahead[1] is None else weights[:2]
    if ahead is not None:
        outs.append(jax.ShapeDtypeStruct(set_shape(ahead, weights), jnp.bfloat16))
        scratch = scratch + [pltpu.SemaphoreType.DMA((2 * len(ahead[0]),))]

    def whole(info, *refs):
        own, far = refs[:n_in], refs[n_in : n_in + len(weights)]
        rest = refs[n_in + len(weights) + len(after) :]
        results, rest = rest[: len(outs)], rest[len(outs) :]
        on = []
        if ahead is not None:
            on = set_copies(ahead, far, info, results[-1], rest[-1])
            rest = rest[:-1]
        body(info, own, results[:n_out], rest, lambda: [copy.start(priority=i % 2) for i, copy in enumerate(on)])
        for copy in on:
            copy.wait()

    return pl.pallas_call(
        whole,
        out_shape=tuple(outs),
        in_specs=[SMEM] + [spec for _, spec in inputs] + [HERE] * (len(weights) + len(after)),
        out_specs=(VMEM,) * len(outs),
        scratch_shapes=scratch,
        compiler_params=pltpu.CompilerParams(vmem_limit_bytes=limit << 20),
        cost_estimate=pl.CostEstimate(flops=1, bytes_accessed=1, transcendentals=0),
        name=name,
    )(info, *[x for x, _ in inputs], *weights, *after)


def stage(info, weights, need, after):
    body = lambda info, own, outs, rest, fetch: fetch()
    return call(body, "stage", info, [], weights, need, after, [], [], 40)[0]


def products(rows, given, to, info):
    most = rows.shape[0] // given.shape[1]
    shares, width = to.shape[0], to.shape[2] // 2
    for m in range(2):
        for x in range(given.shape[1]):
            mine = slice(x * most, (x + 1) * most)
            part = jnp.dot(rows[mine], given[m, x], preferred_element_type=jnp.float32)
            part = part.astype(jnp.bfloat16)
            for q in range(shares):
                j = backwards(q, shares) ^ (info[1] >> 1)
                to[j, mine, m * width : (m + 1) * width] = part[:, q * width : (q + 1) * width]


def send_body(experts, info, own, outs, rest, fetch):
    sources, rank, given = own[:-2], own[-2], own[-1]
    (to, rows), (feed, feed_sem) = outs, rest
    at, feeds = 0, []
    for s, source in enumerate(sources):
        tok = source.shape[0]
        feeds.append(pltpu.make_async_copy(source, feed.at[pl.ds(at, tok)], feed_sem.at[s]))
        at += tok
    for copy in feeds:
        copy.start()
    fetch()
    most = rows.shape[0] // len(experts)
    r = lax.broadcasted_iota(jnp.int32, (most, at), 0).astype(jnp.float32)
    pick = jnp.concatenate(
        [jnp.where(r == rank[e : e + 1, :], 1.0, 0.0).astype(jnp.bfloat16) for e in experts], axis=0
    )
    for copy in feeds:
        copy.wait()
    rows[...] = jnp.dot(pick, feed[...], preferred_element_type=jnp.float32).astype(jnp.bfloat16)
    products(rows, given, to, info)


def keep_body(info, own, outs, rest, fetch):
    fetch()
    rows, given = own
    products(rows, given, outs[0], info)


def part_shape(given, most, n_dp):
    _, experts, _, half = given.shape
    return jax.ShapeDtypeStruct((n_dp // 2, most * experts, 4 * half // n_dp), jnp.bfloat16)


def send_half(feeds, rank, info, given, weights, experts, most, n_dp, ahead, after):
    local = given.shape[2]
    rows = jax.ShapeDtypeStruct((most * len(experts), local), jnp.bfloat16)
    scratch = [
        pltpu.VMEM((rank.shape[1], local), jnp.bfloat16),
        pltpu.SemaphoreType.DMA((len(feeds),)),
    ]
    inputs = [(feed, HERE) for feed in feeds] + [(rank, VMEM), (given, VMEM)]
    outs = [part_shape(given, most, n_dp), rows]
    body = functools.partial(send_body, experts)
    return call(body, "send_half", info, inputs, weights, ahead, after, outs, scratch)


def keep_half(rows, info, given, weights, most, n_dp, ahead):
    inputs = [(rows, VMEM), (given, VMEM)]
    outs = [part_shape(given, most, n_dp)]
    return call(keep_body, "keep_half", info, inputs, weights, ahead, [], outs, [])


def down_body(lanes, experts, first, info, own, outs, rest, fetch):
    fetch()
    parts, (rank, wt, given) = own[: len(lanes)], own[len(lanes) : len(lanes) + 3]
    before = None if first else own[-1]
    hidden, mix, out = rest
    most = hidden.shape[0] // len(experts)
    width = parts[0].shape[-1]
    n_dp = hidden.shape[1] // width
    for part, (at, shares) in zip(parts, lanes):
        for j, l in enumerate(shares):
            hidden[:, units_of(l, info, n_dp, width)] = part[j, :, at : at + width]
    r = lax.broadcasted_iota(jnp.int32, (most, mix.shape[1]), 0).astype(jnp.float32)
    for x, e in enumerate(experts):
        mix[x * most : (x + 1) * most, :] = jnp.where(
            r == rank[e : e + 1, :], wt[e : e + 1, :], 0.0
        ).astype(jnp.bfloat16)
    local = out.shape[1]
    block = 512 if local % 512 == 0 else 256 if local % 256 == 0 else local
    for i in range(local // block):
        cols = slice(i * block, (i + 1) * block)
        for x in range(len(experts)):
            mine = slice(x * most, (x + 1) * most)
            out[mine, cols] = jnp.dot(
                hidden[mine], given[x, :, cols], preferred_element_type=jnp.float32
            ).astype(jnp.bfloat16)
        total = lax.dot_general(
            mix[...], out[:, cols], (((0,), (0,)), ((), ())), preferred_element_type=jnp.float32
        )
        if not first:
            total = total + before[:, cols]
        at = 0
        for to in outs:
            to[:, cols] = total[at : at + to.shape[0]].astype(to.dtype)
            at += to.shape[0]


def down(parts, rank, wt, info, given, weights, total, experts, cuts, ahead, after):
    parts, lanes = [part for part, *_ in parts], [tuple(where) for _, *where in parts]
    rows = parts[0].shape[1]
    _, hidden, local = given.shape
    kind = jnp.bfloat16 if len(cuts) > 1 else jnp.float32
    before = [] if total is None else [total]
    outs = [jax.ShapeDtypeStruct((cut, local), kind) for cut in cuts]
    scratch = [
        pltpu.VMEM((rows, hidden), jnp.bfloat16),
        pltpu.VMEM((rows, rank.shape[1]), jnp.bfloat16),
        pltpu.VMEM((rows, local), jnp.bfloat16),
    ]
    inputs = [(x, VMEM) for x in (*parts, rank, wt, given, *before)]
    body = functools.partial(down_body, lanes, experts, total is None)
    return call(body, "down", info, inputs, weights, ahead, after, outs, scratch)


def finish(total, late, after):
    if after:
        late, *_ = lax.optimization_barrier((late, *after))
    gate_up = total + late.astype(jnp.float32)
    width = gate_up.shape[2] // 2
    return (jax.nn.silu(gate_up[:, :, :width]) * gate_up[:, :, width:]).astype(jnp.bfloat16)


def chip_sums(send, keep, bits):
    total = keep.astype(jnp.float32) + flip(send, "dp", 1).astype(jnp.float32)
    for b in bits[1:-1]:
        total = total[0::2] + flip(total[1::2].astype(jnp.bfloat16), "dp", 1 << b).astype(jnp.float32)
    return total[0::2], total[1::2].astype(jnp.bfloat16)


def everyone_s(share, other, at, bits):
    width = share.shape[2]
    top = 1 << bits[-1]
    parts = [(share, 0, [0]), (other, at, [top])]
    held, whose = jnp.concatenate([share, other[:, :, at : at + width]], axis=0), [0, top]
    for b in reversed(bits[:-1]):
        theirs = flip(held, "dp", 1 << b)
        parts.append((theirs, 0, [l | 1 << b for l in whose]))
        if b > 0:
            held, whose = jnp.concatenate([held, theirs], axis=0), whose + parts[-1][2]
    return parts


def on_device(tokens, expert_ids, scores, w_gate, w_up, w_down):
    n_owner, n_dp = lax.axis_size("expert"), lax.axis_size("dp")
    tok_rows, top = expert_ids.shape
    experts = w_gate.shape[0]
    capacity = 2 * tok_rows * top // (experts * n_owner)
    per_chunk = 2 if experts % 2 == 0 else 1
    most = n_owner * capacity
    chunks = experts // per_chunk

    meta = jnp.concatenate([expert_ids.T.astype(jnp.float32), scores.T], axis=0)
    me = lax.axis_index("dp").astype(jnp.int32)
    first = lax.axis_index("expert").astype(jnp.int32) * experts
    info = jnp.stack([first, me, backwards(me, n_dp)])
    of = lambda c: list(range(c * per_chunk, (c + 1) * per_chunk))
    weights = (w_gate, w_up, w_down)
    needs = [(of(c), side) for c in range(chunks) for side in (1, 0)] + [(of(c), None) for c in range(chunks)]
    given = {0: stage(info, weights, needs[0], [])}

    def fetched(k, outs):
        if k + 2 < len(needs):
            *outs, given[k + 2] = outs
        return outs

    ahead = lambda k: needs[k + 2] if k + 2 < len(needs) else None

    meta = lax.optimization_barrier((meta, given[0]))[0]
    metas = [meta] + [
        lax.ppermute(meta, "expert", [(i, (i - k) % n_owner) for i in range(n_owner)])
        for k in gathered_order(n_owner)[1:]
    ]
    feeds, halfway = gathered(tokens, "expert", metas)
    given[1] = stage(info, weights, needs[1], halfway)
    rank, wt = route(metas, info, experts)

    tall, wide = [feed.shape[0] for feed in feeds], tokens.shape[1]
    bits = bits_of(n_dp)
    cross = 1 << bits[-1]
    sent, parts, total = [], [], None
    share = kept = late = None

    def add(c, after):
        k, cuts = 2 * chunks + c, tall if c == chunks - 1 else [sum(tall)]
        outs = down(parts[c], rank, wt, info, given[k], weights, total, of(c), cuts, ahead(k), after)
        outs = fetched(k, outs)
        return outs if c == chunks - 1 else outs[0]

    for c in range(chunks):
        last = c == chunks - 1
        k = 2 * c
        send, rows = fetched(
            k, send_half(feeds, rank, info, given[k], weights, of(c), most, n_dp, ahead(k), sent[-1:] or [given[1]])
        )
        k = 2 * c + 1
        (keep,) = fetched(k, keep_half(rows, info, given[k], weights, most, n_dp, ahead(k)))
        before, behind = kept, late
        kept, out = chip_sums(send, keep, bits)
        width = out.shape[2]
        if c > 0:
            share = finish(before, behind[:, :, :width], [])
            out = jnp.concatenate([out, share], axis=2)
        sent.append(out)
        late = flip(out, "dp", cross)
        if c > 0:
            parts.append(everyone_s(share, late, width, bits))
        if last:
            for d in range(min(c - 1, 2)):
                total = add(d, [out] if d == 0 else [])
    share = finish(kept, late[:, :, :width], [] if total is None else [total])
    other = flip(share, "dp", cross)
    for c in range(max(min(chunks - 2, 2), 0), chunks - 1):
        total = add(c, [share])
    if total is not None:
        other = lax.optimization_barrier((other, total))[0]
    parts.append(everyone_s(share, other, 0, bits))
    total = add(chunks - 1, [])
    return returned(total, "expert").astype(jnp.bfloat16)


def gathered_order(n):
    near = [d for s in range(1, n // 2) for d in (-s, s)]
    return [0] + near + ([n // 2] if n > 1 else [])


def gathered(x, axis, beside):
    n = lax.axis_size(axis)
    up, down_ = [(i, (i + 1) % n) for i in range(n)], [(i, (i - 1) % n) for i in range(n)]
    below = above = x
    found, halfway = [x], []
    for _ in range(1, n // 2):
        below, above = lax.ppermute(below, axis, up), lax.ppermute(above, axis, down_)
        found += [below, above]
    if n > 1:
        half = x.shape[0] // 2
        below, above, *_ = lax.optimization_barrier((below, above, *beside))
        halfway = [below]
        found += [lax.ppermute(below[:half], axis, up), lax.ppermute(above[half:], axis, down_)]
    return found, halfway


def returned(partials, axis):
    n = lax.axis_size(axis)
    up, down_ = [(i, (i + 1) % n) for i in range(n)], [(i, (i - 1) % n) for i in range(n)]
    wide = lambda x: x.astype(jnp.float32)
    near = {0: partials[0]}
    if n == 1:
        return wide(near[0])
    for k, partial in zip(gathered_order(n)[1:-1], partials[1:-2]):
        near[k] = partial
    half = partials[-1].shape[0]
    low, high = lax.ppermute(partials[-2], axis, down_), lax.ppermute(partials[-1], axis, up)
    halves = True
    for s in range(n // 2 - 1, 0, -1):
        a, b = wide(near[-s]), wide(near[s])
        if halves:
            a = jnp.concatenate([a[:half] + wide(low), a[half:]], axis=0)
            b = jnp.concatenate([b[:half], b[half:] + wide(high)], axis=0)
        else:
            a, b = a + wide(low), b + wide(high)
        low = lax.ppermute(a.astype(jnp.bfloat16), axis, down_)
        high = lax.ppermute(b.astype(jnp.bfloat16), axis, up)
        halves = False
    if halves:
        back = jnp.concatenate([wide(low), wide(high)], axis=0)
    else:
        back = wide(low) + wide(high)
    return wide(near[0]) + back


def solution(mesh):
    in_specs = (
        P(("groups", "expert"), "dp"),
        P(("groups", "expert"), None),
        P(("groups", "expert"), None),
        P("expert", "dp", None),
        P("expert", "dp", None),
        P("expert", None, "dp"),
    )
    out_specs = P(("groups", "expert"), "dp")
    return jax.shard_map(
        on_device, mesh=mesh, in_specs=in_specs, out_specs=out_specs, check_vma=False
    )
```

```python
import functools

import jax
import jax.numpy as jnp
from jax import lax
from jax.experimental import pallas as pl
from jax.experimental.pallas import tpu as pltpu
from jax.sharding import PartitionSpec as P

LANES = 128
VMEM = pl.BlockSpec(memory_space=pltpu.VMEM)
SMEM = pl.BlockSpec(memory_space=pltpu.SMEM)
HERE = pl.BlockSpec(memory_space=pl.ANY)
FAR = pl.BlockSpec(memory_space=pltpu.HBM)
NOWHERE = -1e6


def bits_of(n):
    return [b for b in range(n.bit_length() - 1)]


def flip(x, axis, k):
    return lax.ppermute(x, axis, [(i, i ^ k) for i in range(lax.axis_size(axis))])


def route_body(n, experts, info, *refs):
    meta, (rank, wt) = refs[:n], refs[n:]
    tok, top = meta[0].shape[1], meta[0].shape[0] // 2
    padded = rank.shape[0]
    first = info[0].astype(jnp.float32)
    e = lax.broadcasted_iota(jnp.int32, (padded, tok), 0).astype(jnp.float32)
    before = (
        lax.broadcasted_iota(jnp.int32, (tok, tok), 0) < lax.broadcasted_iota(jnp.int32, (tok, tok), 1)
    ).astype(jnp.bfloat16)
    count = jnp.zeros((padded, 1), jnp.float32)
    for s in range(n):
        ids, scores = meta[s][:top], meta[s][top:]
        affinity = 1.0 / (1.0 + jnp.exp(-scores))
        share = 2.5 * affinity / jnp.sum(affinity, axis=0, keepdims=True)
        named = jnp.zeros((padded, tok), jnp.float32)
        weight = jnp.zeros((padded, tok), jnp.float32)
        for k in range(top):
            hit = jnp.where(ids[k : k + 1] - first == e, 1.0, 0.0)
            named = named + hit
            weight = weight + hit * share[k : k + 1]
        named = jnp.where(e < experts, named, 0.0)
        place = jnp.dot(named.astype(jnp.bfloat16), before, preferred_element_type=jnp.float32) + count
        rank[:, s * tok : (s + 1) * tok] = jnp.where(named > 0, place, NOWHERE)
        wt[:, s * tok : (s + 1) * tok] = weight
        count = count + jnp.sum(named, axis=1, keepdims=True)


def route(meta, info, experts):
    tokens = len(meta) * meta[0].shape[1]
    table = jax.ShapeDtypeStruct((-(-experts // 8) * 8, tokens), jnp.float32)
    return pl.pallas_call(
        functools.partial(route_body, len(meta), experts),
        out_shape=(table, table),
        in_specs=[SMEM] + [VMEM] * len(meta),
        out_specs=(VMEM, VMEM),
        compiler_params=pltpu.CompilerParams(vmem_limit_bytes=40 << 20),
        name="route",
    )(info, *meta)


def backwards(l, n):
    bits = bits_of(n)
    return sum((((l >> b) & 1) << (len(bits) - 1 - b) for b in bits), 0 * l)


def units_of(l, info, n, width):
    return pl.ds(pl.multiple_of((backwards(l, n) ^ info[2]) * width, width), width)


def set_shape(need, weights):
    (_, depth, wide), (experts, side) = weights[0].shape, need
    return (len(experts), depth, wide) if side is None else (2, len(experts), depth, wide // 2)


def set_copies(need, weights, info, to, sem):
    experts, side = need
    if side is None:
        return [pltpu.make_async_copy(weights[0].at[e], to.at[x], sem.at[x]) for x, e in enumerate(experts)]
    half = to.shape[-1]
    units = pl.ds(pl.multiple_of(((info[1] & 1) ^ side) * half, half), half)
    return [
        pltpu.make_async_copy(w.at[e, :, units], to.at[m, x], sem.at[m * len(experts) + x])
        for m, w in enumerate(weights)
        for x, e in enumerate(experts)
    ]


def call(body, name, info, inputs, weights, ahead, after, outs, scratch, limit=24):
    n_in, n_out = len(inputs), len(outs)
    outs = list(outs)
    weights = [] if ahead is None else weights[2:] if ahead[1] is None else weights[:2]
    if ahead is not None:
        outs.append(jax.ShapeDtypeStruct(set_shape(ahead, weights), jnp.bfloat16))
        scratch = scratch + [pltpu.SemaphoreType.DMA((2 * len(ahead[0]),))]

    def whole(info, *refs):
        own, far = refs[:n_in], refs[n_in : n_in + len(weights)]
        rest = refs[n_in + len(weights) + len(after) :]
        results, rest = rest[: len(outs)], rest[len(outs) :]
        on = []
        if ahead is not None:
            on = set_copies(ahead, far, info, results[-1], rest[-1])
            rest = rest[:-1]
        body(info, own, results[:n_out], rest, lambda: [copy.start() for copy in on])
        for copy in on:
            copy.wait()

    return pl.pallas_call(
        whole,
        out_shape=tuple(outs),
        in_specs=[SMEM] + [spec for _, spec in inputs] + [HERE] * (len(weights) + len(after)),
        out_specs=(VMEM,) * len(outs),
        scratch_shapes=scratch,
        compiler_params=pltpu.CompilerParams(vmem_limit_bytes=limit << 20),
        cost_estimate=pl.CostEstimate(flops=1, bytes_accessed=1, transcendentals=0),
        name=name,
    )(info, *[x for x, _ in inputs], *weights, *after)


def stage(info, weights, need, after):
    body = lambda info, own, outs, rest, fetch: fetch()
    return call(body, "stage", info, [], weights, need, after, [], [], 40)[0]


def products(rows, given, to, info):
    count = rows.shape[0]
    most = count // given.shape[1]
    shares, _, width = to.shape
    for m in range(2):
        for x in range(given.shape[1]):
            mine = slice(x * most, (x + 1) * most)
            part = jnp.dot(rows[mine], given[m, x], preferred_element_type=jnp.float32)
            part = part.astype(jnp.bfloat16)
            for q in range(shares):
                j = backwards(q, shares) ^ (info[1] >> 1)
                to[j, m * count + x * most : m * count + (x + 1) * most, :] = part[:, q * width : (q + 1) * width]


def send_body(experts, info, own, outs, rest, fetch):
    sources, rank, given = own[:-2], own[-2], own[-1]
    (to, rows), (feed, feed_sem) = outs, rest
    at, feeds = 0, []
    for s, source in enumerate(sources):
        tok = source.shape[0]
        feeds.append(pltpu.make_async_copy(source, feed.at[pl.ds(at, tok)], feed_sem.at[s]))
        at += tok
    for copy in feeds:
        copy.start()
    fetch()
    most = rows.shape[0] // len(experts)
    r = lax.broadcasted_iota(jnp.int32, (most, at), 0).astype(jnp.float32)
    pick = jnp.concatenate(
        [jnp.where(r == rank[e : e + 1, :], 1.0, 0.0).astype(jnp.bfloat16) for e in experts], axis=0
    )
    for copy in feeds:
        copy.wait()
    rows[...] = jnp.dot(pick, feed[...], preferred_element_type=jnp.float32).astype(jnp.bfloat16)
    products(rows, given, to, info)


def keep_body(info, own, outs, rest, fetch):
    fetch()
    rows, given = own
    products(rows, given, outs[0], info)


def part_shape(given, most, n_dp):
    _, experts, _, half = given.shape
    return jax.ShapeDtypeStruct((n_dp // 2, 2 * most * experts, 2 * half // n_dp), jnp.bfloat16)


def send_half(feeds, rank, info, given, weights, experts, most, n_dp, ahead, after):
    local = given.shape[2]
    rows = jax.ShapeDtypeStruct((most * len(experts), local), jnp.bfloat16)
    scratch = [
        pltpu.VMEM((rank.shape[1], local), jnp.bfloat16),
        pltpu.SemaphoreType.DMA((len(feeds),)),
    ]
    inputs = [(feed, HERE) for feed in feeds] + [(rank, VMEM), (given, VMEM)]
    outs = [part_shape(given, most, n_dp), rows]
    body = functools.partial(send_body, experts)
    return call(body, "send_half", info, inputs, weights, ahead, after, outs, scratch)


def keep_half(rows, info, given, weights, most, n_dp, ahead):
    inputs = [(rows, VMEM), (given, VMEM)]
    outs = [part_shape(given, most, n_dp)]
    return call(keep_body, "keep_half", info, inputs, weights, ahead, [], outs, [])


def down_body(places, experts, first, info, own, outs, rest, fetch):
    fetch()
    parts, (rank, wt, given) = own[: len(places)], own[len(places) : len(places) + 3]
    before = None if first else own[-1]
    hidden, mix, out = rest
    most = hidden.shape[0] // len(experts)
    width = parts[0].shape[-1]
    n_dp = hidden.shape[1] // width
    for part, (at, shares) in zip(parts, places):
        for j, l in enumerate(shares):
            hidden[:, units_of(l, info, n_dp, width)] = part[j, at : at + hidden.shape[0], :]
    r = lax.broadcasted_iota(jnp.int32, (most, mix.shape[1]), 0).astype(jnp.float32)
    for x, e in enumerate(experts):
        mix[x * most : (x + 1) * most, :] = jnp.where(
            r == rank[e : e + 1, :], wt[e : e + 1, :], 0.0
        ).astype(jnp.bfloat16)
    local = out.shape[1]
    block = 512 if local % 512 == 0 else 256 if local % 256 == 0 else local
    for i in range(local // block):
        cols = slice(i * block, (i + 1) * block)
        for x in range(len(experts)):
            mine = slice(x * most, (x + 1) * most)
            out[mine, cols] = jnp.dot(
                hidden[mine], given[x, :, cols], preferred_element_type=jnp.float32
            ).astype(jnp.bfloat16)
        total = lax.dot_general(
            mix[...], out[:, cols], (((0,), (0,)), ((), ())), preferred_element_type=jnp.float32
        )
        if not first:
            total = total + before[:, cols]
        at = 0
        for to in outs:
            to[:, cols] = total[at : at + to.shape[0]].astype(to.dtype)
            at += to.shape[0]


def down(parts, rank, wt, info, given, weights, total, experts, cuts, ahead, after):
    parts, places = [part for part, *_ in parts], [tuple(where) for _, *where in parts]
    rows = parts[0].shape[1]
    _, hidden, local = given.shape
    kind = jnp.bfloat16 if len(cuts) > 1 else jnp.float32
    before = [] if total is None else [total]
    outs = [jax.ShapeDtypeStruct((cut, local), kind) for cut in cuts]
    scratch = [
        pltpu.VMEM((rows, hidden), jnp.bfloat16),
        pltpu.VMEM((rows, rank.shape[1]), jnp.bfloat16),
        pltpu.VMEM((rows, local), jnp.bfloat16),
    ]
    inputs = [(x, VMEM) for x in (*parts, rank, wt, given, *before)]
    body = functools.partial(down_body, places, experts, total is None)
    return call(body, "down", info, inputs, weights, ahead, after, outs, scratch)


def finish(total, late, after):
    if after:
        late, *_ = lax.optimization_barrier((late, *after))
    gate_up = total + late.astype(jnp.float32)
    rows = gate_up.shape[1] // 2
    return (jax.nn.silu(gate_up[:, :rows]) * gate_up[:, rows:]).astype(jnp.bfloat16)


def chip_sums(send, keep, bits):
    total = keep.astype(jnp.float32) + flip(send, "dp", 1).astype(jnp.float32)
    for b in bits[1:-1]:
        total = total[0::2] + flip(total[1::2].astype(jnp.bfloat16), "dp", 1 << b).astype(jnp.float32)
    return total[0::2], total[1::2].astype(jnp.bfloat16)


def everyone_s(share, other, at, bits):
    rows = share.shape[1]
    top = 1 << bits[-1]
    parts = [(share, 0, [0]), (other, at, [top])]
    held, whose = jnp.concatenate([share, other[:, at : at + rows]], axis=0), [0, top]
    for b in reversed(bits[:-1]):
        theirs = flip(held, "dp", 1 << b)
        parts.append((theirs, 0, [l | 1 << b for l in whose]))
        if b > 0:
            held, whose = jnp.concatenate([held, theirs], axis=0), whose + parts[-1][2]
    return parts


def on_device(tokens, expert_ids, scores, w_gate, w_up, w_down):
    n_owner, n_dp = lax.axis_size("expert"), lax.axis_size("dp")
    tok_rows, top = expert_ids.shape
    experts = w_gate.shape[0]
    capacity = 2 * tok_rows * top // (experts * n_owner)
    most = n_owner * capacity
    singles = experts < 4 or experts % 2 > 0
    starts = list(range(experts)) if singles else [0, *range(1, experts, 2)]
    of = [list(range(a, b)) for a, b in zip(starts, starts[1:] + [experts])]
    chunks = len(of)

    meta = jnp.concatenate([expert_ids.T.astype(jnp.float32), scores.T], axis=0)
    me = lax.axis_index("dp").astype(jnp.int32)
    first = lax.axis_index("expert").astype(jnp.int32) * experts
    info = jnp.stack([first, me, backwards(me, n_dp)])
    weights = (w_gate, w_up, w_down)
    needs = [(of[c], side) for c in range(chunks) for side in (1, 0)] + [(of[c], None) for c in range(chunks)]
    given = {k: stage(info, weights, needs[k], []) for k in (0, 1)}

    def fetched(k, outs):
        if k + 2 < len(needs):
            *outs, given[k + 2] = outs
        return outs

    ahead = lambda k: needs[k + 2] if k + 2 < len(needs) else None

    meta = lax.optimization_barrier((meta, given[0], given[1]))[0]
    metas = [meta] + [
        lax.ppermute(meta, "expert", [(i, (i - k) % n_owner) for i in range(n_owner)])
        for k in gathered_order(n_owner)[1:]
    ]
    feeds = gathered(tokens, "expert", metas)
    rank, wt = route(metas, info, experts)

    tall, wide = [feed.shape[0] for feed in feeds], tokens.shape[1]
    bits = bits_of(n_dp)
    cross = 1 << bits[-1]
    sent, parts, total = [], [], None
    share = kept = late = None

    def add(c, after):
        k, cuts = 2 * chunks + c, tall if c == chunks - 1 else [sum(tall)]
        outs = down(parts[c], rank, wt, info, given[k], weights, total, of[c], cuts, ahead(k), after)
        outs = fetched(k, outs)
        return outs if c == chunks - 1 else outs[0]

    for c in range(chunks):
        last = c == chunks - 1
        k = 2 * c
        send, rows = fetched(
            k, send_half(feeds, rank, info, given[k], weights, of[c], most, n_dp, ahead(k), sent[-1:])
        )
        k = 2 * c + 1
        (keep,) = fetched(k, keep_half(rows, info, given[k], weights, most, n_dp, ahead(k)))
        before, behind = kept, late
        kept, out = chip_sums(send, keep, bits)
        sums = out.shape[1]
        if c > 0:
            share = finish(before, behind[:, : before.shape[1]], [])
            out = jnp.concatenate([out, share], axis=1)
        sent.append(out)
        late = flip(out, "dp", cross)
        if c > 0:
            parts.append(everyone_s(share, late, sums, bits))
        if last:
            for d in range(min(c - 1, 2)):
                total = add(d, [out] if d == 0 else [])
    share = finish(kept, late[:, : kept.shape[1]], [] if total is None else [total])
    other = flip(share, "dp", cross)
    for c in range(max(min(chunks - 2, 2), 0), chunks - 1):
        total = add(c, [share])
    if total is not None:
        other = lax.optimization_barrier((other, total))[0]
    parts.append(everyone_s(share, other, 0, bits))
    total = add(chunks - 1, [])
    return returned(total, "expert").astype(jnp.bfloat16)


def gathered_order(n):
    near = [d for s in range(1, n // 2) for d in (-s, s)]
    return [0] + near + ([n // 2] if n > 1 else [])


def gathered(x, axis, beside):
    n = lax.axis_size(axis)
    up, down_ = [(i, (i + 1) % n) for i in range(n)], [(i, (i - 1) % n) for i in range(n)]
    below = above = x
    found = [x]
    for _ in range(1, n // 2):
        below, above = lax.ppermute(below, axis, up), lax.ppermute(above, axis, down_)
        found += [below, above]
    if n > 1:
        half = x.shape[0] // 2
        below, above, *_ = lax.optimization_barrier((below, above, *beside))
        found += [lax.ppermute(below[:half], axis, up), lax.ppermute(above[half:], axis, down_)]
    return found


def returned(partials, axis):
    n = lax.axis_size(axis)
    up, down_ = [(i, (i + 1) % n) for i in range(n)], [(i, (i - 1) % n) for i in range(n)]
    wide = lambda x: x.astype(jnp.float32)
    near = {0: partials[0]}
    if n == 1:
        return wide(near[0])
    for k, partial in zip(gathered_order(n)[1:-1], partials[1:-2]):
        near[k] = partial
    half = partials[-1].shape[0]
    low, high = lax.ppermute(partials[-2], axis, down_), lax.ppermute(partials[-1], axis, up)
    halves = True
    for s in range(n // 2 - 1, 0, -1):
        a, b = wide(near[-s]), wide(near[s])
        if halves:
            a = jnp.concatenate([a[:half] + wide(low), a[half:]], axis=0)
            b = jnp.concatenate([b[:half], b[half:] + wide(high)], axis=0)
        else:
            a, b = a + wide(low), b + wide(high)
        low = lax.ppermute(a.astype(jnp.bfloat16), axis, down_)
        high = lax.ppermute(b.astype(jnp.bfloat16), axis, up)
        halves = False
    if halves:
        back = jnp.concatenate([wide(low), wide(high)], axis=0)
    else:
        back = wide(low) + wide(high)
    return wide(near[0]) + back


def solution(mesh):
    in_specs = (
        P(("groups", "expert"), "dp"),
        P(("groups", "expert"), None),
        P(("groups", "expert"), None),
        P("expert", "dp", None),
        P("expert", "dp", None),
        P("expert", None, "dp"),
    )
    out_specs = P(("groups", "expert"), "dp")
    return jax.shard_map(
        on_device, mesh=mesh, in_specs=in_specs, out_specs=out_specs, check_vma=False
    )
```

```python
import functools

import jax
import jax.numpy as jnp
from jax import lax
from jax.experimental import pallas as pl
from jax.experimental.pallas import tpu as pltpu
from jax.sharding import PartitionSpec as P

LANES = 128
VMEM = pl.BlockSpec(memory_space=pltpu.VMEM)
SMEM = pl.BlockSpec(memory_space=pltpu.SMEM)
HERE = pl.BlockSpec(memory_space=pl.ANY)
FAR = pl.BlockSpec(memory_space=pltpu.HBM)
NOWHERE = -1e6


def bits_of(n):
    return [b for b in range(n.bit_length() - 1)]


def flip(x, axis, k):
    return lax.ppermute(x, axis, [(i, i ^ k) for i in range(lax.axis_size(axis))])


def route_body(n, experts, info, *refs):
    meta, (rank, wt) = refs[:n], refs[n:]
    tok, top = meta[0].shape[1], meta[0].shape[0] // 2
    padded = rank.shape[0]
    first = info[0].astype(jnp.float32)
    e = lax.broadcasted_iota(jnp.int32, (padded, tok), 0).astype(jnp.float32)
    before = (
        lax.broadcasted_iota(jnp.int32, (tok, tok), 0) < lax.broadcasted_iota(jnp.int32, (tok, tok), 1)
    ).astype(jnp.bfloat16)
    count = jnp.zeros((padded, 1), jnp.float32)
    for s in range(n):
        ids, scores = meta[s][:top], meta[s][top:]
        affinity = 1.0 / (1.0 + jnp.exp(-scores))
        share = 2.5 * affinity / jnp.sum(affinity, axis=0, keepdims=True)
        named = jnp.zeros((padded, tok), jnp.float32)
        weight = jnp.zeros((padded, tok), jnp.float32)
        for k in range(top):
            hit = jnp.where(ids[k : k + 1] - first == e, 1.0, 0.0)
            named = named + hit
            weight = weight + hit * share[k : k + 1]
        named = jnp.where(e < experts, named, 0.0)
        place = jnp.dot(named.astype(jnp.bfloat16), before, preferred_element_type=jnp.float32) + count
        rank[:, s * tok : (s + 1) * tok] = jnp.where(named > 0, place, NOWHERE)
        wt[:, s * tok : (s + 1) * tok] = weight
        count = count + jnp.sum(named, axis=1, keepdims=True)


def route(meta, info, experts):
    tokens = len(meta) * meta[0].shape[1]
    table = jax.ShapeDtypeStruct((-(-experts // 8) * 8, tokens), jnp.float32)
    return pl.pallas_call(
        functools.partial(route_body, len(meta), experts),
        out_shape=(table, table),
        in_specs=[SMEM] + [VMEM] * len(meta),
        out_specs=(VMEM, VMEM),
        compiler_params=pltpu.CompilerParams(vmem_limit_bytes=40 << 20),
        name="route",
    )(info, *meta)


def backwards(l, n):
    bits = bits_of(n)
    return sum((((l >> b) & 1) << (len(bits) - 1 - b) for b in bits), 0 * l)


def units_of(l, info, n, width):
    return pl.ds(pl.multiple_of((backwards(l, n) ^ info[2]) * width, width), width)


def set_shape(need, weights):
    (_, depth, wide), (experts, side) = weights[0].shape, need
    return (len(experts), depth, wide) if side is None else (2, len(experts), depth, wide // 2)


def set_copies(need, weights, info, to, sem):
    experts, side = need
    if side is None:
        return [pltpu.make_async_copy(weights[0].at[e], to.at[x], sem.at[x]) for x, e in enumerate(experts)]
    half = to.shape[-1]
    units = pl.ds(pl.multiple_of(((info[1] & 1) ^ side) * half, half), half)
    return [
        pltpu.make_async_copy(w.at[e, :, units], to.at[m, x], sem.at[m * len(experts) + x])
        for m, w in enumerate(weights)
        for x, e in enumerate(experts)
    ]


def call(body, name, info, inputs, weights, ahead, after, outs, scratch, limit=24):
    n_in, n_out = len(inputs), len(outs)
    outs = list(outs)
    weights = [] if ahead is None else weights[2:] if ahead[1] is None else weights[:2]
    if ahead is not None:
        outs.append(jax.ShapeDtypeStruct(set_shape(ahead, weights), jnp.bfloat16))
        scratch = scratch + [pltpu.SemaphoreType.DMA((2 * len(ahead[0]),))]

    def whole(info, *refs):
        own, far = refs[:n_in], refs[n_in : n_in + len(weights)]
        rest = refs[n_in + len(weights) + len(after) :]
        results, rest = rest[: len(outs)], rest[len(outs) :]
        on = []
        if ahead is not None:
            on = set_copies(ahead, far, info, results[-1], rest[-1])
            rest = rest[:-1]
        body(info, own, results[:n_out], rest, lambda: [copy.start() for copy in on])
        for copy in on:
            copy.wait()

    return pl.pallas_call(
        whole,
        out_shape=tuple(outs),
        in_specs=[SMEM] + [spec for _, spec in inputs] + [HERE] * (len(weights) + len(after)),
        out_specs=(VMEM,) * len(outs),
        scratch_shapes=scratch,
        compiler_params=pltpu.CompilerParams(vmem_limit_bytes=limit << 20),
        cost_estimate=pl.CostEstimate(flops=1, bytes_accessed=1, transcendentals=0),
        name=name,
    )(info, *[x for x, _ in inputs], *weights, *after)


def stage(info, weights, need, after):
    body = lambda info, own, outs, rest, fetch: fetch()
    return call(body, "stage", info, [], weights, need, after, [], [], 40)[0]


def products(rows, given, to, info):
    most = rows.shape[0] // given.shape[1]
    shares, width = to.shape[0], to.shape[2] // 2
    for m in range(2):
        for x in range(given.shape[1]):
            mine = slice(x * most, (x + 1) * most)
            part = jnp.dot(rows[mine], given[m, x], preferred_element_type=jnp.float32)
            part = part.astype(jnp.bfloat16)
            for q in range(shares):
                j = backwards(q, shares) ^ (info[1] >> 1)
                to[j, mine, m * width : (m + 1) * width] = part[:, q * width : (q + 1) * width]


def send_body(experts, info, own, outs, rest, fetch):
    sources, rank, given = own[:-2], own[-2], own[-1]
    (to, rows), (feed, feed_sem) = outs, rest
    at, feeds = 0, []
    for s, source in enumerate(sources):
        tok = source.shape[0]
        feeds.append(pltpu.make_async_copy(source, feed.at[pl.ds(at, tok)], feed_sem.at[s]))
        at += tok
    for copy in feeds:
        copy.start()
    fetch()
    most = rows.shape[0] // len(experts)
    r = lax.broadcasted_iota(jnp.int32, (most, at), 0).astype(jnp.float32)
    pick = jnp.concatenate(
        [jnp.where(r == rank[e : e + 1, :], 1.0, 0.0).astype(jnp.bfloat16) for e in experts], axis=0
    )
    for copy in feeds:
        copy.wait()
    rows[...] = jnp.dot(pick, feed[...], preferred_element_type=jnp.float32).astype(jnp.bfloat16)
    products(rows, given, to, info)


def keep_body(info, own, outs, rest, fetch):
    fetch()
    rows, given = own
    products(rows, given, outs[0], info)


def part_shape(given, most, n_dp):
    _, experts, _, half = given.shape
    return jax.ShapeDtypeStruct((n_dp // 2, most * experts, 4 * half // n_dp), jnp.bfloat16)


def send_half(feeds, rank, info, given, weights, experts, most, n_dp, ahead, after):
    local = given.shape[2]
    rows = jax.ShapeDtypeStruct((most * len(experts), local), jnp.bfloat16)
    scratch = [
        pltpu.VMEM((rank.shape[1], local), jnp.bfloat16),
        pltpu.SemaphoreType.DMA((len(feeds),)),
    ]
    inputs = [(feed, HERE) for feed in feeds] + [(rank, VMEM), (given, VMEM)]
    outs = [part_shape(given, most, n_dp), rows]
    body = functools.partial(send_body, experts)
    return call(body, "send_half", info, inputs, weights, ahead, after, outs, scratch)


def keep_half(rows, info, given, weights, most, n_dp, ahead):
    inputs = [(rows, VMEM), (given, VMEM)]
    outs = [part_shape(given, most, n_dp)]
    return call(keep_body, "keep_half", info, inputs, weights, ahead, [], outs, [])


def down_body(lanes, experts, first, info, own, outs, rest, fetch):
    fetch()
    parts, (rank, wt, given) = own[: len(lanes)], own[len(lanes) : len(lanes) + 3]
    before = None if first else own[-1]
    hidden, mix, out = rest
    most = hidden.shape[0] // len(experts)
    width = parts[0].shape[-1]
    n_dp = hidden.shape[1] // width
    for part, (at, shares) in zip(parts, lanes):
        for j, l in enumerate(shares):
            hidden[:, units_of(l, info, n_dp, width)] = part[j, :, at : at + width]
    r = lax.broadcasted_iota(jnp.int32, (most, mix.shape[1]), 0).astype(jnp.float32)
    for x, e in enumerate(experts):
        mix[x * most : (x + 1) * most, :] = jnp.where(
            r == rank[e : e + 1, :], wt[e : e + 1, :], 0.0
        ).astype(jnp.bfloat16)
    local = out.shape[1]
    block = 512 if local % 512 == 0 else 256 if local % 256 == 0 else local
    for i in range(local // block):
        cols = slice(i * block, (i + 1) * block)
        for x in range(len(experts)):
            mine = slice(x * most, (x + 1) * most)
            out[mine, cols] = jnp.dot(
                hidden[mine], given[x, :, cols], preferred_element_type=jnp.float32
            ).astype(jnp.bfloat16)
        total = lax.dot_general(
            mix[...], out[:, cols], (((0,), (0,)), ((), ())), preferred_element_type=jnp.float32
        )
        if not first:
            total = total + before[:, cols]
        at = 0
        for to in outs:
            to[:, cols] = total[at : at + to.shape[0]].astype(to.dtype)
            at += to.shape[0]


def down(parts, rank, wt, info, given, weights, total, experts, cuts, ahead, after):
    parts, lanes = [part for part, *_ in parts], [tuple(where) for _, *where in parts]
    rows = parts[0].shape[1]
    _, hidden, local = given.shape
    kind = jnp.bfloat16 if len(cuts) > 1 else jnp.float32
    before = [] if total is None else [total]
    outs = [jax.ShapeDtypeStruct((cut, local), kind) for cut in cuts]
    scratch = [
        pltpu.VMEM((rows, hidden), jnp.bfloat16),
        pltpu.VMEM((rows, rank.shape[1]), jnp.bfloat16),
        pltpu.VMEM((rows, local), jnp.bfloat16),
    ]
    inputs = [(x, VMEM) for x in (*parts, rank, wt, given, *before)]
    body = functools.partial(down_body, lanes, experts, total is None)
    return call(body, "down", info, inputs, weights, ahead, after, outs, scratch)


def finish(total, late, after):
    if after:
        late, *_ = lax.optimization_barrier((late, *after))
    gate_up = total + late.astype(jnp.float32)
    width = gate_up.shape[2] // 2
    return (jax.nn.silu(gate_up[:, :, :width]) * gate_up[:, :, width:]).astype(jnp.bfloat16)


def chip_sums(send, keep, bits):
    total = keep.astype(jnp.float32) + flip(send, "dp", 1).astype(jnp.float32)
    for b in bits[1:-1]:
        total = total[0::2] + flip(total[1::2].astype(jnp.bfloat16), "dp", 1 << b).astype(jnp.float32)
    return total[0::2], total[1::2].astype(jnp.bfloat16)


def everyone_s(share, other, at, bits):
    width = share.shape[2]
    top = 1 << bits[-1]
    parts = [(share, 0, [0]), (other, at, [top])]
    held, whose = jnp.concatenate([share, other[:, :, at : at + width]], axis=0), [0, top]
    for b in reversed(bits[:-1]):
        theirs = flip(held, "dp", 1 << b)
        parts.append((theirs, 0, [l | 1 << b for l in whose]))
        if b > 0:
            held, whose = jnp.concatenate([held, theirs], axis=0), whose + parts[-1][2]
    return parts


def on_device(tokens, expert_ids, scores, w_gate, w_up, w_down):
    n_owner, n_dp = lax.axis_size("expert"), lax.axis_size("dp")
    tok_rows, top = expert_ids.shape
    experts = w_gate.shape[0]
    capacity = 2 * tok_rows * top // (experts * n_owner)
    per_chunk = 2 if experts % 2 == 0 else 1
    most = n_owner * capacity
    chunks = experts // per_chunk

    meta = jnp.concatenate([expert_ids.T.astype(jnp.float32), scores.T], axis=0)
    me = lax.axis_index("dp").astype(jnp.int32)
    first = lax.axis_index("expert").astype(jnp.int32) * experts
    info = jnp.stack([first, me, backwards(me, n_dp)])
    of = lambda c: list(range(c * per_chunk, (c + 1) * per_chunk))
    weights = (w_gate, w_up, w_down)
    needs = [(of(c), side) for c in range(chunks) for side in (1, 0)] + [(of(c), None) for c in range(chunks)]
    given = {0: stage(info, weights, needs[0], [])}

    def fetched(k, outs):
        if k + 1 < len(needs):
            *outs, given[k + 1] = outs
        return outs

    ahead = lambda k: needs[k + 1] if k + 1 < len(needs) else None

    meta = lax.optimization_barrier((meta, given[0]))[0]
    metas = [meta] + [
        lax.ppermute(meta, "expert", [(i, (i - k) % n_owner) for i in range(n_owner)])
        for k in gathered_order(n_owner)[1:]
    ]
    feeds = gathered(tokens, "expert", metas)
    rank, wt = route(metas, info, experts)

    tall, wide = [feed.shape[0] for feed in feeds], tokens.shape[1]
    bits = bits_of(n_dp)
    cross = 1 << bits[-1]
    sent, parts, total = [], [], None
    share = kept = late = None

    def add(c, after):
        k, cuts = 2 * chunks + c, tall if c == chunks - 1 else [sum(tall)]
        outs = down(parts[c], rank, wt, info, given[k], weights, total, of(c), cuts, ahead(k), after)
        outs = fetched(k, outs)
        return outs if c == chunks - 1 else outs[0]

    for c in range(chunks):
        last = c == chunks - 1
        k = 2 * c
        send, rows = fetched(
            k, send_half(feeds, rank, info, given[k], weights, of(c), most, n_dp, ahead(k), sent[-1:])
        )
        k = 2 * c + 1
        (keep,) = fetched(k, keep_half(rows, info, given[k], weights, most, n_dp, ahead(k)))
        before, behind = kept, late
        kept, out = chip_sums(send, keep, bits)
        width = out.shape[2]
        if c > 0:
            share = finish(before, behind[:, :, :width], [])
            out = jnp.concatenate([out, share], axis=2)
        sent.append(out)
        late = flip(out, "dp", cross)
        if c > 0:
            parts.append(everyone_s(share, late, width, bits))
        if last:
            for d in range(min(c - 1, 2)):
                total = add(d, [out] if d == 0 else [])
    share = finish(kept, late[:, :, :width], [] if total is None else [total])
    other = flip(share, "dp", cross)
    for c in range(max(min(chunks - 2, 2), 0), chunks - 1):
        total = add(c, [share])
    if total is not None:
        other = lax.optimization_barrier((other, total))[0]
    parts.append(everyone_s(share, other, 0, bits))
    total = add(chunks - 1, [])
    return returned(total, "expert").astype(jnp.bfloat16)


def gathered_order(n):
    near = [d for s in range(1, n // 2) for d in (-s, s)]
    return [0] + near + ([n // 2] if n > 1 else [])


def gathered(x, axis, beside):
    n = lax.axis_size(axis)
    up, down_ = [(i, (i + 1) % n) for i in range(n)], [(i, (i - 1) % n) for i in range(n)]
    below = above = x
    found = [x]
    for _ in range(1, n // 2):
        below, above = lax.ppermute(below, axis, up), lax.ppermute(above, axis, down_)
        found += [below, above]
    if n > 1:
        half = x.shape[0] // 2
        below, above, *_ = lax.optimization_barrier((below, above, *beside))
        found += [lax.ppermute(below[:half], axis, up), lax.ppermute(above[half:], axis, down_)]
    return found


def returned(partials, axis):
    n = lax.axis_size(axis)
    up, down_ = [(i, (i + 1) % n) for i in range(n)], [(i, (i - 1) % n) for i in range(n)]
    wide = lambda x: x.astype(jnp.float32)
    near = {0: partials[0]}
    if n == 1:
        return wide(near[0])
    for k, partial in zip(gathered_order(n)[1:-1], partials[1:-2]):
        near[k] = partial
    half = partials[-1].shape[0]
    low, high = lax.ppermute(partials[-2], axis, down_), lax.ppermute(partials[-1], axis, up)
    halves = True
    for s in range(n // 2 - 1, 0, -1):
        a, b = wide(near[-s]), wide(near[s])
        if halves:
            a = jnp.concatenate([a[:half] + wide(low), a[half:]], axis=0)
            b = jnp.concatenate([b[:half], b[half:] + wide(high)], axis=0)
        else:
            a, b = a + wide(low), b + wide(high)
        low = lax.ppermute(a.astype(jnp.bfloat16), axis, down_)
        high = lax.ppermute(b.astype(jnp.bfloat16), axis, up)
        halves = False
    if halves:
        back = jnp.concatenate([wide(low), wide(high)], axis=0)
    else:
        back = wide(low) + wide(high)
    return wide(near[0]) + back


def solution(mesh):
    in_specs = (
        P(("groups", "expert"), "dp"),
        P(("groups", "expert"), None),
        P(("groups", "expert"), None),
        P("expert", "dp", None),
        P("expert", "dp", None),
        P("expert", None, "dp"),
    )
    out_specs = P(("groups", "expert"), "dp")
    return jax.shard_map(
        on_device, mesh=mesh, in_specs=in_specs, out_specs=out_specs, check_vma=False
    )
```

```python
import functools

import jax
import jax.numpy as jnp
from jax import lax
from jax.experimental import pallas as pl
from jax.experimental.pallas import tpu as pltpu
from jax.sharding import PartitionSpec as P

LANES = 128
VMEM = pl.BlockSpec(memory_space=pltpu.VMEM)
SMEM = pl.BlockSpec(memory_space=pltpu.SMEM)
HERE = pl.BlockSpec(memory_space=pl.ANY)
FAR = pl.BlockSpec(memory_space=pltpu.HBM)
NOWHERE = -1e6


def bits_of(n):
    return [b for b in range(n.bit_length() - 1)]


def flip(x, axis, k):
    return lax.ppermute(x, axis, [(i, i ^ k) for i in range(lax.axis_size(axis))])


def route_body(n, experts, info, *refs):
    meta, (rank, wt) = refs[:n], refs[n:]
    tok, top = meta[0].shape[1], meta[0].shape[0] // 2
    padded = rank.shape[0]
    first = info[0].astype(jnp.float32)
    e = lax.broadcasted_iota(jnp.int32, (padded, tok), 0).astype(jnp.float32)
    before = (
        lax.broadcasted_iota(jnp.int32, (tok, tok), 0) < lax.broadcasted_iota(jnp.int32, (tok, tok), 1)
    ).astype(jnp.bfloat16)
    count = jnp.zeros((padded, 1), jnp.float32)
    for s in range(n):
        ids, scores = meta[s][:top], meta[s][top:]
        affinity = 1.0 / (1.0 + jnp.exp(-scores))
        share = 2.5 * affinity / jnp.sum(affinity, axis=0, keepdims=True)
        named = jnp.zeros((padded, tok), jnp.float32)
        weight = jnp.zeros((padded, tok), jnp.float32)
        for k in range(top):
            hit = jnp.where(ids[k : k + 1] - first == e, 1.0, 0.0)
            named = named + hit
            weight = weight + hit * share[k : k + 1]
        named = jnp.where(e < experts, named, 0.0)
        place = jnp.dot(named.astype(jnp.bfloat16), before, preferred_element_type=jnp.float32) + count
        rank[:, s * tok : (s + 1) * tok] = jnp.where(named > 0, place, NOWHERE)
        wt[:, s * tok : (s + 1) * tok] = weight
        count = count + jnp.sum(named, axis=1, keepdims=True)


def route(meta, info, experts):
    tokens = len(meta) * meta[0].shape[1]
    table = jax.ShapeDtypeStruct((-(-experts // 8) * 8, tokens), jnp.float32)
    return pl.pallas_call(
        functools.partial(route_body, len(meta), experts),
        out_shape=(table, table),
        in_specs=[SMEM] + [VMEM] * len(meta),
        out_specs=(VMEM, VMEM),
        compiler_params=pltpu.CompilerParams(vmem_limit_bytes=40 << 20),
        name="route",
    )(info, *meta)


def backwards(l, n):
    bits = bits_of(n)
    return sum((((l >> b) & 1) << (len(bits) - 1 - b) for b in bits), 0 * l)


def units_of(l, info, n, width):
    return pl.ds(pl.multiple_of((backwards(l, n) ^ info[2]) * width, width), width)


def set_shape(need, weights):
    (_, depth, wide), (experts, side) = weights[0].shape, need
    return (len(experts), depth, wide) if side is None else (2, len(experts), depth, wide // 2)


def set_copies(need, weights, info, to, sem):
    experts, side = need
    if side is None:
        return [pltpu.make_async_copy(weights[0].at[e], to.at[x], sem.at[x]) for x, e in enumerate(experts)]
    half = to.shape[-1]
    units = pl.ds(pl.multiple_of(((info[1] & 1) ^ side) * half, half), half)
    return [
        pltpu.make_async_copy(w.at[e, :, units], to.at[m, x], sem.at[m * len(experts) + x])
        for m, w in enumerate(weights)
        for x, e in enumerate(experts)
    ]


def call(body, name, info, inputs, weights, ahead, after, outs, scratch, limit=24):
    n_in, n_out = len(inputs), len(outs)
    outs = list(outs)
    weights = [] if ahead is None else weights[2:] if ahead[1] is None else weights[:2]
    if ahead is not None:
        outs.append(jax.ShapeDtypeStruct(set_shape(ahead, weights), jnp.bfloat16))
        scratch = scratch + [pltpu.SemaphoreType.DMA((2 * len(ahead[0]),))]

    def whole(info, *refs):
        own, far = refs[:n_in], refs[n_in : n_in + len(weights)]
        rest = refs[n_in + len(weights) + len(after) :]
        results, rest = rest[: len(outs)], rest[len(outs) :]
        on = []
        if ahead is not None:
            on = set_copies(ahead, far, info, results[-1], rest[-1])
            rest = rest[:-1]
        body(info, own, results[:n_out], rest, lambda: [copy.start() for copy in on])
        for copy in on:
            copy.wait()

    return pl.pallas_call(
        whole,
        out_shape=tuple(outs),
        in_specs=[SMEM] + [spec for _, spec in inputs] + [HERE] * (len(weights) + len(after)),
        out_specs=(VMEM,) * len(outs),
        scratch_shapes=scratch,
        compiler_params=pltpu.CompilerParams(vmem_limit_bytes=limit << 20),
        cost_estimate=pl.CostEstimate(flops=1, bytes_accessed=1, transcendentals=0),
        name=name,
    )(info, *[x for x, _ in inputs], *weights, *after)


def stage(info, weights, need, after):
    body = lambda info, own, outs, rest, fetch: fetch()
    return call(body, "stage", info, [], weights, need, after, [], [], 40)[0]


def products(rows, given, to, info):
    most = rows.shape[0] // given.shape[1]
    shares, width = to.shape[0], to.shape[2] // 2
    for m in range(2):
        for x in range(given.shape[1]):
            mine = slice(x * most, (x + 1) * most)
            part = jnp.dot(rows[mine], given[m, x], preferred_element_type=jnp.float32)
            part = part.astype(jnp.bfloat16)
            for q in range(shares):
                j = backwards(q, shares) ^ (info[1] >> 1)
                to[j, mine, m * width : (m + 1) * width] = part[:, q * width : (q + 1) * width]


def send_body(experts, info, own, outs, rest, fetch):
    sources, rank, given = own[:-2], own[-2], own[-1]
    (to, rows), (feed, feed_sem) = outs, rest
    at, feeds = 0, []
    for s, source in enumerate(sources):
        tok = source.shape[0]
        feeds.append(pltpu.make_async_copy(source, feed.at[pl.ds(at, tok)], feed_sem.at[s]))
        at += tok
    for copy in feeds:
        copy.start()
    fetch()
    most = rows.shape[0] // len(experts)
    r = lax.broadcasted_iota(jnp.int32, (most, at), 0).astype(jnp.float32)
    pick = jnp.concatenate(
        [jnp.where(r == rank[e : e + 1, :], 1.0, 0.0).astype(jnp.bfloat16) for e in experts], axis=0
    )
    for copy in feeds:
        copy.wait()
    rows[...] = jnp.dot(pick, feed[...], preferred_element_type=jnp.float32).astype(jnp.bfloat16)
    products(rows, given, to, info)


def keep_body(info, own, outs, rest, fetch):
    fetch()
    rows, given = own
    products(rows, given, outs[0], info)


def part_shape(given, most, n_dp):
    _, experts, _, half = given.shape
    return jax.ShapeDtypeStruct((n_dp // 2, most * experts, 4 * half // n_dp), jnp.bfloat16)


def send_half(feeds, rank, info, given, weights, experts, most, n_dp, ahead, after):
    local = given.shape[2]
    rows = jax.ShapeDtypeStruct((most * len(experts), local), jnp.bfloat16)
    scratch = [
        pltpu.VMEM((rank.shape[1], local), jnp.bfloat16),
        pltpu.SemaphoreType.DMA((len(feeds),)),
    ]
    inputs = [(feed, HERE) for feed in feeds] + [(rank, VMEM), (given, VMEM)]
    outs = [part_shape(given, most, n_dp), rows]
    body = functools.partial(send_body, experts)
    return call(body, "send_half", info, inputs, weights, ahead, after, outs, scratch)


def keep_half(rows, info, given, weights, most, n_dp, ahead):
    inputs = [(rows, VMEM), (given, VMEM)]
    outs = [part_shape(given, most, n_dp)]
    return call(keep_body, "keep_half", info, inputs, weights, ahead, [], outs, [])


def down_body(lanes, experts, first, info, own, outs, rest, fetch):
    fetch()
    parts, (rank, wt, given) = own[: len(lanes)], own[len(lanes) : len(lanes) + 3]
    before = None if first else own[-1]
    hidden, mix, out = rest
    most = hidden.shape[0] // len(experts)
    width = parts[0].shape[-1]
    n_dp = hidden.shape[1] // width
    for part, (at, shares) in zip(parts, lanes):
        for j, l in enumerate(shares):
            hidden[:, units_of(l, info, n_dp, width)] = part[j, :, at : at + width]
    r = lax.broadcasted_iota(jnp.int32, (most, mix.shape[1]), 0).astype(jnp.float32)
    for x, e in enumerate(experts):
        mix[x * most : (x + 1) * most, :] = jnp.where(
            r == rank[e : e + 1, :], wt[e : e + 1, :], 0.0
        ).astype(jnp.bfloat16)
    local = out.shape[1]
    block = 512 if local % 512 == 0 else 256 if local % 256 == 0 else local
    for i in range(local // block):
        cols = slice(i * block, (i + 1) * block)
        for x in range(len(experts)):
            mine = slice(x * most, (x + 1) * most)
            out[mine, cols] = jnp.dot(
                hidden[mine], given[x, :, cols], preferred_element_type=jnp.float32
            ).astype(jnp.bfloat16)
        total = lax.dot_general(
            mix[...], out[:, cols], (((0,), (0,)), ((), ())), preferred_element_type=jnp.float32
        )
        if not first:
            total = total + before[:, cols]
        at = 0
        for to in outs:
            to[:, cols] = total[at : at + to.shape[0]].astype(to.dtype)
            at += to.shape[0]


def down(parts, rank, wt, info, given, weights, total, experts, cuts, ahead, after):
    parts, lanes = [part for part, *_ in parts], [tuple(where) for _, *where in parts]
    rows = parts[0].shape[1]
    _, hidden, local = given.shape
    kind = jnp.bfloat16 if len(cuts) > 1 else jnp.float32
    before = [] if total is None else [total]
    outs = [jax.ShapeDtypeStruct((cut, local), kind) for cut in cuts]
    scratch = [
        pltpu.VMEM((rows, hidden), jnp.bfloat16),
        pltpu.VMEM((rows, rank.shape[1]), jnp.bfloat16),
        pltpu.VMEM((rows, local), jnp.bfloat16),
    ]
    inputs = [(x, VMEM) for x in (*parts, rank, wt, given, *before)]
    body = functools.partial(down_body, lanes, experts, total is None)
    return call(body, "down", info, inputs, weights, ahead, after, outs, scratch)


def finish(total, late, after):
    if after:
        late, *_ = lax.optimization_barrier((late, *after))
    gate_up = total + late.astype(jnp.float32)
    width = gate_up.shape[2] // 2
    return (jax.nn.silu(gate_up[:, :, :width]) * gate_up[:, :, width:]).astype(jnp.bfloat16)


def chip_sums(send, keep, bits):
    total = keep.astype(jnp.float32) + flip(send, "dp", 1).astype(jnp.float32)
    for b in bits[1:-1]:
        total = total[0::2] + flip(total[1::2].astype(jnp.bfloat16), "dp", 1 << b).astype(jnp.float32)
    return total[0::2], total[1::2].astype(jnp.bfloat16)


def everyone_s(share, other, at, bits):
    width = share.shape[2]
    top = 1 << bits[-1]
    parts = [(share, 0, [0]), (other, at, [top])]
    held, whose = jnp.concatenate([share, other[:, :, at : at + width]], axis=0), [0, top]
    for b in reversed(bits[:-1]):
        theirs = flip(held, "dp", 1 << b)
        parts.append((theirs, 0, [l | 1 << b for l in whose]))
        if b > 0:
            held, whose = jnp.concatenate([held, theirs], axis=0), whose + parts[-1][2]
    return parts


def on_device(tokens, expert_ids, scores, w_gate, w_up, w_down):
    n_owner, n_dp = lax.axis_size("expert"), lax.axis_size("dp")
    tok_rows, top = expert_ids.shape
    experts = w_gate.shape[0]
    capacity = 2 * tok_rows * top // (experts * n_owner)
    per_chunk = 2 if experts % 2 == 0 else 1
    most = n_owner * capacity
    chunks = experts // per_chunk

    meta = jnp.concatenate([expert_ids.T.astype(jnp.float32), scores.T], axis=0)
    me = lax.axis_index("dp").astype(jnp.int32)
    first = lax.axis_index("expert").astype(jnp.int32) * experts
    info = jnp.stack([first, me, backwards(me, n_dp)])
    of = lambda c: list(range(c * per_chunk, (c + 1) * per_chunk))
    weights = (w_gate, w_up, w_down)
    needs = [(of(c), side) for c in range(chunks) for side in (1, 0)] + [(of(c), None) for c in range(chunks)]
    given = {0: stage(info, weights, needs[0], [])}

    def fetched(k, outs):
        if k + 1 < len(needs):
            *outs, given[k + 1] = outs
        return outs

    ahead = lambda k: needs[k + 1] if k + 1 < len(needs) else None

    metas = [meta] + [
        lax.ppermute(meta, "expert", [(i, (i - k) % n_owner) for i in range(n_owner)])
        for k in gathered_order(n_owner)[1:]
    ]
    feeds = gathered(tokens, "expert")
    rank, wt = route(metas, info, experts)

    tall, wide = [feed.shape[0] for feed in feeds], tokens.shape[1]
    bits = bits_of(n_dp)
    cross = 1 << bits[-1]
    sent, parts, total = [], [], None
    share = kept = late = None

    def add(c, after):
        k, cuts = 2 * chunks + c, tall if c == chunks - 1 else [sum(tall)]
        outs = down(parts[c], rank, wt, info, given[k], weights, total, of(c), cuts, ahead(k), after)
        outs = fetched(k, outs)
        return outs if c == chunks - 1 else outs[0]

    for c in range(chunks):
        last = c == chunks - 1
        k = 2 * c
        send, rows = fetched(
            k, send_half(feeds, rank, info, given[k], weights, of(c), most, n_dp, ahead(k), sent[-1:])
        )
        k = 2 * c + 1
        (keep,) = fetched(k, keep_half(rows, info, given[k], weights, most, n_dp, ahead(k)))
        before, behind = kept, late
        kept, out = chip_sums(send, keep, bits)
        width = out.shape[2]
        if c > 0:
            share = finish(before, behind[:, :, :width], [])
            out = jnp.concatenate([out, share], axis=2)
        sent.append(out)
        late = flip(out, "dp", cross)
        if c > 0:
            parts.append(everyone_s(share, late, width, bits))
        if last:
            for d in range(min(c - 1, 2)):
                total = add(d, [out] if d == 0 else [])
    share = finish(kept, late[:, :, :width], [] if total is None else [total])
    other = flip(share, "dp", cross)
    for c in range(max(min(chunks - 2, 2), 0), chunks - 1):
        total = add(c, [share])
    if total is not None:
        other = lax.optimization_barrier((other, total))[0]
    parts.append(everyone_s(share, other, 0, bits))
    total = add(chunks - 1, [])
    return returned(total, "expert").astype(jnp.bfloat16)


def gathered_order(n):
    near = [d for s in range(1, n // 2) for d in (-s, s)]
    return [0] + near + ([n // 2] if n > 1 else [])


def gathered(x, axis):
    n = lax.axis_size(axis)
    up, down_ = [(i, (i + 1) % n) for i in range(n)], [(i, (i - 1) % n) for i in range(n)]
    below = above = x
    found = [x]
    for _ in range(1, n // 2):
        below, above = lax.ppermute(below, axis, up), lax.ppermute(above, axis, down_)
        found += [below, above]
    if n > 1:
        half = x.shape[0] // 2
        found += [lax.ppermute(below[:half], axis, up), lax.ppermute(above[half:], axis, down_)]
    return found


def returned(partials, axis):
    n = lax.axis_size(axis)
    up, down_ = [(i, (i + 1) % n) for i in range(n)], [(i, (i - 1) % n) for i in range(n)]
    wide = lambda x: x.astype(jnp.float32)
    near = {0: partials[0]}
    if n == 1:
        return wide(near[0])
    for k, partial in zip(gathered_order(n)[1:-1], partials[1:-2]):
        near[k] = partial
    half = partials[-1].shape[0]
    low, high = lax.ppermute(partials[-2], axis, down_), lax.ppermute(partials[-1], axis, up)
    halves = True
    for s in range(n // 2 - 1, 0, -1):
        a, b = wide(near[-s]), wide(near[s])
        if halves:
            a = jnp.concatenate([a[:half] + wide(low), a[half:]], axis=0)
            b = jnp.concatenate([b[:half], b[half:] + wide(high)], axis=0)
        else:
            a, b = a + wide(low), b + wide(high)
        low = lax.ppermute(a.astype(jnp.bfloat16), axis, down_)
        high = lax.ppermute(b.astype(jnp.bfloat16), axis, up)
        halves = False
    if halves:
        back = jnp.concatenate([wide(low), wide(high)], axis=0)
    else:
        back = wide(low) + wide(high)
    return wide(near[0]) + back


def solution(mesh):
    in_specs = (
        P(("groups", "expert"), "dp"),
        P(("groups", "expert"), None),
        P(("groups", "expert"), None),
        P("expert", "dp", None),
        P("expert", "dp", None),
        P("expert", None, "dp"),
    )
    out_specs = P(("groups", "expert"), "dp")
    return jax.shard_map(
        on_device, mesh=mesh, in_specs=in_specs, out_specs=out_specs, check_vma=False
    )
```

```python
import functools

import jax
import jax.numpy as jnp
from jax import lax
from jax.experimental import pallas as pl
from jax.experimental.pallas import tpu as pltpu
from jax.sharding import PartitionSpec as P

LANES = 128
VMEM = pl.BlockSpec(memory_space=pltpu.VMEM)
SMEM = pl.BlockSpec(memory_space=pltpu.SMEM)
HERE = pl.BlockSpec(memory_space=pl.ANY)
FAR = pl.BlockSpec(memory_space=pltpu.HBM)
NOWHERE = -1e6


def bits_of(n):
    return [b for b in range(n.bit_length() - 1)]


def flip(x, axis, k):
    return lax.ppermute(x, axis, [(i, i ^ k) for i in range(lax.axis_size(axis))])


def route_body(n, experts, info, *refs):
    meta, (rank, wt) = refs[:n], refs[n:]
    tok, top = meta[0].shape[1], meta[0].shape[0] // 2
    padded = rank.shape[0]
    first = info[0].astype(jnp.float32)
    e = lax.broadcasted_iota(jnp.int32, (padded, tok), 0).astype(jnp.float32)
    before = (
        lax.broadcasted_iota(jnp.int32, (tok, tok), 0) < lax.broadcasted_iota(jnp.int32, (tok, tok), 1)
    ).astype(jnp.bfloat16)
    count = jnp.zeros((padded, 1), jnp.float32)
    for s in range(n):
        ids, scores = meta[s][:top], meta[s][top:]
        affinity = 1.0 / (1.0 + jnp.exp(-scores))
        share = 2.5 * affinity / jnp.sum(affinity, axis=0, keepdims=True)
        named = jnp.zeros((padded, tok), jnp.float32)
        weight = jnp.zeros((padded, tok), jnp.float32)
        for k in range(top):
            hit = jnp.where(ids[k : k + 1] - first == e, 1.0, 0.0)
            named = named + hit
            weight = weight + hit * share[k : k + 1]
        named = jnp.where(e < experts, named, 0.0)
        place = jnp.dot(named.astype(jnp.bfloat16), before, preferred_element_type=jnp.float32) + count
        rank[:, s * tok : (s + 1) * tok] = jnp.where(named > 0, place, NOWHERE)
        wt[:, s * tok : (s + 1) * tok] = weight
        count = count + jnp.sum(named, axis=1, keepdims=True)


def route(meta, info, experts):
    tokens = len(meta) * meta[0].shape[1]
    table = jax.ShapeDtypeStruct((-(-experts // 8) * 8, tokens), jnp.float32)
    return pl.pallas_call(
        functools.partial(route_body, len(meta), experts),
        out_shape=(table, table),
        in_specs=[SMEM] + [VMEM] * len(meta),
        out_specs=(VMEM, VMEM),
        compiler_params=pltpu.CompilerParams(vmem_limit_bytes=40 << 20),
        name="route",
    )(info, *meta)


def backwards(l, n):
    bits = bits_of(n)
    return sum((((l >> b) & 1) << (len(bits) - 1 - b) for b in bits), 0 * l)


def units_of(l, info, n, width):
    return pl.ds(pl.multiple_of((backwards(l, n) ^ info[2]) * width, width), width)


def set_shape(need, weights):
    (_, depth, wide), (experts, side) = weights[0].shape, need
    return (len(experts), depth, wide) if side is None else (2, len(experts), depth, wide // 2)


def set_copies(need, weights, info, to, sem):
    experts, side = need
    if side is None:
        return [pltpu.make_async_copy(weights[0].at[e], to.at[x], sem.at[x]) for x, e in enumerate(experts)]
    half = to.shape[-1]
    units = pl.ds(pl.multiple_of(((info[1] & 1) ^ side) * half, half), half)
    return [
        pltpu.make_async_copy(w.at[e, :, units], to.at[m, x], sem.at[m * len(experts) + x])
        for m, w in enumerate(weights)
        for x, e in enumerate(experts)
    ]


def call(body, name, info, inputs, weights, ahead, after, outs, scratch, limit=24):
    n_in, n_out = len(inputs), len(outs)
    outs = list(outs)
    weights = [] if ahead is None else weights[2:] if ahead[1] is None else weights[:2]
    if ahead is not None:
        outs.append(jax.ShapeDtypeStruct(set_shape(ahead, weights), jnp.bfloat16))
        scratch = scratch + [pltpu.SemaphoreType.DMA((2 * len(ahead[0]),))]

    def whole(info, *refs):
        own, far = refs[:n_in], refs[n_in : n_in + len(weights)]
        rest = refs[n_in + len(weights) + len(after) :]
        results, rest = rest[: len(outs)], rest[len(outs) :]
        on = []
        if ahead is not None:
            on = set_copies(ahead, far, info, results[-1], rest[-1])
            rest = rest[:-1]
        body(info, own, results[:n_out], rest, lambda: [copy.start() for copy in on])
        for copy in on:
            copy.wait()

    return pl.pallas_call(
        whole,
        out_shape=tuple(outs),
        in_specs=[SMEM] + [spec for _, spec in inputs] + [HERE] * (len(weights) + len(after)),
        out_specs=(VMEM,) * len(outs),
        scratch_shapes=scratch,
        compiler_params=pltpu.CompilerParams(vmem_limit_bytes=limit << 20),
        cost_estimate=pl.CostEstimate(flops=1, bytes_accessed=1, transcendentals=0),
        name=name,
    )(info, *[x for x, _ in inputs], *weights, *after)


def stage(info, weights, need, after):
    body = lambda info, own, outs, rest, fetch: fetch()
    return call(body, "stage", info, [], weights, need, after, [], [], 40)[0]


def products(rows, given, to, info):
    most = rows.shape[0] // given.shape[1]
    shares, width = to.shape[0], to.shape[2] // 2
    for m in range(2):
        for x in range(given.shape[1]):
            mine = slice(x * most, (x + 1) * most)
            part = jnp.dot(rows[mine], given[m, x], preferred_element_type=jnp.float32)
            part = part.astype(jnp.bfloat16)
            for q in range(shares):
                j = backwards(q, shares) ^ (info[1] >> 1)
                to[j, mine, m * width : (m + 1) * width] = part[:, q * width : (q + 1) * width]


def send_body(experts, info, own, outs, rest, fetch):
    sources, rank, given = own[:-2], own[-2], own[-1]
    (to, rows), (feed, feed_sem) = outs, rest
    at, feeds = 0, []
    for s, source in enumerate(sources):
        tok = source.shape[0]
        feeds.append(pltpu.make_async_copy(source, feed.at[pl.ds(at, tok)], feed_sem.at[s]))
        at += tok
    for copy in feeds:
        copy.start()
    fetch()
    most = rows.shape[0] // len(experts)
    r = lax.broadcasted_iota(jnp.int32, (most, at), 0).astype(jnp.float32)
    pick = jnp.concatenate(
        [jnp.where(r == rank[e : e + 1, :], 1.0, 0.0).astype(jnp.bfloat16) for e in experts], axis=0
    )
    for copy in feeds:
        copy.wait()
    rows[...] = jnp.dot(pick, feed[...], preferred_element_type=jnp.float32).astype(jnp.bfloat16)
    products(rows, given, to, info)


def keep_body(info, own, outs, rest, fetch):
    fetch()
    rows, given = own
    products(rows, given, outs[0], info)


def part_shape(given, most, n_dp):
    _, experts, _, half = given.shape
    return jax.ShapeDtypeStruct((n_dp // 2, most * experts, 4 * half // n_dp), jnp.bfloat16)


def send_half(feeds, rank, info, given, weights, experts, most, n_dp, ahead, after):
    local = given.shape[2]
    rows = jax.ShapeDtypeStruct((most * len(experts), local), jnp.bfloat16)
    scratch = [
        pltpu.VMEM((rank.shape[1], local), jnp.bfloat16),
        pltpu.SemaphoreType.DMA((len(feeds),)),
    ]
    inputs = [(feed, HERE) for feed in feeds] + [(rank, VMEM), (given, VMEM)]
    outs = [part_shape(given, most, n_dp), rows]
    body = functools.partial(send_body, experts)
    return call(body, "send_half", info, inputs, weights, ahead, after, outs, scratch)


def keep_half(rows, info, given, weights, most, n_dp, ahead):
    inputs = [(rows, VMEM), (given, VMEM)]
    outs = [part_shape(given, most, n_dp)]
    return call(keep_body, "keep_half", info, inputs, weights, ahead, [], outs, [])


def down_body(lanes, experts, first, info, own, outs, rest, fetch):
    fetch()
    parts, (rank, wt, given) = own[: len(lanes)], own[len(lanes) : len(lanes) + 3]
    before = None if first else own[-1]
    hidden, mix, out = rest
    most = hidden.shape[0] // len(experts)
    width = parts[0].shape[-1]
    n_dp = hidden.shape[1] // width
    for part, (at, shares) in zip(parts, lanes):
        for j, l in enumerate(shares):
            hidden[:, units_of(l, info, n_dp, width)] = part[j, :, at : at + width]
    r = lax.broadcasted_iota(jnp.int32, (most, mix.shape[1]), 0).astype(jnp.float32)
    for x, e in enumerate(experts):
        mix[x * most : (x + 1) * most, :] = jnp.where(
            r == rank[e : e + 1, :], wt[e : e + 1, :], 0.0
        ).astype(jnp.bfloat16)
    local = out.shape[1]
    block = 512 if local % 512 == 0 else 256 if local % 256 == 0 else local
    for i in range(local // block):
        cols = slice(i * block, (i + 1) * block)
        for x in range(len(experts)):
            mine = slice(x * most, (x + 1) * most)
            out[mine, cols] = jnp.dot(
                hidden[mine], given[x, :, cols], preferred_element_type=jnp.float32
            ).astype(jnp.bfloat16)
        total = lax.dot_general(
            mix[...], out[:, cols], (((0,), (0,)), ((), ())), preferred_element_type=jnp.float32
        )
        if not first:
            total = total + before[:, cols]
        at = 0
        for to in outs:
            to[:, cols] = total[at : at + to.shape[0]].astype(to.dtype)
            at += to.shape[0]


def down(parts, rank, wt, info, given, weights, total, experts, cuts, ahead, after):
    parts, lanes = [part for part, *_ in parts], [tuple(where) for _, *where in parts]
    rows = parts[0].shape[1]
    _, hidden, local = given.shape
    kind = jnp.bfloat16 if len(cuts) > 1 else jnp.float32
    before = [] if total is None else [total]
    outs = [jax.ShapeDtypeStruct((cut, local), kind) for cut in cuts]
    scratch = [
        pltpu.VMEM((rows, hidden), jnp.bfloat16),
        pltpu.VMEM((rows, rank.shape[1]), jnp.bfloat16),
        pltpu.VMEM((rows, local), jnp.bfloat16),
    ]
    inputs = [(x, VMEM) for x in (*parts, rank, wt, given, *before)]
    body = functools.partial(down_body, lanes, experts, total is None)
    return call(body, "down", info, inputs, weights, ahead, after, outs, scratch)


def finish(total, late, after):
    if after:
        late, *_ = lax.optimization_barrier((late, *after))
    gate_up = total + late.astype(jnp.float32)
    width = gate_up.shape[2] // 2
    return (jax.nn.silu(gate_up[:, :, :width]) * gate_up[:, :, width:]).astype(jnp.bfloat16)


def chip_sums(send, keep, bits):
    total = keep.astype(jnp.float32) + flip(send, "dp", 1).astype(jnp.float32)
    for b in bits[1:-1]:
        total = total[0::2] + flip(total[1::2].astype(jnp.bfloat16), "dp", 1 << b).astype(jnp.float32)
    return total[0::2], total[1::2].astype(jnp.bfloat16)


def everyone_s(share, other, at, bits):
    width = share.shape[2]
    top = 1 << bits[-1]
    parts = [(share, 0, [0]), (other, at, [top])]
    held, whose = jnp.concatenate([share, other[:, :, at : at + width]], axis=0), [0, top]
    for b in reversed(bits[:-1]):
        theirs = flip(held, "dp", 1 << b)
        parts.append((theirs, 0, [l | 1 << b for l in whose]))
        if b > 0:
            held, whose = jnp.concatenate([held, theirs], axis=0), whose + parts[-1][2]
    return parts


def on_device(tokens, expert_ids, scores, w_gate, w_up, w_down):
    n_owner, n_dp = lax.axis_size("expert"), lax.axis_size("dp")
    tok_rows, top = expert_ids.shape
    experts = w_gate.shape[0]
    capacity = 2 * tok_rows * top // (experts * n_owner)
    per_chunk = 2 if experts % 2 == 0 else 1
    most = n_owner * capacity
    chunks = experts // per_chunk

    meta = jnp.concatenate([expert_ids.T.astype(jnp.float32), scores.T], axis=0)
    me = lax.axis_index("dp").astype(jnp.int32)
    first = lax.axis_index("expert").astype(jnp.int32) * experts
    info = jnp.stack([first, me, backwards(me, n_dp)])
    of = lambda c: list(range(c * per_chunk, (c + 1) * per_chunk))
    weights = (w_gate, w_up, w_down)
    needs = [(of(c), side) for c in range(chunks) for side in (1, 0)] + [(of(c), None) for c in range(chunks)]
    given = {0: stage(info, weights, needs[0], [])}

    def fetched(k, outs):
        if k + 1 < len(needs):
            *outs, given[k + 1] = outs
        return outs

    ahead = lambda k: needs[k + 1] if k + 1 < len(needs) else None

    metas = [meta] + [
        lax.ppermute(meta, "expert", [(i, (i - k) % n_owner) for i in range(n_owner)])
        for k in gathered_order(n_owner)[1:]
    ]
    feeds = gathered(tokens, "expert")
    rank, wt = route(metas, info, experts)

    tall, wide = [feed.shape[0] for feed in feeds], tokens.shape[1]
    bits = bits_of(n_dp)
    cross = 1 << bits[-1]
    sent, parts, total = [], [], None
    share = kept = late = None

    def add(c, after):
        k, cuts = 2 * chunks + c, tall if c == chunks - 1 else [sum(tall)]
        outs = down(parts[c], rank, wt, info, given[k], weights, total, of(c), cuts, ahead(k), after)
        outs = fetched(k, outs)
        return outs if c == chunks - 1 else outs[0]

    for c in range(chunks):
        last = c == chunks - 1
        k = 2 * c
        send, rows = fetched(
            k, send_half(feeds, rank, info, given[k], weights, of(c), most, n_dp, ahead(k), sent[-1:])
        )
        k = 2 * c + 1
        (keep,) = fetched(k, keep_half(rows, info, given[k], weights, most, n_dp, ahead(k)))
        before, behind = kept, late
        kept, out = chip_sums(send, keep, bits)
        width = out.shape[2]
        if c > 0:
            share = finish(before, behind[:, :, :width], [])
            out = jnp.concatenate([out, share], axis=2)
        sent.append(out)
        late = flip(out, "dp", cross)
        if c > 0:
            parts.append(everyone_s(share, late, width, bits))
        if last:
            for d in range(min(c - 1, 2)):
                total = add(d, [out] if d == 0 else [])
    share = finish(kept, late[:, :, :width], [] if total is None else [total])
    other = flip(share, "dp", cross)
    for c in range(max(min(chunks - 2, 2), 0), chunks - 1):
        total = add(c, [share])
    if total is not None:
        other = lax.optimization_barrier((other, total))[0]
    parts.append(everyone_s(share, other, 0, bits))
    total = add(chunks - 1, [])
    return returned(total, "expert").astype(jnp.bfloat16)


def gathered_order(n):
    near = [d for s in range(1, n // 2) for d in (-s, s)]
    return [0] + near + ([n // 2] if n > 1 else [])


def ways(n):
    return [(i, (i + 1) % n) for i in range(n)], [(i, (i - 1) % n) for i in range(n)]


def gathered(x, axis):
    n = lax.axis_size(axis)
    up, down_ = ways(n)
    half = x.shape[0] // 2
    below = above = [x[:half], x[half:]]
    found = [x]
    for _ in range(1, n // 2):
        far_up, far_down = lax.ppermute(below[0], axis, up), lax.ppermute(above[1], axis, down_)
        below = [far_up, lax.ppermute(below[1], axis, up)]
        above = [lax.ppermute(above[0], axis, down_), far_down]
        found += below + above
    if n > 1:
        found += [lax.ppermute(below[0], axis, up), lax.ppermute(above[1], axis, down_)]
    return found


def returned(partials, axis):
    n = lax.axis_size(axis)
    up, down_ = ways(n)
    wide = lambda x: x.astype(jnp.float32)
    mixed = wide(partials[0])
    if n == 1:
        return mixed
    half = mixed.shape[0] // 2

    def hop(there, partial, perm):
        total = partial if there is None else (wide(partial) + wide(there)).astype(jnp.bfloat16)
        return lax.ppermute(total, axis, perm)

    low = [hop(None, partials[-2], down_), None]
    high = [None, hop(None, partials[-1], up)]
    for s in range(n // 2 - 1, 0, -1):
        near = partials[4 * s - 3 : 4 * s + 1]
        low = [hop(low[0], near[0], down_), hop(low[1], near[1], down_)]
        high = [hop(high[0], near[2], up), hop(high[1], near[3], up)]
    halves = []
    for h, own in enumerate((mixed[:half], mixed[half:])):
        for there in (low[h], high[h]):
            own = own if there is None else own + wide(there)
        halves.append(own)
    return jnp.concatenate(halves, axis=0)


def solution(mesh):
    in_specs = (
        P(("groups", "expert"), "dp"),
        P(("groups", "expert"), None),
        P(("groups", "expert"), None),
        P("expert", "dp", None),
        P("expert", "dp", None),
        P("expert", None, "dp"),
    )
    out_specs = P(("groups", "expert"), "dp")
    return jax.shard_map(
        on_device, mesh=mesh, in_specs=in_specs, out_specs=out_specs, check_vma=False
    )
```

```python
import functools

import jax
import jax.numpy as jnp
from jax import lax
from jax.experimental import pallas as pl
from jax.experimental.pallas import tpu as pltpu
from jax.sharding import PartitionSpec as P

LANES = 128
VMEM = pl.BlockSpec(memory_space=pltpu.VMEM)
SMEM = pl.BlockSpec(memory_space=pltpu.SMEM)
HERE = pl.BlockSpec(memory_space=pl.ANY)
FAR = pl.BlockSpec(memory_space=pltpu.HBM)
NOWHERE = -1e6


def bits_of(n):
    return [b for b in range(n.bit_length() - 1)]


def flip(x, axis, k):
    return lax.ppermute(x, axis, [(i, i ^ k) for i in range(lax.axis_size(axis))])


def route_body(n, experts, info, *refs):
    meta, (rank, wt) = refs[:n], refs[n:]
    tok, top = meta[0].shape[1], meta[0].shape[0] // 2
    padded = rank.shape[0]
    first = info[0].astype(jnp.float32)
    e = lax.broadcasted_iota(jnp.int32, (padded, tok), 0).astype(jnp.float32)
    before = (
        lax.broadcasted_iota(jnp.int32, (tok, tok), 0) < lax.broadcasted_iota(jnp.int32, (tok, tok), 1)
    ).astype(jnp.bfloat16)
    count = jnp.zeros((padded, 1), jnp.float32)
    for s in range(n):
        ids, scores = meta[s][:top], meta[s][top:]
        affinity = 1.0 / (1.0 + jnp.exp(-scores))
        share = 2.5 * affinity / jnp.sum(affinity, axis=0, keepdims=True)
        named = jnp.zeros((padded, tok), jnp.float32)
        weight = jnp.zeros((padded, tok), jnp.float32)
        for k in range(top):
            hit = jnp.where(ids[k : k + 1] - first == e, 1.0, 0.0)
            named = named + hit
            weight = weight + hit * share[k : k + 1]
        named = jnp.where(e < experts, named, 0.0)
        place = jnp.dot(named.astype(jnp.bfloat16), before, preferred_element_type=jnp.float32) + count
        rank[:, s * tok : (s + 1) * tok] = jnp.where(named > 0, place, NOWHERE)
        wt[:, s * tok : (s + 1) * tok] = weight
        count = count + jnp.sum(named, axis=1, keepdims=True)


def route(meta, info, experts):
    tokens = len(meta) * meta[0].shape[1]
    table = jax.ShapeDtypeStruct((-(-experts // 8) * 8, tokens), jnp.float32)
    return pl.pallas_call(
        functools.partial(route_body, len(meta), experts),
        out_shape=(table, table),
        in_specs=[SMEM] + [VMEM] * len(meta),
        out_specs=(VMEM, VMEM),
        compiler_params=pltpu.CompilerParams(vmem_limit_bytes=40 << 20),
        name="route",
    )(info, *meta)


def backwards(l, n):
    bits = bits_of(n)
    return sum((((l >> b) & 1) << (len(bits) - 1 - b) for b in bits), 0 * l)


def units_of(l, info, n, width):
    return pl.ds(pl.multiple_of((backwards(l, n) ^ info[2]) * width, width), width)


def set_shape(need, weights):
    (_, depth, wide), (experts, side) = weights[0].shape, need
    return (len(experts), depth, wide) if side is None else (2, len(experts), depth, wide // 2)


def set_copies(need, weights, info, to, sem):
    experts, side = need
    if side is None:
        return [pltpu.make_async_copy(weights[0].at[e], to.at[x], sem.at[x]) for x, e in enumerate(experts)]
    half = to.shape[-1]
    units = pl.ds(pl.multiple_of(((info[1] & 1) ^ side) * half, half), half)
    return [
        pltpu.make_async_copy(w.at[e, :, units], to.at[m, x], sem.at[m * len(experts) + x])
        for m, w in enumerate(weights)
        for x, e in enumerate(experts)
    ]


def call(body, name, info, inputs, weights, ahead, after, outs, scratch, limit=24):
    n_in, n_out = len(inputs), len(outs)
    outs = list(outs)
    weights = [] if ahead is None else weights[2:] if ahead[1] is None else weights[:2]
    if ahead is not None:
        outs.append(jax.ShapeDtypeStruct(set_shape(ahead, weights), jnp.bfloat16))
        scratch = scratch + [pltpu.SemaphoreType.DMA((2 * len(ahead[0]),))]

    def whole(info, *refs):
        own, far = refs[:n_in], refs[n_in : n_in + len(weights)]
        rest = refs[n_in + len(weights) + len(after) :]
        results, rest = rest[: len(outs)], rest[len(outs) :]
        on = []
        if ahead is not None:
            on = set_copies(ahead, far, info, results[-1], rest[-1])
            rest = rest[:-1]
        body(info, own, results[:n_out], rest, lambda: [copy.start() for copy in on])
        for copy in on:
            copy.wait()

    return pl.pallas_call(
        whole,
        out_shape=tuple(outs),
        in_specs=[SMEM] + [spec for _, spec in inputs] + [HERE] * (len(weights) + len(after)),
        out_specs=(VMEM,) * len(outs),
        scratch_shapes=scratch,
        compiler_params=pltpu.CompilerParams(vmem_limit_bytes=limit << 20),
        cost_estimate=pl.CostEstimate(flops=1, bytes_accessed=1, transcendentals=0),
        name=name,
    )(info, *[x for x, _ in inputs], *weights, *after)


def stage(info, weights, need, after):
    body = lambda info, own, outs, rest, fetch: fetch()
    return call(body, "stage", info, [], weights, need, after, [], [], 40)[0]


def products(rows, given, to, info):
    most = rows.shape[0] // given.shape[1]
    shares, width = to.shape[0], to.shape[2] // 2
    for m in range(2):
        for x in range(given.shape[1]):
            mine = slice(x * most, (x + 1) * most)
            part = jnp.dot(rows[mine], given[m, x], preferred_element_type=jnp.float32)
            part = part.astype(jnp.bfloat16)
            for q in range(shares):
                j = backwards(q, shares) ^ (info[1] >> 1)
                to[j, mine, m * width : (m + 1) * width] = part[:, q * width : (q + 1) * width]


def send_body(experts, info, own, outs, rest, fetch):
    sources, rank, given = own[:-2], own[-2], own[-1]
    (to, rows), (feed, feed_sem) = outs, rest
    at, feeds = 0, []
    for s, source in enumerate(sources):
        tok = source.shape[0]
        feeds.append(pltpu.make_async_copy(source, feed.at[pl.ds(at, tok)], feed_sem.at[s]))
        at += tok
    for copy in feeds:
        copy.start()
    fetch()
    most = rows.shape[0] // len(experts)
    r = lax.broadcasted_iota(jnp.int32, (most, at), 0).astype(jnp.float32)
    pick = jnp.concatenate(
        [jnp.where(r == rank[e : e + 1, :], 1.0, 0.0).astype(jnp.bfloat16) for e in experts], axis=0
    )
    for copy in feeds:
        copy.wait()
    rows[...] = jnp.dot(pick, feed[...], preferred_element_type=jnp.float32).astype(jnp.bfloat16)
    products(rows, given, to, info)


def keep_body(info, own, outs, rest, fetch):
    fetch()
    rows, given = own
    products(rows, given, outs[0], info)


def part_shape(given, most, n_dp):
    _, experts, _, half = given.shape
    return jax.ShapeDtypeStruct((n_dp // 2, most * experts, 4 * half // n_dp), jnp.bfloat16)


def send_half(feeds, rank, info, given, weights, experts, most, n_dp, ahead, after):
    local = given.shape[2]
    rows = jax.ShapeDtypeStruct((most * len(experts), local), jnp.bfloat16)
    scratch = [
        pltpu.VMEM((rank.shape[1], local), jnp.bfloat16),
        pltpu.SemaphoreType.DMA((len(feeds),)),
    ]
    inputs = [(feed, HERE) for feed in feeds] + [(rank, VMEM), (given, VMEM)]
    outs = [part_shape(given, most, n_dp), rows]
    body = functools.partial(send_body, experts)
    return call(body, "send_half", info, inputs, weights, ahead, after, outs, scratch)


def keep_half(rows, info, given, weights, most, n_dp, ahead):
    inputs = [(rows, VMEM), (given, VMEM)]
    outs = [part_shape(given, most, n_dp)]
    return call(keep_body, "keep_half", info, inputs, weights, ahead, [], outs, [])


def down_body(lanes, experts, first, info, own, outs, rest, fetch):
    fetch()
    parts, (rank, wt, given) = own[: len(lanes)], own[len(lanes) : len(lanes) + 3]
    before = None if first else own[-1]
    hidden, mix, out = rest
    most = hidden.shape[0] // len(experts)
    width = parts[0].shape[-1]
    n_dp = hidden.shape[1] // width
    for part, (at, shares) in zip(parts, lanes):
        for j, l in enumerate(shares):
            hidden[:, units_of(l, info, n_dp, width)] = part[j, :, at : at + width]
    r = lax.broadcasted_iota(jnp.int32, (most, mix.shape[1]), 0).astype(jnp.float32)
    for x, e in enumerate(experts):
        mix[x * most : (x + 1) * most, :] = jnp.where(
            r == rank[e : e + 1, :], wt[e : e + 1, :], 0.0
        ).astype(jnp.bfloat16)
    local = out.shape[1]
    block = 512 if local % 512 == 0 else 256 if local % 256 == 0 else local
    for i in range(local // block):
        cols = slice(i * block, (i + 1) * block)
        for x in range(len(experts)):
            mine = slice(x * most, (x + 1) * most)
            out[mine, cols] = jnp.dot(
                hidden[mine], given[x, :, cols], preferred_element_type=jnp.float32
            ).astype(jnp.bfloat16)
        total = lax.dot_general(
            mix[...], out[:, cols], (((0,), (0,)), ((), ())), preferred_element_type=jnp.float32
        )
        if not first:
            total = total + before[:, cols]
        at = 0
        for to in outs:
            to[:, cols] = total[at : at + to.shape[0]].astype(to.dtype)
            at += to.shape[0]


def down(parts, rank, wt, info, given, weights, total, experts, cuts, ahead, after):
    parts, lanes = [part for part, *_ in parts], [tuple(where) for _, *where in parts]
    rows = parts[0].shape[1]
    _, hidden, local = given.shape
    kind = jnp.bfloat16 if len(cuts) > 1 else jnp.float32
    before = [] if total is None else [total]
    outs = [jax.ShapeDtypeStruct((cut, local), kind) for cut in cuts]
    scratch = [
        pltpu.VMEM((rows, hidden), jnp.bfloat16),
        pltpu.VMEM((rows, rank.shape[1]), jnp.bfloat16),
        pltpu.VMEM((rows, local), jnp.bfloat16),
    ]
    inputs = [(x, VMEM) for x in (*parts, rank, wt, given, *before)]
    body = functools.partial(down_body, lanes, experts, total is None)
    return call(body, "down", info, inputs, weights, ahead, after, outs, scratch)


def finish(total, late, after):
    if after:
        late, *_ = lax.optimization_barrier((late, *after))
    gate_up = total + late.astype(jnp.float32)
    width = gate_up.shape[2] // 2
    return (jax.nn.silu(gate_up[:, :, :width]) * gate_up[:, :, width:]).astype(jnp.bfloat16)


def chip_sums(send, keep, bits):
    total = keep.astype(jnp.float32) + flip(send, "dp", 1).astype(jnp.float32)
    for b in bits[1:-1]:
        total = total[0::2] + flip(total[1::2].astype(jnp.bfloat16), "dp", 1 << b).astype(jnp.float32)
    return total[0::2], total[1::2].astype(jnp.bfloat16)


def everyone_s(share, other, at, bits):
    width = share.shape[2]
    top = 1 << bits[-1]
    parts = [(share, 0, [0]), (other, at, [top])]
    held, whose = jnp.concatenate([share, other[:, :, at : at + width]], axis=0), [0, top]
    for b in reversed(bits[:-1]):
        theirs = flip(held, "dp", 1 << b)
        parts.append((theirs, 0, [l | 1 << b for l in whose]))
        if b > 0:
            held, whose = jnp.concatenate([held, theirs], axis=0), whose + parts[-1][2]
    return parts


def on_device(tokens, expert_ids, scores, w_gate, w_up, w_down):
    n_owner, n_dp = lax.axis_size("expert"), lax.axis_size("dp")
    tok_rows, top = expert_ids.shape
    experts = w_gate.shape[0]
    capacity = 2 * tok_rows * top // (experts * n_owner)
    per_chunk = 2 if experts % 2 == 0 else 1
    most = n_owner * capacity
    chunks = experts // per_chunk

    meta = jnp.concatenate([expert_ids.T.astype(jnp.float32), scores.T], axis=0)
    me = lax.axis_index("dp").astype(jnp.int32)
    first = lax.axis_index("expert").astype(jnp.int32) * experts
    info = jnp.stack([first, me, backwards(me, n_dp)])
    of = lambda c: list(range(c * per_chunk, (c + 1) * per_chunk))
    weights = (w_gate, w_up, w_down)
    needs = [(of(c), side) for c in range(chunks) for side in (1, 0)] + [(of(c), None) for c in range(chunks)]
    given = {0: stage(info, weights, needs[0], [])}

    def fetched(k, outs):
        if k + 1 < len(needs):
            *outs, given[k + 1] = outs
        return outs

    ahead = lambda k: needs[k + 1] if k + 1 < len(needs) else None

    metas = [meta] + [
        lax.ppermute(meta, "expert", [(i, (i - k) % n_owner) for i in range(n_owner)])
        for k in gathered_order(n_owner)[1:]
    ]
    feeds = gathered(tokens, "expert")
    rank, wt = route(metas, info, experts)

    tall, wide = [tok_rows] + [tok_rows // 2] * (2 * n_owner - 2), tokens.shape[1]
    bits = bits_of(n_dp)
    cross = 1 << bits[-1]
    sent, parts, total = [], [], None
    share = kept = late = None

    def add(c, after):
        k, cuts = 2 * chunks + c, tall if c == chunks - 1 else [sum(tall)]
        outs = down(parts[c], rank, wt, info, given[k], weights, total, of(c), cuts, ahead(k), after)
        outs = fetched(k, outs)
        return outs if c == chunks - 1 else outs[0]

    for c in range(chunks):
        last = c == chunks - 1
        k = 2 * c
        send, rows = fetched(
            k, send_half(feeds, rank, info, given[k], weights, of(c), most, n_dp, ahead(k), sent[-1:])
        )
        k = 2 * c + 1
        (keep,) = fetched(k, keep_half(rows, info, given[k], weights, most, n_dp, ahead(k)))
        before, behind = kept, late
        kept, out = chip_sums(send, keep, bits)
        width = out.shape[2]
        if c > 0:
            share = finish(before, behind[:, :, :width], [])
            out = jnp.concatenate([out, share], axis=2)
        sent.append(out)
        late = flip(out, "dp", cross)
        if c > 0:
            parts.append(everyone_s(share, late, width, bits))
        if last:
            for d in range(min(c - 1, 2)):
                total = add(d, [out] if d == 0 else [])
    share = finish(kept, late[:, :, :width], [] if total is None else [total])
    other = flip(share, "dp", cross)
    for c in range(max(min(chunks - 2, 2), 0), chunks - 1):
        total = add(c, [share])
    if total is not None:
        other = lax.optimization_barrier((other, total))[0]
    parts.append(everyone_s(share, other, 0, bits))
    total = add(chunks - 1, [])
    return returned(total, "expert").astype(jnp.bfloat16)


def gathered_order(n):
    near = [d for s in range(1, n // 2) for d in (-s, s)]
    return [0] + near + ([n // 2] if n > 1 else [])


def ways(n):
    return [(i, (i + 1) % n) for i in range(n)], [(i, (i - 1) % n) for i in range(n)]


def gathered(x, axis):
    n = lax.axis_size(axis)
    up, down_ = [(i, (i + 1) % n) for i in range(n)], [(i, (i - 1) % n) for i in range(n)]
    below = above = x
    found = [x]
    for _ in range(1, n // 2):
        below, above = lax.ppermute(below, axis, up), lax.ppermute(above, axis, down_)
        found += [below, above]
    if n > 1:
        half = x.shape[0] // 2
        found += [lax.ppermute(below[:half], axis, up), lax.ppermute(above[half:], axis, down_)]
    return found


def returned(partials, axis):
    n = lax.axis_size(axis)
    up, down_ = ways(n)
    wide = lambda x: x.astype(jnp.float32)
    mixed = wide(partials[0])
    if n == 1:
        return mixed
    half = mixed.shape[0] // 2

    def hop(there, partial, perm):
        total = partial if there is None else (wide(partial) + wide(there)).astype(jnp.bfloat16)
        return lax.ppermute(total, axis, perm)

    low = [hop(None, partials[-2], down_), None]
    high = [None, hop(None, partials[-1], up)]
    for s in range(n // 2 - 1, 0, -1):
        near = partials[4 * s - 3 : 4 * s + 1]
        low = [hop(low[0], near[0], down_), hop(low[1], near[1], down_)]
        high = [hop(high[0], near[2], up), hop(high[1], near[3], up)]
    halves = []
    for h, own in enumerate((mixed[:half], mixed[half:])):
        for there in (low[h], high[h]):
            own = own if there is None else own + wide(there)
        halves.append(own)
    return jnp.concatenate(halves, axis=0)


def solution(mesh):
    in_specs = (
        P(("groups", "expert"), "dp"),
        P(("groups", "expert"), None),
        P(("groups", "expert"), None),
        P("expert", "dp", None),
        P("expert", "dp", None),
        P("expert", None, "dp"),
    )
    out_specs = P(("groups", "expert"), "dp")
    return jax.shard_map(
        on_device, mesh=mesh, in_specs=in_specs, out_specs=out_specs, check_vma=False
    )
```

```python
import functools

import jax
import jax.numpy as jnp
from jax import lax
from jax.experimental import pallas as pl
from jax.experimental.pallas import tpu as pltpu
from jax.sharding import PartitionSpec as P

LANES = 128
VMEM = pl.BlockSpec(memory_space=pltpu.VMEM)
SMEM = pl.BlockSpec(memory_space=pltpu.SMEM)
HERE = pl.BlockSpec(memory_space=pl.ANY)
FAR = pl.BlockSpec(memory_space=pltpu.HBM)
NOWHERE = -1e6


def bits_of(n):
    return [b for b in range(n.bit_length() - 1)]


def flip(x, axis, k):
    return lax.ppermute(x, axis, [(i, i ^ k) for i in range(lax.axis_size(axis))])


def route_body(n, experts, info, *refs):
    meta, (rank, wt) = refs[:n], refs[n:]
    tok, top = meta[0].shape[1], meta[0].shape[0] // 2
    padded = rank.shape[0]
    first = info[0].astype(jnp.float32)
    e = lax.broadcasted_iota(jnp.int32, (padded, tok), 0).astype(jnp.float32)
    before = (
        lax.broadcasted_iota(jnp.int32, (tok, tok), 0) < lax.broadcasted_iota(jnp.int32, (tok, tok), 1)
    ).astype(jnp.bfloat16)
    count = jnp.zeros((padded, 1), jnp.float32)
    for s in range(n):
        ids, scores = meta[s][:top], meta[s][top:]
        affinity = 1.0 / (1.0 + jnp.exp(-scores))
        share = 2.5 * affinity / jnp.sum(affinity, axis=0, keepdims=True)
        named = jnp.zeros((padded, tok), jnp.float32)
        weight = jnp.zeros((padded, tok), jnp.float32)
        for k in range(top):
            hit = jnp.where(ids[k : k + 1] - first == e, 1.0, 0.0)
            named = named + hit
            weight = weight + hit * share[k : k + 1]
        named = jnp.where(e < experts, named, 0.0)
        place = jnp.dot(named.astype(jnp.bfloat16), before, preferred_element_type=jnp.float32) + count
        rank[:, s * tok : (s + 1) * tok] = jnp.where(named > 0, place, NOWHERE)
        wt[:, s * tok : (s + 1) * tok] = weight
        count = count + jnp.sum(named, axis=1, keepdims=True)


def route(meta, info, experts):
    tokens = len(meta) * meta[0].shape[1]
    table = jax.ShapeDtypeStruct((-(-experts // 8) * 8, tokens), jnp.float32)
    return pl.pallas_call(
        functools.partial(route_body, len(meta), experts),
        out_shape=(table, table),
        in_specs=[SMEM] + [VMEM] * len(meta),
        out_specs=(VMEM, VMEM),
        compiler_params=pltpu.CompilerParams(vmem_limit_bytes=40 << 20),
        name="route",
    )(info, *meta)


def backwards(l, n):
    bits = bits_of(n)
    return sum((((l >> b) & 1) << (len(bits) - 1 - b) for b in bits), 0 * l)


def units_of(l, info, n, width):
    return pl.ds(pl.multiple_of((backwards(l, n) ^ info[2]) * width, width), width)


def set_shape(need, weights):
    (_, depth, wide), (experts, side) = weights[0].shape, need
    return (len(experts), depth, wide) if side is None else (2, len(experts), depth, wide // 2)


def set_copies(need, weights, info, to, sem):
    experts, side = need
    if side is None:
        return [pltpu.make_async_copy(weights[0].at[e], to.at[x], sem.at[x]) for x, e in enumerate(experts)]
    half = to.shape[-1]
    units = pl.ds(pl.multiple_of(((info[1] & 1) ^ side) * half, half), half)
    depth = to.shape[2]
    piece = depth // 3 if depth % 48 == 0 else depth
    places = [
        (m, x, pl.ds(at, piece)) for m in range(2) for x in range(len(experts)) for at in range(0, depth, piece)
    ]
    return [
        pltpu.make_async_copy(weights[m].at[experts[x], deep, units], to.at[m, x, deep], sem.at[i])
        for i, (m, x, deep) in enumerate(places)
    ]


def call(body, name, info, inputs, weights, ahead, after, outs, scratch, limit=24):
    n_in, n_out = len(inputs), len(outs)
    outs = list(outs)
    weights = [] if ahead is None else weights[2:] if ahead[1] is None else weights[:2]
    if ahead is not None:
        outs.append(jax.ShapeDtypeStruct(set_shape(ahead, weights), jnp.bfloat16))
        scratch = scratch + [pltpu.SemaphoreType.DMA((6 * len(ahead[0]),))]

    def whole(info, *refs):
        own, far = refs[:n_in], refs[n_in : n_in + len(weights)]
        rest = refs[n_in + len(weights) + len(after) :]
        results, rest = rest[: len(outs)], rest[len(outs) :]
        on = []
        if ahead is not None:
            on = set_copies(ahead, far, info, results[-1], rest[-1])
            rest = rest[:-1]
        body(info, own, results[:n_out], rest, lambda: [copy.start() for copy in on])
        for copy in on:
            copy.wait()

    return pl.pallas_call(
        whole,
        out_shape=tuple(outs),
        in_specs=[SMEM] + [spec for _, spec in inputs] + [HERE] * (len(weights) + len(after)),
        out_specs=(VMEM,) * len(outs),
        scratch_shapes=scratch,
        compiler_params=pltpu.CompilerParams(vmem_limit_bytes=limit << 20),
        cost_estimate=pl.CostEstimate(flops=1, bytes_accessed=1, transcendentals=0),
        name=name,
    )(info, *[x for x, _ in inputs], *weights, *after)


def stage(info, weights, need, after):
    body = lambda info, own, outs, rest, fetch: fetch()
    return call(body, "stage", info, [], weights, need, after, [], [], 40)[0]


def products(rows, given, to, info):
    most = rows.shape[0] // given.shape[1]
    shares, width = to.shape[0], to.shape[2] // 2
    for m in range(2):
        for x in range(given.shape[1]):
            mine = slice(x * most, (x + 1) * most)
            part = jnp.dot(rows[mine], given[m, x], preferred_element_type=jnp.float32)
            part = part.astype(jnp.bfloat16)
            for q in range(shares):
                j = backwards(q, shares) ^ (info[1] >> 1)
                to[j, mine, m * width : (m + 1) * width] = part[:, q * width : (q + 1) * width]


def send_body(experts, info, own, outs, rest, fetch):
    sources, rank, given = own[:-2], own[-2], own[-1]
    (to, rows), (feed, feed_sem) = outs, rest
    at, feeds = 0, []
    for s, source in enumerate(sources):
        tok = source.shape[0]
        feeds.append(pltpu.make_async_copy(source, feed.at[pl.ds(at, tok)], feed_sem.at[s]))
        at += tok
    for copy in feeds:
        copy.start()
    fetch()
    most = rows.shape[0] // len(experts)
    r = lax.broadcasted_iota(jnp.int32, (most, at), 0).astype(jnp.float32)
    pick = jnp.concatenate(
        [jnp.where(r == rank[e : e + 1, :], 1.0, 0.0).astype(jnp.bfloat16) for e in experts], axis=0
    )
    for copy in feeds:
        copy.wait()
    rows[...] = jnp.dot(pick, feed[...], preferred_element_type=jnp.float32).astype(jnp.bfloat16)
    products(rows, given, to, info)


def keep_body(info, own, outs, rest, fetch):
    fetch()
    rows, given = own
    products(rows, given, outs[0], info)


def part_shape(given, most, n_dp):
    _, experts, _, half = given.shape
    return jax.ShapeDtypeStruct((n_dp // 2, most * experts, 4 * half // n_dp), jnp.bfloat16)


def send_half(feeds, rank, info, given, weights, experts, most, n_dp, ahead, after):
    local = given.shape[2]
    rows = jax.ShapeDtypeStruct((most * len(experts), local), jnp.bfloat16)
    scratch = [
        pltpu.VMEM((rank.shape[1], local), jnp.bfloat16),
        pltpu.SemaphoreType.DMA((len(feeds),)),
    ]
    inputs = [(feed, HERE) for feed in feeds] + [(rank, VMEM), (given, VMEM)]
    outs = [part_shape(given, most, n_dp), rows]
    body = functools.partial(send_body, experts)
    return call(body, "send_half", info, inputs, weights, ahead, after, outs, scratch)


def keep_half(rows, info, given, weights, most, n_dp, ahead):
    inputs = [(rows, VMEM), (given, VMEM)]
    outs = [part_shape(given, most, n_dp)]
    return call(keep_body, "keep_half", info, inputs, weights, ahead, [], outs, [])


def down_body(lanes, experts, first, info, own, outs, rest, fetch):
    fetch()
    parts, (rank, wt, given) = own[: len(lanes)], own[len(lanes) : len(lanes) + 3]
    before = None if first else own[-1]
    hidden, mix, out = rest
    most = hidden.shape[0] // len(experts)
    width = parts[0].shape[-1]
    n_dp = hidden.shape[1] // width
    for part, (at, shares) in zip(parts, lanes):
        for j, l in enumerate(shares):
            hidden[:, units_of(l, info, n_dp, width)] = part[j, :, at : at + width]
    r = lax.broadcasted_iota(jnp.int32, (most, mix.shape[1]), 0).astype(jnp.float32)
    for x, e in enumerate(experts):
        mix[x * most : (x + 1) * most, :] = jnp.where(
            r == rank[e : e + 1, :], wt[e : e + 1, :], 0.0
        ).astype(jnp.bfloat16)
    local = out.shape[1]
    block = 512 if local % 512 == 0 else 256 if local % 256 == 0 else local
    for i in range(local // block):
        cols = slice(i * block, (i + 1) * block)
        for x in range(len(experts)):
            mine = slice(x * most, (x + 1) * most)
            out[mine, cols] = jnp.dot(
                hidden[mine], given[x, :, cols], preferred_element_type=jnp.float32
            ).astype(jnp.bfloat16)
        total = lax.dot_general(
            mix[...], out[:, cols], (((0,), (0,)), ((), ())), preferred_element_type=jnp.float32
        )
        if not first:
            total = total + before[:, cols]
        at = 0
        for to in outs:
            to[:, cols] = total[at : at + to.shape[0]].astype(to.dtype)
            at += to.shape[0]


def down(parts, rank, wt, info, given, weights, total, experts, cuts, ahead, after):
    parts, lanes = [part for part, *_ in parts], [tuple(where) for _, *where in parts]
    rows = parts[0].shape[1]
    _, hidden, local = given.shape
    kind = jnp.bfloat16 if len(cuts) > 1 else jnp.float32
    before = [] if total is None else [total]
    outs = [jax.ShapeDtypeStruct((cut, local), kind) for cut in cuts]
    scratch = [
        pltpu.VMEM((rows, hidden), jnp.bfloat16),
        pltpu.VMEM((rows, rank.shape[1]), jnp.bfloat16),
        pltpu.VMEM((rows, local), jnp.bfloat16),
    ]
    inputs = [(x, VMEM) for x in (*parts, rank, wt, given, *before)]
    body = functools.partial(down_body, lanes, experts, total is None)
    return call(body, "down", info, inputs, weights, ahead, after, outs, scratch)


def finish(total, late, after):
    if after:
        late, *_ = lax.optimization_barrier((late, *after))
    gate_up = total + late.astype(jnp.float32)
    width = gate_up.shape[2] // 2
    return (jax.nn.silu(gate_up[:, :, :width]) * gate_up[:, :, width:]).astype(jnp.bfloat16)


def chip_sums(send, keep, bits):
    total = keep.astype(jnp.float32) + flip(send, "dp", 1).astype(jnp.float32)
    for b in bits[1:-1]:
        total = total[0::2] + flip(total[1::2].astype(jnp.bfloat16), "dp", 1 << b).astype(jnp.float32)
    return total[0::2], total[1::2].astype(jnp.bfloat16)


def everyone_s(share, other, at, bits):
    width = share.shape[2]
    top = 1 << bits[-1]
    parts = [(share, 0, [0]), (other, at, [top])]
    held, whose = jnp.concatenate([share, other[:, :, at : at + width]], axis=0), [0, top]
    for b in reversed(bits[:-1]):
        theirs = flip(held, "dp", 1 << b)
        parts.append((theirs, 0, [l | 1 << b for l in whose]))
        if b > 0:
            held, whose = jnp.concatenate([held, theirs], axis=0), whose + parts[-1][2]
    return parts


def on_device(tokens, expert_ids, scores, w_gate, w_up, w_down):
    n_owner, n_dp = lax.axis_size("expert"), lax.axis_size("dp")
    tok_rows, top = expert_ids.shape
    experts = w_gate.shape[0]
    capacity = 2 * tok_rows * top // (experts * n_owner)
    per_chunk = 2 if experts % 2 == 0 else 1
    most = n_owner * capacity
    chunks = experts // per_chunk

    meta = jnp.concatenate([expert_ids.T.astype(jnp.float32), scores.T], axis=0)
    me = lax.axis_index("dp").astype(jnp.int32)
    first = lax.axis_index("expert").astype(jnp.int32) * experts
    info = jnp.stack([first, me, backwards(me, n_dp)])
    of = lambda c: list(range(c * per_chunk, (c + 1) * per_chunk))
    weights = (w_gate, w_up, w_down)
    needs = [(of(c), side) for c in range(chunks) for side in (1, 0)] + [(of(c), None) for c in range(chunks)]
    given = {0: stage(info, weights, needs[0], [])}

    def fetched(k, outs):
        if k + 1 < len(needs):
            *outs, given[k + 1] = outs
        return outs

    ahead = lambda k: needs[k + 1] if k + 1 < len(needs) else None

    metas = [meta] + [
        lax.ppermute(meta, "expert", [(i, (i - k) % n_owner) for i in range(n_owner)])
        for k in gathered_order(n_owner)[1:]
    ]
    feeds = gathered(tokens, "expert")
    rank, wt = route(metas, info, experts)

    tall, wide = [tok_rows] + [tok_rows // 2] * (2 * n_owner - 2), tokens.shape[1]
    bits = bits_of(n_dp)
    cross = 1 << bits[-1]
    sent, parts, total = [], [], None
    share = kept = late = None

    def add(c, after):
        k, cuts = 2 * chunks + c, tall if c == chunks - 1 else [sum(tall)]
        outs = down(parts[c], rank, wt, info, given[k], weights, total, of(c), cuts, ahead(k), after)
        outs = fetched(k, outs)
        return outs if c == chunks - 1 else outs[0]

    for c in range(chunks):
        last = c == chunks - 1
        k = 2 * c
        send, rows = fetched(
            k, send_half(feeds, rank, info, given[k], weights, of(c), most, n_dp, ahead(k), sent[-1:])
        )
        k = 2 * c + 1
        (keep,) = fetched(k, keep_half(rows, info, given[k], weights, most, n_dp, ahead(k)))
        before, behind = kept, late
        kept, out = chip_sums(send, keep, bits)
        width = out.shape[2]
        if c > 0:
            share = finish(before, behind[:, :, :width], [])
            out = jnp.concatenate([out, share], axis=2)
        sent.append(out)
        late = flip(out, "dp", cross)
        if c > 0:
            parts.append(everyone_s(share, late, width, bits))
        if last:
            for d in range(min(c - 1, 2)):
                total = add(d, [out] if d == 0 else [])
    share = finish(kept, late[:, :, :width], [] if total is None else [total])
    other = flip(share, "dp", cross)
    for c in range(max(min(chunks - 2, 2), 0), chunks - 1):
        total = add(c, [share])
    if total is not None:
        other = lax.optimization_barrier((other, total))[0]
    parts.append(everyone_s(share, other, 0, bits))
    total = add(chunks - 1, [])
    return returned(total, "expert").astype(jnp.bfloat16)


def gathered_order(n):
    near = [d for s in range(1, n // 2) for d in (-s, s)]
    return [0] + near + ([n // 2] if n > 1 else [])


def ways(n):
    return [(i, (i + 1) % n) for i in range(n)], [(i, (i - 1) % n) for i in range(n)]


def gathered(x, axis):
    n = lax.axis_size(axis)
    up, down_ = [(i, (i + 1) % n) for i in range(n)], [(i, (i - 1) % n) for i in range(n)]
    below = above = x
    found = [x]
    for _ in range(1, n // 2):
        below, above = lax.ppermute(below, axis, up), lax.ppermute(above, axis, down_)
        found += [below, above]
    if n > 1:
        half = x.shape[0] // 2
        found += [lax.ppermute(below[:half], axis, up), lax.ppermute(above[half:], axis, down_)]
    return found


def returned(partials, axis):
    n = lax.axis_size(axis)
    up, down_ = ways(n)
    wide = lambda x: x.astype(jnp.float32)
    mixed = wide(partials[0])
    if n == 1:
        return mixed
    half = mixed.shape[0] // 2

    def hop(there, partial, perm):
        total = partial if there is None else (wide(partial) + wide(there)).astype(jnp.bfloat16)
        return lax.ppermute(total, axis, perm)

    low = [hop(None, partials[-2], down_), None]
    high = [None, hop(None, partials[-1], up)]
    for s in range(n // 2 - 1, 0, -1):
        near = partials[4 * s - 3 : 4 * s + 1]
        low = [hop(low[0], near[0], down_), hop(low[1], near[1], down_)]
        high = [hop(high[0], near[2], up), hop(high[1], near[3], up)]
    halves = []
    for h, own in enumerate((mixed[:half], mixed[half:])):
        for there in (low[h], high[h]):
            own = own if there is None else own + wide(there)
        halves.append(own)
    return jnp.concatenate(halves, axis=0)


def solution(mesh):
    in_specs = (
        P(("groups", "expert"), "dp"),
        P(("groups", "expert"), None),
        P(("groups", "expert"), None),
        P("expert", "dp", None),
        P("expert", "dp", None),
        P("expert", None, "dp"),
    )
    out_specs = P(("groups", "expert"), "dp")
    return jax.shard_map(
        on_device, mesh=mesh, in_specs=in_specs, out_specs=out_specs, check_vma=False
    )
```

```python
import functools

import jax
import jax.numpy as jnp
from jax import lax
from jax.experimental import pallas as pl
from jax.experimental.pallas import tpu as pltpu
from jax.sharding import PartitionSpec as P

LANES = 128
VMEM = pl.BlockSpec(memory_space=pltpu.VMEM)
SMEM = pl.BlockSpec(memory_space=pltpu.SMEM)
HERE = pl.BlockSpec(memory_space=pl.ANY)
FAR = pl.BlockSpec(memory_space=pltpu.HBM)
NOWHERE = -1e6


def bits_of(n):
    return [b for b in range(n.bit_length() - 1)]


def flip(x, axis, k):
    return lax.ppermute(x, axis, [(i, i ^ k) for i in range(lax.axis_size(axis))])


def route_body(n, experts, info, *refs):
    meta, (rank, wt) = refs[:n], refs[n:]
    tok, top = meta[0].shape[1], meta[0].shape[0] // 2
    padded = rank.shape[0]
    first = info[0].astype(jnp.float32)
    e = lax.broadcasted_iota(jnp.int32, (padded, tok), 0).astype(jnp.float32)
    before = (
        lax.broadcasted_iota(jnp.int32, (tok, tok), 0) < lax.broadcasted_iota(jnp.int32, (tok, tok), 1)
    ).astype(jnp.bfloat16)
    count = jnp.zeros((padded, 1), jnp.float32)
    for s in range(n):
        ids, scores = meta[s][:top], meta[s][top:]
        affinity = 1.0 / (1.0 + jnp.exp(-scores))
        share = 2.5 * affinity / jnp.sum(affinity, axis=0, keepdims=True)
        named = jnp.zeros((padded, tok), jnp.float32)
        weight = jnp.zeros((padded, tok), jnp.float32)
        for k in range(top):
            hit = jnp.where(ids[k : k + 1] - first == e, 1.0, 0.0)
            named = named + hit
            weight = weight + hit * share[k : k + 1]
        named = jnp.where(e < experts, named, 0.0)
        place = jnp.dot(named.astype(jnp.bfloat16), before, preferred_element_type=jnp.float32) + count
        rank[:, s * tok : (s + 1) * tok] = jnp.where(named > 0, place, NOWHERE)
        wt[:, s * tok : (s + 1) * tok] = weight
        count = count + jnp.sum(named, axis=1, keepdims=True)


def route(meta, info, experts):
    tokens = len(meta) * meta[0].shape[1]
    table = jax.ShapeDtypeStruct((-(-experts // 8) * 8, tokens), jnp.float32)
    return pl.pallas_call(
        functools.partial(route_body, len(meta), experts),
        out_shape=(table, table),
        in_specs=[SMEM] + [VMEM] * len(meta),
        out_specs=(VMEM, VMEM),
        compiler_params=pltpu.CompilerParams(vmem_limit_bytes=40 << 20),
        name="route",
    )(info, *meta)


def backwards(l, n):
    bits = bits_of(n)
    return sum((((l >> b) & 1) << (len(bits) - 1 - b) for b in bits), 0 * l)


def units_of(l, info, n, width):
    return pl.ds(pl.multiple_of((backwards(l, n) ^ info[2]) * width, width), width)


def set_shape(need, weights):
    (_, depth, wide), (experts, side) = weights[0].shape, need
    return (len(experts), depth, wide) if side is None else (2, len(experts), depth, wide // 2)


def set_copies(need, weights, info, to, sem):
    experts, side = need
    if side is None:
        return [pltpu.make_async_copy(weights[0].at[e], to.at[x], sem.at[x]) for x, e in enumerate(experts)]
    half = to.shape[-1]
    units = pl.ds(pl.multiple_of(((info[1] & 1) ^ side) * half, half), half)
    return [
        pltpu.make_async_copy(w.at[e, :, units], to.at[m, x], sem.at[m * len(experts) + x])
        for m, w in enumerate(weights)
        for x, e in enumerate(experts)
    ]


def call(body, name, info, inputs, weights, ahead, after, outs, scratch, limit=24):
    n_in, n_out = len(inputs), len(outs)
    outs = list(outs)
    weights = [] if ahead is None else weights[2:] if ahead[1] is None else weights[:2]
    if ahead is not None:
        outs.append(jax.ShapeDtypeStruct(set_shape(ahead, weights), jnp.bfloat16))
        scratch = scratch + [pltpu.SemaphoreType.DMA((2 * len(ahead[0]),))]

    def whole(info, *refs):
        own, far = refs[:n_in], refs[n_in : n_in + len(weights)]
        rest = refs[n_in + len(weights) + len(after) :]
        results, rest = rest[: len(outs)], rest[len(outs) :]
        on = []
        if ahead is not None:
            on = set_copies(ahead, far, info, results[-1], rest[-1])
            rest = rest[:-1]
        body(info, own, results[:n_out], rest, lambda: [copy.start() for copy in on])
        for copy in on:
            copy.wait()

    return pl.pallas_call(
        whole,
        out_shape=tuple(outs),
        in_specs=[SMEM] + [spec for _, spec in inputs] + [HERE] * (len(weights) + len(after)),
        out_specs=(VMEM,) * len(outs),
        scratch_shapes=scratch,
        compiler_params=pltpu.CompilerParams(vmem_limit_bytes=limit << 20),
        cost_estimate=pl.CostEstimate(flops=1, bytes_accessed=1, transcendentals=0),
        name=name,
    )(info, *[x for x, _ in inputs], *weights, *after)


def stage(info, weights, need, after):
    body = lambda info, own, outs, rest, fetch: fetch()
    return call(body, "stage", info, [], weights, need, after, [], [], 40)[0]


def products(rows, given, to, info):
    most = rows.shape[0] // given.shape[1]
    shares, width = to.shape[0], to.shape[2] // 2
    for m in range(2):
        for x in range(given.shape[1]):
            mine = slice(x * most, (x + 1) * most)
            part = jnp.dot(rows[mine], given[m, x], preferred_element_type=jnp.float32)
            part = part.astype(jnp.bfloat16)
            for q in range(shares):
                j = backwards(q, shares) ^ (info[1] >> 1)
                to[j, mine, m * width : (m + 1) * width] = part[:, q * width : (q + 1) * width]


def send_body(experts, info, own, outs, rest, fetch):
    sources, rank, given = own[:-2], own[-2], own[-1]
    (to, rows), (feed, feed_sem) = outs, rest
    at, feeds = 0, []
    for s, source in enumerate(sources):
        tok = source.shape[0]
        feeds.append(pltpu.make_async_copy(source, feed.at[pl.ds(at, tok)], feed_sem.at[s]))
        at += tok
    for copy in feeds:
        copy.start()
    fetch()
    most = rows.shape[0] // len(experts)
    r = lax.broadcasted_iota(jnp.int32, (most, at), 0).astype(jnp.float32)
    pick = jnp.concatenate(
        [jnp.where(r == rank[e : e + 1, :], 1.0, 0.0).astype(jnp.bfloat16) for e in experts], axis=0
    )
    for copy in feeds:
        copy.wait()
    rows[...] = jnp.dot(pick, feed[...], preferred_element_type=jnp.float32).astype(jnp.bfloat16)
    products(rows, given, to, info)


def keep_body(info, own, outs, rest, fetch):
    fetch()
    rows, given = own
    products(rows, given, outs[0], info)


def part_shape(given, most, n_dp):
    _, experts, _, half = given.shape
    return jax.ShapeDtypeStruct((n_dp // 2, most * experts, 4 * half // n_dp), jnp.bfloat16)


def send_half(feeds, rank, info, given, weights, experts, most, n_dp, ahead, after):
    local = given.shape[2]
    rows = jax.ShapeDtypeStruct((most * len(experts), local), jnp.bfloat16)
    scratch = [
        pltpu.VMEM((rank.shape[1], local), jnp.bfloat16),
        pltpu.SemaphoreType.DMA((len(feeds),)),
    ]
    inputs = [(feed, HERE) for feed in feeds] + [(rank, VMEM), (given, VMEM)]
    outs = [part_shape(given, most, n_dp), rows]
    body = functools.partial(send_body, experts)
    return call(body, "send_half", info, inputs, weights, ahead, after, outs, scratch)


def keep_half(rows, info, given, weights, most, n_dp, ahead):
    inputs = [(rows, VMEM), (given, VMEM)]
    outs = [part_shape(given, most, n_dp)]
    return call(keep_body, "keep_half", info, inputs, weights, ahead, [], outs, [])


def down_body(lanes, experts, first, info, own, outs, rest, fetch):
    fetch()
    parts, (rank, wt, given) = own[: len(lanes)], own[len(lanes) : len(lanes) + 3]
    before = None if first else own[-1]
    mix, out, *hidden = rest
    hidden = hidden[0] if hidden else None
    most = mix.shape[0] // len(experts)
    width = parts[0].shape[-1]
    n_dp = given.shape[1] // width
    for part, (at, shares) in zip(parts, lanes) if hidden is not None else ():
        for j, l in enumerate(shares):
            hidden[:, units_of(l, info, n_dp, width)] = part[j, :, at : at + width]

    def product(x, mine, cols):
        if hidden is not None:
            return jnp.dot(hidden[mine], given[x, :, cols], preferred_element_type=jnp.float32)
        total = 0.0
        for part, (at, shares) in zip(parts, lanes):
            for j, l in enumerate(shares):
                weights = given[x, units_of(l, info, n_dp, width), cols]
                total = total + jnp.dot(
                    part[j, mine, at : at + width], weights, preferred_element_type=jnp.float32
                )
        return total

    r = lax.broadcasted_iota(jnp.int32, (most, mix.shape[1]), 0).astype(jnp.float32)
    for x, e in enumerate(experts):
        mix[x * most : (x + 1) * most, :] = jnp.where(
            r == rank[e : e + 1, :], wt[e : e + 1, :], 0.0
        ).astype(jnp.bfloat16)
    local = out.shape[1]
    block = 512 if local % 512 == 0 else 256 if local % 256 == 0 else local
    for i in range(local // block):
        cols = slice(i * block, (i + 1) * block)
        for x in range(len(experts)):
            mine = slice(x * most, (x + 1) * most)
            out[mine, cols] = product(x, mine, cols).astype(jnp.bfloat16)
        total = lax.dot_general(
            mix[...], out[:, cols], (((0,), (0,)), ((), ())), preferred_element_type=jnp.float32
        )
        if not first:
            total = total + before[:, cols]
        at = 0
        for to in outs:
            to[:, cols] = total[at : at + to.shape[0]].astype(to.dtype)
            at += to.shape[0]


def down(parts, rank, wt, info, given, weights, total, experts, cuts, ahead, after):
    parts, lanes = [part for part, *_ in parts], [tuple(where) for _, *where in parts]
    rows = parts[0].shape[1]
    _, hidden, local = given.shape
    kind = jnp.bfloat16 if len(cuts) > 1 else jnp.float32
    before = [] if total is None else [total]
    outs = [jax.ShapeDtypeStruct((cut, local), kind) for cut in cuts]
    scratch = [
        pltpu.VMEM((rows, rank.shape[1]), jnp.bfloat16),
        pltpu.VMEM((rows, local), jnp.bfloat16),
    ]
    if sum(len(shares) for _, shares in lanes) * parts[0].shape[2] == hidden:
        scratch.append(pltpu.VMEM((rows, hidden), jnp.bfloat16))
    inputs = [(x, VMEM) for x in (*parts, rank, wt, given, *before)]
    body = functools.partial(down_body, lanes, experts, total is None)
    return call(body, "down", info, inputs, weights, ahead, after, outs, scratch)


def finish(total, late, after):
    if after:
        late, *_ = lax.optimization_barrier((late, *after))
    gate_up = total + late.astype(jnp.float32)
    width = gate_up.shape[2] // 2
    return (jax.nn.silu(gate_up[:, :, :width]) * gate_up[:, :, width:]).astype(jnp.bfloat16)


def chip_sums(send, keep, bits):
    total = keep.astype(jnp.float32) + flip(send, "dp", 1).astype(jnp.float32)
    for b in bits[1:-1]:
        total = total[0::2] + flip(total[1::2].astype(jnp.bfloat16), "dp", 1 << b).astype(jnp.float32)
    return total[0::2], total[1::2].astype(jnp.bfloat16)


def everyone_s(share, other, at, bits):
    width = share.shape[2]
    top = 1 << bits[-1]
    parts = [(share, 0, [0]), (other, at, [top])]
    held, whose = jnp.concatenate([share, other[:, :, at : at + width]], axis=0), [0, top]
    for b in reversed(bits[:-1]):
        theirs = flip(held, "dp", 1 << b)
        parts.append((theirs, 0, [l | 1 << b for l in whose]))
        if b > 0:
            held, whose = jnp.concatenate([held, theirs], axis=0), whose + parts[-1][2]
    return parts


def spread(held, whose, bits):
    parts, whose = [(held, 0, [whose])], [whose]
    for b in reversed(bits[:-1]):
        theirs = flip(held, "dp", 1 << b)
        parts.append((theirs, 0, [l | 1 << b for l in whose]))
        if b > 0:
            held, whose = jnp.concatenate([held, theirs], axis=0), whose + parts[-1][2]
    return parts


def on_device(tokens, expert_ids, scores, w_gate, w_up, w_down):
    n_owner, n_dp = lax.axis_size("expert"), lax.axis_size("dp")
    tok_rows, top = expert_ids.shape
    experts = w_gate.shape[0]
    capacity = 2 * tok_rows * top // (experts * n_owner)
    per_chunk = 2 if experts % 2 == 0 else 1
    most = n_owner * capacity
    chunks = experts // per_chunk

    meta = jnp.concatenate([expert_ids.T.astype(jnp.float32), scores.T], axis=0)
    me = lax.axis_index("dp").astype(jnp.int32)
    first = lax.axis_index("expert").astype(jnp.int32) * experts
    info = jnp.stack([first, me, backwards(me, n_dp)])
    of = lambda c: list(range(c * per_chunk, (c + 1) * per_chunk))
    weights = (w_gate, w_up, w_down)
    needs = [(of(c), side) for c in range(chunks) for side in (1, 0)] + [(of(c), None) for c in range(chunks)]
    given = {0: stage(info, weights, needs[0], [])}

    def fetched(k, outs):
        if k + 1 < len(needs):
            *outs, given[k + 1] = outs
        return outs

    ahead = lambda k: needs[k + 1] if k + 1 < len(needs) else None

    metas = [meta] + [
        lax.ppermute(meta, "expert", [(i, (i - k) % n_owner) for i in range(n_owner)])
        for k in gathered_order(n_owner)[1:]
    ]
    feeds = gathered(tokens, "expert")
    rank, wt = route(metas, info, experts)

    tall, wide = [tok_rows] + [tok_rows // 2] * (2 * n_owner - 2), tokens.shape[1]
    bits = bits_of(n_dp)
    cross = 1 << bits[-1]
    sent, parts, total = [], [], None
    share = kept = late = None

    def add(c, after):
        k = 2 * chunks + c
        outs = down(parts[c], rank, wt, info, given[k], weights, total, of(c), [sum(tall)], ahead(k), after)
        return fetched(k, outs)[0]

    for c in range(chunks):
        last = c == chunks - 1
        k = 2 * c
        send, rows = fetched(
            k, send_half(feeds, rank, info, given[k], weights, of(c), most, n_dp, ahead(k), sent[-1:])
        )
        k = 2 * c + 1
        (keep,) = fetched(k, keep_half(rows, info, given[k], weights, most, n_dp, ahead(k)))
        before, behind = kept, late
        kept, out = chip_sums(send, keep, bits)
        width = out.shape[2]
        if c > 0:
            share = finish(before, behind[:, :, :width], [])
            out = jnp.concatenate([out, share], axis=2)
        sent.append(out)
        late = flip(out, "dp", cross)
        if c > 0:
            parts.append(everyone_s(share, late, width, bits))
        if last:
            for d in range(min(c - 1, 2)):
                total = add(d, [out] if d == 0 else [])
    share = finish(kept, late[:, :, :width], [] if total is None else [total])
    other = flip(share, "dp", cross)
    for c in range(max(min(chunks - 2, 2), 0), chunks - 1):
        total = add(c, [share])
    k = 3 * chunks - 1
    near = spread(share, 0, bits)
    total = down(near, rank, wt, info, given[k], weights, total, of(chunks - 1), [sum(tall)], None, [])[0]
    far = spread(lax.optimization_barrier((other, total))[0], cross, bits)
    total = down(far, rank, wt, info, given[k], weights, total, of(chunks - 1), tall, None, [])
    return returned(total, "expert").astype(jnp.bfloat16)


def gathered_order(n):
    near = [d for s in range(1, n // 2) for d in (-s, s)]
    return [0] + near + ([n // 2] if n > 1 else [])


def ways(n):
    return [(i, (i + 1) % n) for i in range(n)], [(i, (i - 1) % n) for i in range(n)]


def gathered(x, axis):
    n = lax.axis_size(axis)
    up, down_ = [(i, (i + 1) % n) for i in range(n)], [(i, (i - 1) % n) for i in range(n)]
    below = above = x
    found = [x]
    for _ in range(1, n // 2):
        below, above = lax.ppermute(below, axis, up), lax.ppermute(above, axis, down_)
        found += [below, above]
    if n > 1:
        half = x.shape[0] // 2
        found += [lax.ppermute(below[:half], axis, up), lax.ppermute(above[half:], axis, down_)]
    return found


def returned(partials, axis):
    n = lax.axis_size(axis)
    up, down_ = ways(n)
    wide = lambda x: x.astype(jnp.float32)
    mixed = wide(partials[0])
    if n == 1:
        return mixed
    half = mixed.shape[0] // 2

    def hop(there, partial, perm):
        total = partial if there is None else (wide(partial) + wide(there)).astype(jnp.bfloat16)
        return lax.ppermute(total, axis, perm)

    low = [hop(None, partials[-2], down_), None]
    high = [None, hop(None, partials[-1], up)]
    for s in range(n // 2 - 1, 0, -1):
        near = partials[4 * s - 3 : 4 * s + 1]
        low = [hop(low[0], near[0], down_), hop(low[1], near[1], down_)]
        high = [hop(high[0], near[2], up), hop(high[1], near[3], up)]
    halves = []
    for h, own in enumerate((mixed[:half], mixed[half:])):
        for there in (low[h], high[h]):
            own = own if there is None else own + wide(there)
        halves.append(own)
    return jnp.concatenate(halves, axis=0)


def solution(mesh):
    in_specs = (
        P(("groups", "expert"), "dp"),
        P(("groups", "expert"), None),
        P(("groups", "expert"), None),
        P("expert", "dp", None),
        P("expert", "dp", None),
        P("expert", None, "dp"),
    )
    out_specs = P(("groups", "expert"), "dp")
    return jax.shard_map(
        on_device, mesh=mesh, in_specs=in_specs, out_specs=out_specs, check_vma=False
    )
```

```python
import functools

import jax
import jax.numpy as jnp
from jax import lax
from jax.experimental import pallas as pl
from jax.experimental.pallas import tpu as pltpu
from jax.sharding import PartitionSpec as P

LANES = 128
VMEM = pl.BlockSpec(memory_space=pltpu.VMEM)
SMEM = pl.BlockSpec(memory_space=pltpu.SMEM)
HERE = pl.BlockSpec(memory_space=pl.ANY)
FAR = pl.BlockSpec(memory_space=pltpu.HBM)
NOWHERE = -1e6


def bits_of(n):
    return [b for b in range(n.bit_length() - 1)]


def flip(x, axis, k):
    return lax.ppermute(x, axis, [(i, i ^ k) for i in range(lax.axis_size(axis))])


def route_body(n, experts, info, *refs):
    meta, (rank, wt) = refs[:n], refs[n:]
    tok, top = meta[0].shape[1], meta[0].shape[0] // 2
    padded = rank.shape[0]
    first = info[0].astype(jnp.float32)
    e = lax.broadcasted_iota(jnp.int32, (padded, tok), 0).astype(jnp.float32)
    before = (
        lax.broadcasted_iota(jnp.int32, (tok, tok), 0) < lax.broadcasted_iota(jnp.int32, (tok, tok), 1)
    ).astype(jnp.bfloat16)
    count = jnp.zeros((padded, 1), jnp.float32)
    for s in range(n):
        ids, scores = meta[s][:top], meta[s][top:]
        affinity = 1.0 / (1.0 + jnp.exp(-scores))
        share = 2.5 * affinity / jnp.sum(affinity, axis=0, keepdims=True)
        named = jnp.zeros((padded, tok), jnp.float32)
        weight = jnp.zeros((padded, tok), jnp.float32)
        for k in range(top):
            hit = jnp.where(ids[k : k + 1] - first == e, 1.0, 0.0)
            named = named + hit
            weight = weight + hit * share[k : k + 1]
        named = jnp.where(e < experts, named, 0.0)
        place = jnp.dot(named.astype(jnp.bfloat16), before, preferred_element_type=jnp.float32) + count
        rank[:, s * tok : (s + 1) * tok] = jnp.where(named > 0, place, NOWHERE)
        wt[:, s * tok : (s + 1) * tok] = weight
        count = count + jnp.sum(named, axis=1, keepdims=True)


def route(meta, info, experts):
    tokens = len(meta) * meta[0].shape[1]
    table = jax.ShapeDtypeStruct((-(-experts // 8) * 8, tokens), jnp.float32)
    return pl.pallas_call(
        functools.partial(route_body, len(meta), experts),
        out_shape=(table, table),
        in_specs=[SMEM] + [VMEM] * len(meta),
        out_specs=(VMEM, VMEM),
        compiler_params=pltpu.CompilerParams(vmem_limit_bytes=40 << 20),
        name="route",
    )(info, *meta)


def backwards(l, n):
    bits = bits_of(n)
    return sum((((l >> b) & 1) << (len(bits) - 1 - b) for b in bits), 0 * l)


def units_of(l, info, n, width):
    return pl.ds(pl.multiple_of((backwards(l, n) ^ info[2]) * width, width), width)


def set_shape(need, weights):
    (_, depth, wide), (experts, side) = weights[0].shape, need
    return (len(experts), depth, wide) if side is None else (2, len(experts), depth, wide // 2)


def set_copies(need, weights, info, to, sem):
    experts, side = need
    if side is None:
        return [pltpu.make_async_copy(weights[0].at[e], to.at[x], sem.at[x]) for x, e in enumerate(experts)]
    half = to.shape[-1]
    units = pl.ds(pl.multiple_of(((info[1] & 1) ^ side) * half, half), half)
    return [
        pltpu.make_async_copy(w.at[e, :, units], to.at[m, x], sem.at[m * len(experts) + x])
        for m, w in enumerate(weights)
        for x, e in enumerate(experts)
    ]


def call(body, name, info, inputs, weights, ahead, after, outs, scratch, limit=24):
    n_in, n_out = len(inputs), len(outs)
    outs = list(outs)
    weights = [] if ahead is None else weights[2:] if ahead[1] is None else weights[:2]
    if ahead is not None:
        outs.append(jax.ShapeDtypeStruct(set_shape(ahead, weights), jnp.bfloat16))
        scratch = scratch + [pltpu.SemaphoreType.DMA((2 * len(ahead[0]),))]

    def whole(info, *refs):
        own, far = refs[:n_in], refs[n_in : n_in + len(weights)]
        rest = refs[n_in + len(weights) + len(after) :]
        results, rest = rest[: len(outs)], rest[len(outs) :]
        on = []
        if ahead is not None:
            on = set_copies(ahead, far, info, results[-1], rest[-1])
            rest = rest[:-1]
        body(info, own, results[:n_out], rest, lambda: [copy.start() for copy in on])
        for copy in on:
            copy.wait()

    return pl.pallas_call(
        whole,
        out_shape=tuple(outs),
        in_specs=[SMEM] + [spec for _, spec in inputs] + [HERE] * (len(weights) + len(after)),
        out_specs=(VMEM,) * len(outs),
        scratch_shapes=scratch,
        compiler_params=pltpu.CompilerParams(vmem_limit_bytes=limit << 20),
        cost_estimate=pl.CostEstimate(flops=1, bytes_accessed=1, transcendentals=0),
        name=name,
    )(info, *[x for x, _ in inputs], *weights, *after)


def stage(info, weights, need, after):
    body = lambda info, own, outs, rest, fetch: fetch()
    return call(body, "stage", info, [], weights, need, after, [], [], 40)[0]


def products(rows, given, to, info):
    most = rows.shape[0] // given.shape[1]
    shares, width = to.shape[0], to.shape[2] // 2
    for m in range(2):
        for x in range(given.shape[1]):
            mine = slice(x * most, (x + 1) * most)
            part = jnp.dot(rows[mine], given[m, x], preferred_element_type=jnp.float32)
            part = part.astype(jnp.bfloat16)
            for q in range(shares):
                j = backwards(q, shares) ^ (info[1] >> 1)
                to[j, mine, m * width : (m + 1) * width] = part[:, q * width : (q + 1) * width]


def send_body(experts, info, own, outs, rest, fetch):
    sources, rank, given = own[:-2], own[-2], own[-1]
    (to, rows), (feed, feed_sem) = outs, rest
    at, feeds = 0, []
    for s, source in enumerate(sources):
        tok = source.shape[0]
        feeds.append(pltpu.make_async_copy(source, feed.at[pl.ds(at, tok)], feed_sem.at[s]))
        at += tok
    for copy in feeds:
        copy.start()
    fetch()
    most = rows.shape[0] // len(experts)
    r = lax.broadcasted_iota(jnp.int32, (most, at), 0).astype(jnp.float32)
    pick = jnp.concatenate(
        [jnp.where(r == rank[e : e + 1, :], 1.0, 0.0).astype(jnp.bfloat16) for e in experts], axis=0
    )
    for copy in feeds:
        copy.wait()
    rows[...] = jnp.dot(pick, feed[...], preferred_element_type=jnp.float32).astype(jnp.bfloat16)
    products(rows, given, to, info)


def keep_body(info, own, outs, rest, fetch):
    fetch()
    rows, given = own
    products(rows, given, outs[0], info)


def part_shape(given, most, n_dp):
    _, experts, _, half = given.shape
    return jax.ShapeDtypeStruct((n_dp // 2, most * experts, 4 * half // n_dp), jnp.bfloat16)


def send_half(feeds, rank, info, given, weights, experts, most, n_dp, ahead, after):
    local = given.shape[2]
    rows = jax.ShapeDtypeStruct((most * len(experts), local), jnp.bfloat16)
    scratch = [
        pltpu.VMEM((rank.shape[1], local), jnp.bfloat16),
        pltpu.SemaphoreType.DMA((len(feeds),)),
    ]
    inputs = [(feed, HERE) for feed in feeds] + [(rank, VMEM), (given, VMEM)]
    outs = [part_shape(given, most, n_dp), rows]
    body = functools.partial(send_body, experts)
    return call(body, "send_half", info, inputs, weights, ahead, after, outs, scratch)


def keep_half(rows, info, given, weights, most, n_dp, ahead):
    inputs = [(rows, VMEM), (given, VMEM)]
    outs = [part_shape(given, most, n_dp)]
    return call(keep_body, "keep_half", info, inputs, weights, ahead, [], outs, [])


def down_body(lanes, experts, first, info, own, outs, rest, fetch):
    fetch()
    parts, (rank, wt, given) = own[: len(lanes)], own[len(lanes) : len(lanes) + 3]
    before = None if first else own[-1]
    hidden, mix, out = rest
    most = hidden.shape[0] // len(experts)
    width = parts[0].shape[-1]
    n_dp = hidden.shape[1] // width
    for part, (at, shares) in zip(parts, lanes):
        for j, l in enumerate(shares):
            hidden[:, units_of(l, info, n_dp, width)] = part[j, :, at : at + width]
    r = lax.broadcasted_iota(jnp.int32, (most, mix.shape[1]), 0).astype(jnp.float32)
    for x, e in enumerate(experts):
        mix[x * most : (x + 1) * most, :] = jnp.where(
            r == rank[e : e + 1, :], wt[e : e + 1, :], 0.0
        ).astype(jnp.bfloat16)
    local = out.shape[1]
    block = 512 if local % 512 == 0 else 256 if local % 256 == 0 else local
    for i in range(local // block):
        cols = slice(i * block, (i + 1) * block)
        for x in range(len(experts)):
            mine = slice(x * most, (x + 1) * most)
            out[mine, cols] = jnp.dot(
                hidden[mine], given[x, :, cols], preferred_element_type=jnp.float32
            ).astype(jnp.bfloat16)
        total = lax.dot_general(
            mix[...], out[:, cols], (((0,), (0,)), ((), ())), preferred_element_type=jnp.float32
        )
        if not first:
            total = total + before[:, cols]
        at = 0
        for to in outs:
            to[:, cols] = total[at : at + to.shape[0]].astype(to.dtype)
            at += to.shape[0]


def down(parts, rank, wt, info, given, weights, total, experts, cuts, ahead, after):
    parts, lanes = [part for part, *_ in parts], [tuple(where) for _, *where in parts]
    rows = parts[0].shape[1]
    _, hidden, local = given.shape
    kind = jnp.bfloat16 if len(cuts) > 1 else jnp.float32
    before = [] if total is None else [total]
    outs = [jax.ShapeDtypeStruct((cut, local), kind) for cut in cuts]
    scratch = [
        pltpu.VMEM((rows, hidden), jnp.bfloat16),
        pltpu.VMEM((rows, rank.shape[1]), jnp.bfloat16),
        pltpu.VMEM((rows, local), jnp.bfloat16),
    ]
    inputs = [(x, VMEM) for x in (*parts, rank, wt, given, *before)]
    body = functools.partial(down_body, lanes, experts, total is None)
    return call(body, "down", info, inputs, weights, ahead, after, outs, scratch)


def finish(total, late, after):
    if after:
        late, *_ = lax.optimization_barrier((late, *after))
    gate_up = total + late.astype(jnp.float32)
    width = gate_up.shape[2] // 2
    return (jax.nn.silu(gate_up[:, :, :width]) * gate_up[:, :, width:]).astype(jnp.bfloat16)


def chip_sums(send, keep, bits):
    total = keep.astype(jnp.float32) + flip(send, "dp", 1).astype(jnp.float32)
    for b in bits[1:-1]:
        total = total[0::2] + flip(total[1::2].astype(jnp.bfloat16), "dp", 1 << b).astype(jnp.float32)
    return total[0::2], total[1::2].astype(jnp.bfloat16)


def everyone_s(share, other, at, bits):
    width = share.shape[2]
    top = 1 << bits[-1]
    parts = [(share, 0, [0]), (other, at, [top])]
    held, whose = jnp.concatenate([share, other[:, :, at : at + width]], axis=0), [0, top]
    for b in reversed(bits[:-1]):
        theirs = flip(held, "dp", 1 << b)
        parts.append((theirs, 0, [l | 1 << b for l in whose]))
        if b > 0:
            held, whose = jnp.concatenate([held, theirs], axis=0), whose + parts[-1][2]
    return parts


def on_device(tokens, expert_ids, scores, w_gate, w_up, w_down):
    n_owner, n_dp = lax.axis_size("expert"), lax.axis_size("dp")
    tok_rows, top = expert_ids.shape
    experts = w_gate.shape[0]
    capacity = 2 * tok_rows * top // (experts * n_owner)
    per_chunk = 2 if experts % 2 == 0 else 1
    most = n_owner * capacity
    chunks = experts // per_chunk

    meta = jnp.concatenate([expert_ids.T.astype(jnp.float32), scores.T], axis=0)
    me = lax.axis_index("dp").astype(jnp.int32)
    first = lax.axis_index("expert").astype(jnp.int32) * experts
    info = jnp.stack([first, me, backwards(me, n_dp)])
    of = lambda c: list(range(c * per_chunk, (c + 1) * per_chunk))
    weights = (w_gate, w_up, w_down)
    needs = [(of(c), side) for c in range(chunks) for side in (1, 0)] + [(of(c), None) for c in range(chunks)]
    given = {0: stage(info, weights, needs[0], [])}

    def fetched(k, outs):
        if k + 1 < len(needs):
            *outs, given[k + 1] = outs
        return outs

    ahead = lambda k: needs[k + 1] if k + 1 < len(needs) else None

    metas = [meta] + [
        lax.ppermute(meta, "expert", [(i, (i - k) % n_owner) for i in range(n_owner)])
        for k in gathered_order(n_owner)[1:]
    ]
    feeds = gathered(tokens, "expert")
    rank, wt = route(metas, info, experts)

    tall, wide = [tok_rows] + [tok_rows // 2] * (2 * n_owner - 2), tokens.shape[1]
    bits = bits_of(n_dp)
    cross = 1 << bits[-1]
    sent, parts, total = [], [], None
    share = kept = late = None

    def add(c, after):
        k, cuts = 2 * chunks + c, tall if c == chunks - 1 else [sum(tall)]
        outs = down(parts[c], rank, wt, info, given[k], weights, total, of(c), cuts, ahead(k), after)
        outs = fetched(k, outs)
        return outs if c == chunks - 1 else outs[0]

    for c in range(chunks):
        last = c == chunks - 1
        k = 2 * c
        send, rows = fetched(
            k, send_half(feeds, rank, info, given[k], weights, of(c), most, n_dp, ahead(k), sent[-1:])
        )
        k = 2 * c + 1
        (keep,) = fetched(k, keep_half(rows, info, given[k], weights, most, n_dp, ahead(k)))
        before, behind = kept, late
        kept, out = chip_sums(send, keep, bits)
        width = out.shape[2]
        if c > 0:
            share = finish(before, behind[:, :, :width], [])
            alone = last and c > 1
            out = lax.optimization_barrier((out, share))[0] if alone else jnp.concatenate([out, share], axis=2)
        sent.append(out)
        late = flip(out, "dp", cross)
        if c > 0 and not alone:
            parts.append(everyone_s(share, late, width, bits))
        if last:
            for d in range(min(c - 1, 2)):
                total = add(d, [out] if d == 0 else [])
                if d == 0:
                    share = lax.optimization_barrier((share, total))[0]
                    parts.append(everyone_s(share, flip(share, "dp", cross), 0, bits))
    share = finish(kept, late[:, :, :width], [] if total is None else [total])
    other = flip(share, "dp", cross)
    for c in range(max(min(chunks - 2, 2), 0), chunks - 1):
        total = add(c, [share])
    if total is not None:
        other = lax.optimization_barrier((other, total))[0]
    parts.append(everyone_s(share, other, 0, bits))
    total = add(chunks - 1, [])
    return returned(total, "expert").astype(jnp.bfloat16)


def gathered_order(n):
    near = [d for s in range(1, n // 2) for d in (-s, s)]
    return [0] + near + ([n // 2] if n > 1 else [])


def ways(n):
    return [(i, (i + 1) % n) for i in range(n)], [(i, (i - 1) % n) for i in range(n)]


def gathered(x, axis):
    n = lax.axis_size(axis)
    up, down_ = [(i, (i + 1) % n) for i in range(n)], [(i, (i - 1) % n) for i in range(n)]
    below = above = x
    found = [x]
    for _ in range(1, n // 2):
        below, above = lax.ppermute(below, axis, up), lax.ppermute(above, axis, down_)
        found += [below, above]
    if n > 1:
        half = x.shape[0] // 2
        found += [lax.ppermute(below[:half], axis, up), lax.ppermute(above[half:], axis, down_)]
    return found


def returned(partials, axis):
    n = lax.axis_size(axis)
    up, down_ = ways(n)
    wide = lambda x: x.astype(jnp.float32)
    mixed = wide(partials[0])
    if n == 1:
        return mixed
    half = mixed.shape[0] // 2

    def hop(there, partial, perm):
        total = partial if there is None else (wide(partial) + wide(there)).astype(jnp.bfloat16)
        return lax.ppermute(total, axis, perm)

    low = [hop(None, partials[-2], down_), None]
    high = [None, hop(None, partials[-1], up)]
    for s in range(n // 2 - 1, 0, -1):
        near = partials[4 * s - 3 : 4 * s + 1]
        low = [hop(low[0], near[0], down_), hop(low[1], near[1], down_)]
        high = [hop(high[0], near[2], up), hop(high[1], near[3], up)]
    halves = []
    for h, own in enumerate((mixed[:half], mixed[half:])):
        for there in (low[h], high[h]):
            own = own if there is None else own + wide(there)
        halves.append(own)
    return jnp.concatenate(halves, axis=0)


def solution(mesh):
    in_specs = (
        P(("groups", "expert"), "dp"),
        P(("groups", "expert"), None),
        P(("groups", "expert"), None),
        P("expert", "dp", None),
        P("expert", "dp", None),
        P("expert", None, "dp"),
    )
    out_specs = P(("groups", "expert"), "dp")
    return jax.shard_map(
        on_device, mesh=mesh, in_specs=in_specs, out_specs=out_specs, check_vma=False
    )
```

```python
import functools

import jax
import jax.numpy as jnp
from jax import lax
from jax.experimental import pallas as pl
from jax.experimental.pallas import tpu as pltpu
from jax.sharding import PartitionSpec as P

LANES = 128
VMEM = pl.BlockSpec(memory_space=pltpu.VMEM)
SMEM = pl.BlockSpec(memory_space=pltpu.SMEM)
HERE = pl.BlockSpec(memory_space=pl.ANY)
FAR = pl.BlockSpec(memory_space=pltpu.HBM)
NOWHERE = -1e6


def bits_of(n):
    return [b for b in range(n.bit_length() - 1)]


def flip(x, axis, k):
    return lax.ppermute(x, axis, [(i, i ^ k) for i in range(lax.axis_size(axis))])


def route_body(n, experts, info, *refs):
    meta, (rank, wt) = refs[:n], refs[n:]
    tok, top = meta[0].shape[1], meta[0].shape[0] // 2
    padded = rank.shape[0]
    first = info[0].astype(jnp.float32)
    e = lax.broadcasted_iota(jnp.int32, (padded, tok), 0).astype(jnp.float32)
    before = (
        lax.broadcasted_iota(jnp.int32, (tok, tok), 0) < lax.broadcasted_iota(jnp.int32, (tok, tok), 1)
    ).astype(jnp.bfloat16)
    count = jnp.zeros((padded, 1), jnp.float32)
    for s in range(n):
        ids, scores = meta[s][:top], meta[s][top:]
        affinity = 1.0 / (1.0 + jnp.exp(-scores))
        share = 2.5 * affinity / jnp.sum(affinity, axis=0, keepdims=True)
        named = jnp.zeros((padded, tok), jnp.float32)
        weight = jnp.zeros((padded, tok), jnp.float32)
        for k in range(top):
            hit = jnp.where(ids[k : k + 1] - first == e, 1.0, 0.0)
            named = named + hit
            weight = weight + hit * share[k : k + 1]
        named = jnp.where(e < experts, named, 0.0)
        place = jnp.dot(named.astype(jnp.bfloat16), before, preferred_element_type=jnp.float32) + count
        rank[:, s * tok : (s + 1) * tok] = jnp.where(named > 0, place, NOWHERE)
        wt[:, s * tok : (s + 1) * tok] = weight
        count = count + jnp.sum(named, axis=1, keepdims=True)


def route(meta, info, experts):
    tokens = len(meta) * meta[0].shape[1]
    table = jax.ShapeDtypeStruct((-(-experts // 8) * 8, tokens), jnp.float32)
    return pl.pallas_call(
        functools.partial(route_body, len(meta), experts),
        out_shape=(table, table),
        in_specs=[SMEM] + [VMEM] * len(meta),
        out_specs=(VMEM, VMEM),
        compiler_params=pltpu.CompilerParams(vmem_limit_bytes=40 << 20),
        name="route",
    )(info, *meta)


def backwards(l, n):
    bits = bits_of(n)
    return sum((((l >> b) & 1) << (len(bits) - 1 - b) for b in bits), 0 * l)


def units_of(l, info, n, width):
    return pl.ds(pl.multiple_of((backwards(l, n) ^ info[2]) * width, width), width)


def set_shape(need, weights):
    (_, depth, wide), (experts, side) = weights[0].shape, need
    return (len(experts), depth, wide) if side is None else (2, len(experts), depth, wide // 2)


def set_copies(need, weights, info, to, sem):
    experts, side = need
    if side is None:
        return [pltpu.make_async_copy(weights[0].at[e], to.at[x], sem.at[x]) for x, e in enumerate(experts)]
    half = to.shape[-1]
    units = pl.ds(pl.multiple_of(((info[1] & 1) ^ side) * half, half), half)
    return [
        pltpu.make_async_copy(w.at[e, :, units], to.at[m, x], sem.at[m * len(experts) + x])
        for m, w in enumerate(weights)
        for x, e in enumerate(experts)
    ]


def call(body, name, info, inputs, weights, ahead, after, outs, scratch, limit=24):
    n_in, n_out = len(inputs), len(outs)
    outs = list(outs)
    weights = [] if ahead is None else weights[2:] if ahead[1] is None else weights[:2]
    if ahead is not None:
        outs.append(jax.ShapeDtypeStruct(set_shape(ahead, weights), jnp.bfloat16))
        scratch = scratch + [pltpu.SemaphoreType.DMA((2 * len(ahead[0]),))]

    def whole(info, *refs):
        own, far = refs[:n_in], refs[n_in : n_in + len(weights)]
        rest = refs[n_in + len(weights) + len(after) :]
        results, rest = rest[: len(outs)], rest[len(outs) :]
        on = []
        if ahead is not None:
            on = set_copies(ahead, far, info, results[-1], rest[-1])
            rest = rest[:-1]
        body(info, own, results[:n_out], rest, lambda: [copy.start() for copy in on])
        for copy in on:
            copy.wait()

    return pl.pallas_call(
        whole,
        out_shape=tuple(outs),
        in_specs=[SMEM] + [spec for _, spec in inputs] + [HERE] * (len(weights) + len(after)),
        out_specs=(VMEM,) * len(outs),
        scratch_shapes=scratch,
        compiler_params=pltpu.CompilerParams(vmem_limit_bytes=limit << 20),
        cost_estimate=pl.CostEstimate(flops=1, bytes_accessed=1, transcendentals=0),
        name=name,
    )(info, *[x for x, _ in inputs], *weights, *after)


def stage(info, weights, need, after):
    body = lambda info, own, outs, rest, fetch: fetch()
    return call(body, "stage", info, [], weights, need, after, [], [], 40)[0]


def products(rows, given, to, info):
    most = rows.shape[0] // given.shape[1]
    shares, width = to.shape[0], to.shape[2] // 2
    for m in range(2):
        for x in range(given.shape[1]):
            mine = slice(x * most, (x + 1) * most)
            part = jnp.dot(rows[mine], given[m, x], preferred_element_type=jnp.float32)
            part = part.astype(jnp.bfloat16)
            for q in range(shares):
                j = backwards(q, shares) ^ (info[1] >> 1)
                to[j, mine, m * width : (m + 1) * width] = part[:, q * width : (q + 1) * width]


def send_body(experts, info, own, outs, rest, fetch):
    sources, rank, given = own[:-2], own[-2], own[-1]
    (to, rows), (feed, feed_sem) = outs, rest
    at, feeds = 0, []
    for s, source in enumerate(sources):
        tok = source.shape[0]
        feeds.append(pltpu.make_async_copy(source, feed.at[pl.ds(at, tok)], feed_sem.at[s]))
        at += tok
    for copy in feeds:
        copy.start()
    fetch()
    most = rows.shape[0] // len(experts)
    r = lax.broadcasted_iota(jnp.int32, (most, at), 0).astype(jnp.float32)
    pick = jnp.concatenate(
        [jnp.where(r == rank[e : e + 1, :], 1.0, 0.0).astype(jnp.bfloat16) for e in experts], axis=0
    )
    for copy in feeds:
        copy.wait()
    rows[...] = jnp.dot(pick, feed[...], preferred_element_type=jnp.float32).astype(jnp.bfloat16)
    products(rows, given, to, info)


def keep_body(info, own, outs, rest, fetch):
    fetch()
    rows, given = own
    products(rows, given, outs[0], info)


def part_shape(given, most, n_dp):
    _, experts, _, half = given.shape
    return jax.ShapeDtypeStruct((n_dp // 2, most * experts, 4 * half // n_dp), jnp.bfloat16)


def send_half(feeds, rank, info, given, weights, experts, most, n_dp, ahead, after):
    local = given.shape[2]
    rows = jax.ShapeDtypeStruct((most * len(experts), local), jnp.bfloat16)
    scratch = [
        pltpu.VMEM((rank.shape[1], local), jnp.bfloat16),
        pltpu.SemaphoreType.DMA((len(feeds),)),
    ]
    inputs = [(feed, HERE) for feed in feeds] + [(rank, VMEM), (given, VMEM)]
    outs = [part_shape(given, most, n_dp), rows]
    body = functools.partial(send_body, experts)
    return call(body, "send_half", info, inputs, weights, ahead, after, outs, scratch)


def keep_half(rows, info, given, weights, most, n_dp, ahead):
    inputs = [(rows, VMEM), (given, VMEM)]
    outs = [part_shape(given, most, n_dp)]
    return call(keep_body, "keep_half", info, inputs, weights, ahead, [], outs, [])


def down_body(lanes, experts, first, info, own, outs, rest, fetch):
    fetch()
    parts, (rank, wt, given) = own[: len(lanes)], own[len(lanes) : len(lanes) + 3]
    before = None if first else own[-1]
    hidden, mix, out = rest
    most = hidden.shape[0] // len(experts)
    width = parts[0].shape[-1]
    n_dp = hidden.shape[1] // width
    for part, (at, shares) in zip(parts, lanes):
        for j, l in enumerate(shares):
            hidden[:, units_of(l, info, n_dp, width)] = part[j, :, at : at + width]
    r = lax.broadcasted_iota(jnp.int32, (most, mix.shape[1]), 0).astype(jnp.float32)
    for x, e in enumerate(experts):
        mix[x * most : (x + 1) * most, :] = jnp.where(
            r == rank[e : e + 1, :], wt[e : e + 1, :], 0.0
        ).astype(jnp.bfloat16)
    local = out.shape[1]
    block = local // 2 if local % 512 == 0 else 256 if local % 256 == 0 else local
    for i in range(local // block):
        cols = slice(i * block, (i + 1) * block)
        for x in range(len(experts)):
            mine = slice(x * most, (x + 1) * most)
            out[mine, cols] = jnp.dot(
                hidden[mine], given[x, :, cols], preferred_element_type=jnp.float32
            ).astype(jnp.bfloat16)
        total = lax.dot_general(
            mix[...], out[:, cols], (((0,), (0,)), ((), ())), preferred_element_type=jnp.float32
        )
        if not first:
            total = total + before[:, cols]
        at = 0
        for to in outs:
            to[:, cols] = total[at : at + to.shape[0]].astype(to.dtype)
            at += to.shape[0]


def down(parts, rank, wt, info, given, weights, total, experts, cuts, ahead, after):
    parts, lanes = [part for part, *_ in parts], [tuple(where) for _, *where in parts]
    rows = parts[0].shape[1]
    _, hidden, local = given.shape
    kind = jnp.bfloat16 if len(cuts) > 1 else jnp.float32
    before = [] if total is None else [total]
    outs = [jax.ShapeDtypeStruct((cut, local), kind) for cut in cuts]
    scratch = [
        pltpu.VMEM((rows, hidden), jnp.bfloat16),
        pltpu.VMEM((rows, rank.shape[1]), jnp.bfloat16),
        pltpu.VMEM((rows, local), jnp.bfloat16),
    ]
    inputs = [(x, VMEM) for x in (*parts, rank, wt, given, *before)]
    body = functools.partial(down_body, lanes, experts, total is None)
    return call(body, "down", info, inputs, weights, ahead, after, outs, scratch)


def finish(total, late, after):
    if after:
        late, *_ = lax.optimization_barrier((late, *after))
    gate_up = total + late.astype(jnp.float32)
    width = gate_up.shape[2] // 2
    return (jax.nn.silu(gate_up[:, :, :width]) * gate_up[:, :, width:]).astype(jnp.bfloat16)


def chip_sums(send, keep, bits):
    total = keep.astype(jnp.float32) + flip(send, "dp", 1).astype(jnp.float32)
    for b in bits[1:-1]:
        total = total[0::2] + flip(total[1::2].astype(jnp.bfloat16), "dp", 1 << b).astype(jnp.float32)
    return total[0::2], total[1::2].astype(jnp.bfloat16)


def everyone_s(share, other, at, bits):
    width = share.shape[2]
    top = 1 << bits[-1]
    parts = [(share, 0, [0]), (other, at, [top])]
    held, whose = jnp.concatenate([share, other[:, :, at : at + width]], axis=0), [0, top]
    for b in reversed(bits[:-1]):
        theirs = flip(held, "dp", 1 << b)
        parts.append((theirs, 0, [l | 1 << b for l in whose]))
        if b > 0:
            held, whose = jnp.concatenate([held, theirs], axis=0), whose + parts[-1][2]
    return parts


def on_device(tokens, expert_ids, scores, w_gate, w_up, w_down):
    n_owner, n_dp = lax.axis_size("expert"), lax.axis_size("dp")
    tok_rows, top = expert_ids.shape
    experts = w_gate.shape[0]
    capacity = 2 * tok_rows * top // (experts * n_owner)
    per_chunk = 2 if experts % 2 == 0 else 1
    most = n_owner * capacity
    chunks = experts // per_chunk

    meta = jnp.concatenate([expert_ids.T.astype(jnp.float32), scores.T], axis=0)
    me = lax.axis_index("dp").astype(jnp.int32)
    first = lax.axis_index("expert").astype(jnp.int32) * experts
    info = jnp.stack([first, me, backwards(me, n_dp)])
    of = lambda c: list(range(c * per_chunk, (c + 1) * per_chunk))
    weights = (w_gate, w_up, w_down)
    needs = [(of(c), side) for c in range(chunks) for side in (1, 0)] + [(of(c), None) for c in range(chunks)]
    given = {0: stage(info, weights, needs[0], [])}

    def fetched(k, outs):
        if k + 1 < len(needs):
            *outs, given[k + 1] = outs
        return outs

    ahead = lambda k: needs[k + 1] if k + 1 < len(needs) else None

    metas = [meta] + [
        lax.ppermute(meta, "expert", [(i, (i - k) % n_owner) for i in range(n_owner)])
        for k in gathered_order(n_owner)[1:]
    ]
    feeds = gathered(tokens, "expert")
    rank, wt = route(metas, info, experts)

    tall, wide = [tok_rows] + [tok_rows // 2] * (2 * n_owner - 2), tokens.shape[1]
    bits = bits_of(n_dp)
    cross = 1 << bits[-1]
    sent, parts, total = [], [], None
    share = kept = late = None

    def add(c, after):
        k, cuts = 2 * chunks + c, tall if c == chunks - 1 else [sum(tall)]
        outs = down(parts[c], rank, wt, info, given[k], weights, total, of(c), cuts, ahead(k), after)
        outs = fetched(k, outs)
        return outs if c == chunks - 1 else outs[0]

    for c in range(chunks):
        last = c == chunks - 1
        k = 2 * c
        send, rows = fetched(
            k, send_half(feeds, rank, info, given[k], weights, of(c), most, n_dp, ahead(k), sent[-1:])
        )
        k = 2 * c + 1
        (keep,) = fetched(k, keep_half(rows, info, given[k], weights, most, n_dp, ahead(k)))
        before, behind = kept, late
        kept, out = chip_sums(send, keep, bits)
        width = out.shape[2]
        if c > 0:
            share = finish(before, behind[:, :, :width], [])
            out = jnp.concatenate([out, share], axis=2)
        sent.append(out)
        late = flip(out, "dp", cross)
        if c > 0:
            parts.append(everyone_s(share, late, width, bits))
        if last:
            for d in range(min(c - 1, 2)):
                total = add(d, [out] if d == 0 else [])
    share = finish(kept, late[:, :, :width], [] if total is None else [total])
    other = flip(share, "dp", cross)
    for c in range(max(min(chunks - 2, 2), 0), chunks - 1):
        total = add(c, [share])
    if total is not None:
        other = lax.optimization_barrier((other, total))[0]
    parts.append(everyone_s(share, other, 0, bits))
    total = add(chunks - 1, [])
    return returned(total, "expert").astype(jnp.bfloat16)


def gathered_order(n):
    near = [d for s in range(1, n // 2) for d in (-s, s)]
    return [0] + near + ([n // 2] if n > 1 else [])


def ways(n):
    return [(i, (i + 1) % n) for i in range(n)], [(i, (i - 1) % n) for i in range(n)]


def gathered(x, axis):
    n = lax.axis_size(axis)
    up, down_ = [(i, (i + 1) % n) for i in range(n)], [(i, (i - 1) % n) for i in range(n)]
    below = above = x
    found = [x]
    for _ in range(1, n // 2):
        below, above = lax.ppermute(below, axis, up), lax.ppermute(above, axis, down_)
        found += [below, above]
    if n > 1:
        half = x.shape[0] // 2
        found += [lax.ppermute(below[:half], axis, up), lax.ppermute(above[half:], axis, down_)]
    return found


def returned(partials, axis):
    n = lax.axis_size(axis)
    up, down_ = ways(n)
    wide = lambda x: x.astype(jnp.float32)
    mixed = wide(partials[0])
    if n == 1:
        return mixed
    half = mixed.shape[0] // 2

    def hop(there, partial, perm):
        total = partial if there is None else (wide(partial) + wide(there)).astype(jnp.bfloat16)
        return lax.ppermute(total, axis, perm)

    low = [hop(None, partials[-2], down_), None]
    high = [None, hop(None, partials[-1], up)]
    for s in range(n // 2 - 1, 0, -1):
        near = partials[4 * s - 3 : 4 * s + 1]
        low = [hop(low[0], near[0], down_), hop(low[1], near[1], down_)]
        high = [hop(high[0], near[2], up), hop(high[1], near[3], up)]
    halves = []
    for h, own in enumerate((mixed[:half], mixed[half:])):
        for there in (low[h], high[h]):
            own = own if there is None else own + wide(there)
        halves.append(own)
    return jnp.concatenate(halves, axis=0)


def solution(mesh):
    in_specs = (
        P(("groups", "expert"), "dp"),
        P(("groups", "expert"), None),
        P(("groups", "expert"), None),
        P("expert", "dp", None),
        P("expert", "dp", None),
        P("expert", None, "dp"),
    )
    out_specs = P(("groups", "expert"), "dp")
    return jax.shard_map(
        on_device, mesh=mesh, in_specs=in_specs, out_specs=out_specs, check_vma=False
    )
```

```python
import functools

import jax
import jax.numpy as jnp
from jax import lax
from jax.experimental import pallas as pl
from jax.experimental.pallas import tpu as pltpu
from jax.sharding import PartitionSpec as P

LANES = 128
VMEM = pl.BlockSpec(memory_space=pltpu.VMEM)
SMEM = pl.BlockSpec(memory_space=pltpu.SMEM)
HERE = pl.BlockSpec(memory_space=pl.ANY)
FAR = pl.BlockSpec(memory_space=pltpu.HBM)
NOWHERE = -1e6


def bits_of(n):
    return [b for b in range(n.bit_length() - 1)]


def flip(x, axis, k):
    return lax.ppermute(x, axis, [(i, i ^ k) for i in range(lax.axis_size(axis))])


def route_body(n, experts, info, *refs):
    meta, (rank, wt) = refs[:n], refs[n:]
    tok, top = meta[0].shape[1], meta[0].shape[0] // 2
    padded = rank.shape[0]
    first = info[0].astype(jnp.float32)
    e = lax.broadcasted_iota(jnp.int32, (padded, tok), 0).astype(jnp.float32)
    before = (
        lax.broadcasted_iota(jnp.int32, (tok, tok), 0) < lax.broadcasted_iota(jnp.int32, (tok, tok), 1)
    ).astype(jnp.bfloat16)
    count = jnp.zeros((padded, 1), jnp.float32)
    for s in range(n):
        ids, scores = meta[s][:top], meta[s][top:]
        affinity = 1.0 / (1.0 + jnp.exp(-scores))
        share = 2.5 * affinity / jnp.sum(affinity, axis=0, keepdims=True)
        named = jnp.zeros((padded, tok), jnp.float32)
        weight = jnp.zeros((padded, tok), jnp.float32)
        for k in range(top):
            hit = jnp.where(ids[k : k + 1] - first == e, 1.0, 0.0)
            named = named + hit
            weight = weight + hit * share[k : k + 1]
        named = jnp.where(e < experts, named, 0.0)
        place = jnp.dot(named.astype(jnp.bfloat16), before, preferred_element_type=jnp.float32) + count
        rank[:, s * tok : (s + 1) * tok] = jnp.where(named > 0, place, NOWHERE)
        wt[:, s * tok : (s + 1) * tok] = weight
        count = count + jnp.sum(named, axis=1, keepdims=True)


def route(meta, info, experts):
    tokens = len(meta) * meta[0].shape[1]
    table = jax.ShapeDtypeStruct((-(-experts // 8) * 8, tokens), jnp.float32)
    return pl.pallas_call(
        functools.partial(route_body, len(meta), experts),
        out_shape=(table, table),
        in_specs=[SMEM] + [VMEM] * len(meta),
        out_specs=(VMEM, VMEM),
        compiler_params=pltpu.CompilerParams(vmem_limit_bytes=40 << 20),
        name="route",
    )(info, *meta)


def backwards(l, n):
    bits = bits_of(n)
    return sum((((l >> b) & 1) << (len(bits) - 1 - b) for b in bits), 0 * l)


def units_of(l, info, n, width):
    return pl.ds(pl.multiple_of((backwards(l, n) ^ info[2]) * width, width), width)


def set_shape(need, weights):
    (_, depth, wide), (experts, side) = weights[0].shape, need
    return (len(experts), depth, wide) if side is None else (2, len(experts), depth, wide // 2)


def set_copies(need, weights, info, to, sem):
    experts, side = need
    if side is None:
        return [pltpu.make_async_copy(weights[0].at[e], to.at[x], sem.at[x]) for x, e in enumerate(experts)]
    half = to.shape[-1]
    units = pl.ds(pl.multiple_of(((info[1] & 1) ^ side) * half, half), half)
    return [
        pltpu.make_async_copy(w.at[e, :, units], to.at[m, x], sem.at[m * len(experts) + x])
        for m, w in enumerate(weights)
        for x, e in enumerate(experts)
    ]


def call(body, name, info, inputs, weights, ahead, after, outs, scratch, limit=24):
    n_in, n_out = len(inputs), len(outs)
    outs = list(outs)
    weights = [] if ahead is None else weights[2:] if ahead[1] is None else weights[:2]
    if ahead is not None:
        outs.append(jax.ShapeDtypeStruct(set_shape(ahead, weights), jnp.bfloat16))
        scratch = scratch + [pltpu.SemaphoreType.DMA((2 * len(ahead[0]),))]

    def whole(info, *refs):
        own, far = refs[:n_in], refs[n_in : n_in + len(weights)]
        rest = refs[n_in + len(weights) + len(after) :]
        results, rest = rest[: len(outs)], rest[len(outs) :]
        on = []
        if ahead is not None:
            on = set_copies(ahead, far, info, results[-1], rest[-1])
            rest = rest[:-1]
        body(info, own, results[:n_out], rest, lambda: [copy.start() for copy in on])
        for copy in on:
            copy.wait()

    return pl.pallas_call(
        whole,
        out_shape=tuple(outs),
        in_specs=[SMEM] + [spec for _, spec in inputs] + [HERE] * (len(weights) + len(after)),
        out_specs=(VMEM,) * len(outs),
        scratch_shapes=scratch,
        compiler_params=pltpu.CompilerParams(vmem_limit_bytes=limit << 20),
        cost_estimate=pl.CostEstimate(flops=1, bytes_accessed=1, transcendentals=0),
        name=name,
    )(info, *[x for x, _ in inputs], *weights, *after)


def stage(info, weights, need, after):
    body = lambda info, own, outs, rest, fetch: fetch()
    return call(body, "stage", info, [], weights, need, after, [], [], 40)[0]


def products(rows, given, to, info):
    most = rows.shape[0] // given.shape[1]
    shares, width = to.shape[0], to.shape[2] // 2
    for m in range(2):
        for x in range(given.shape[1]):
            mine = slice(x * most, (x + 1) * most)
            part = jnp.dot(rows[mine], given[m, x], preferred_element_type=jnp.float32)
            part = part.astype(jnp.bfloat16)
            for q in range(shares):
                j = backwards(q, shares) ^ (info[1] >> 1)
                to[j, mine, m * width : (m + 1) * width] = part[:, q * width : (q + 1) * width]


def send_body(experts, info, own, outs, rest, fetch):
    sources, rank, given = own[:-2], own[-2], own[-1]
    (to, rows), (feed, feed_sem) = outs, rest
    at, feeds = 0, []
    for s, source in enumerate(sources):
        tok = source.shape[0]
        feeds.append(pltpu.make_async_copy(source, feed.at[pl.ds(at, tok)], feed_sem.at[s]))
        at += tok
    for copy in feeds:
        copy.start()
    fetch()
    most = rows.shape[0] // len(experts)
    r = lax.broadcasted_iota(jnp.int32, (most, at), 0).astype(jnp.float32)
    pick = jnp.concatenate(
        [jnp.where(r == rank[e : e + 1, :], 1.0, 0.0).astype(jnp.bfloat16) for e in experts], axis=0
    )
    for copy in feeds:
        copy.wait()
    rows[...] = jnp.dot(pick, feed[...], preferred_element_type=jnp.float32).astype(jnp.bfloat16)
    products(rows, given, to, info)


def keep_body(info, own, outs, rest, fetch):
    fetch()
    rows, given = own
    products(rows, given, outs[0], info)


def part_shape(given, most, n_dp):
    _, experts, _, half = given.shape
    return jax.ShapeDtypeStruct((n_dp // 2, most * experts, 4 * half // n_dp), jnp.bfloat16)


def send_half(feeds, rank, info, given, weights, experts, most, n_dp, ahead, after):
    local = given.shape[2]
    rows = jax.ShapeDtypeStruct((most * len(experts), local), jnp.bfloat16)
    scratch = [
        pltpu.VMEM((rank.shape[1], local), jnp.bfloat16),
        pltpu.SemaphoreType.DMA((len(feeds),)),
    ]
    inputs = [(feed, HERE) for feed in feeds] + [(rank, VMEM), (given, VMEM)]
    outs = [part_shape(given, most, n_dp), rows]
    body = functools.partial(send_body, experts)
    return call(body, "send_half", info, inputs, weights, ahead, after, outs, scratch)


def keep_half(rows, info, given, weights, most, n_dp, ahead):
    inputs = [(rows, VMEM), (given, VMEM)]
    outs = [part_shape(given, most, n_dp)]
    return call(keep_body, "keep_half", info, inputs, weights, ahead, [], outs, [])


def down_body(lanes, experts, first, info, own, outs, rest, fetch):
    fetch()
    parts, (rank, wt, given) = own[: len(lanes)], own[len(lanes) : len(lanes) + 3]
    before = None if first else own[-1]
    hidden, mix, out = rest
    most = hidden.shape[0] // len(experts)
    width = parts[0].shape[-1]
    n_dp = hidden.shape[1] // width
    for part, (at, shares) in zip(parts, lanes):
        for j, l in enumerate(shares):
            hidden[:, units_of(l, info, n_dp, width)] = part[j, :, at : at + width]
    r = lax.broadcasted_iota(jnp.int32, (most, mix.shape[1]), 0).astype(jnp.float32)
    for x, e in enumerate(experts):
        mix[x * most : (x + 1) * most, :] = jnp.where(
            r == rank[e : e + 1, :], wt[e : e + 1, :], 0.0
        ).astype(jnp.bfloat16)
    local = out.shape[1]
    block = local
    for i in range(local // block):
        cols = slice(i * block, (i + 1) * block)
        for x in range(len(experts)):
            mine = slice(x * most, (x + 1) * most)
            out[mine, cols] = jnp.dot(
                hidden[mine], given[x, :, cols], preferred_element_type=jnp.float32
            ).astype(jnp.bfloat16)
        total = lax.dot_general(
            mix[...], out[:, cols], (((0,), (0,)), ((), ())), preferred_element_type=jnp.float32
        )
        if not first:
            total = total + before[:, cols]
        at = 0
        for to in outs:
            to[:, cols] = total[at : at + to.shape[0]].astype(to.dtype)
            at += to.shape[0]


def down(parts, rank, wt, info, given, weights, total, experts, cuts, ahead, after):
    parts, lanes = [part for part, *_ in parts], [tuple(where) for _, *where in parts]
    rows = parts[0].shape[1]
    _, hidden, local = given.shape
    kind = jnp.bfloat16 if len(cuts) > 1 else jnp.float32
    before = [] if total is None else [total]
    outs = [jax.ShapeDtypeStruct((cut, local), kind) for cut in cuts]
    scratch = [
        pltpu.VMEM((rows, hidden), jnp.bfloat16),
        pltpu.VMEM((rows, rank.shape[1]), jnp.bfloat16),
        pltpu.VMEM((rows, local), jnp.bfloat16),
    ]
    inputs = [(x, VMEM) for x in (*parts, rank, wt, given, *before)]
    body = functools.partial(down_body, lanes, experts, total is None)
    return call(body, "down", info, inputs, weights, ahead, after, outs, scratch)


def finish(total, late, after):
    if after:
        late, *_ = lax.optimization_barrier((late, *after))
    gate_up = total + late.astype(jnp.float32)
    width = gate_up.shape[2] // 2
    return (jax.nn.silu(gate_up[:, :, :width]) * gate_up[:, :, width:]).astype(jnp.bfloat16)


def chip_sums(send, keep, bits):
    total = keep.astype(jnp.float32) + flip(send, "dp", 1).astype(jnp.float32)
    for b in bits[1:-1]:
        total = total[0::2] + flip(total[1::2].astype(jnp.bfloat16), "dp", 1 << b).astype(jnp.float32)
    return total[0::2], total[1::2].astype(jnp.bfloat16)


def everyone_s(share, other, at, bits):
    width = share.shape[2]
    top = 1 << bits[-1]
    parts = [(share, 0, [0]), (other, at, [top])]
    held, whose = jnp.concatenate([share, other[:, :, at : at + width]], axis=0), [0, top]
    for b in reversed(bits[:-1]):
        theirs = flip(held, "dp", 1 << b)
        parts.append((theirs, 0, [l | 1 << b for l in whose]))
        if b > 0:
            held, whose = jnp.concatenate([held, theirs], axis=0), whose + parts[-1][2]
    return parts


def on_device(tokens, expert_ids, scores, w_gate, w_up, w_down):
    n_owner, n_dp = lax.axis_size("expert"), lax.axis_size("dp")
    tok_rows, top = expert_ids.shape
    experts = w_gate.shape[0]
    capacity = 2 * tok_rows * top // (experts * n_owner)
    per_chunk = 2 if experts % 2 == 0 else 1
    most = n_owner * capacity
    chunks = experts // per_chunk

    meta = jnp.concatenate([expert_ids.T.astype(jnp.float32), scores.T], axis=0)
    me = lax.axis_index("dp").astype(jnp.int32)
    first = lax.axis_index("expert").astype(jnp.int32) * experts
    info = jnp.stack([first, me, backwards(me, n_dp)])
    of = lambda c: list(range(c * per_chunk, (c + 1) * per_chunk))
    weights = (w_gate, w_up, w_down)
    needs = [(of(c), side) for c in range(chunks) for side in (1, 0)] + [(of(c), None) for c in range(chunks)]
    given = {0: stage(info, weights, needs[0], [])}

    def fetched(k, outs):
        if k + 1 < len(needs):
            *outs, given[k + 1] = outs
        return outs

    ahead = lambda k: needs[k + 1] if k + 1 < len(needs) else None

    metas = [meta] + [
        lax.ppermute(meta, "expert", [(i, (i - k) % n_owner) for i in range(n_owner)])
        for k in gathered_order(n_owner)[1:]
    ]
    feeds = gathered(tokens, "expert")
    rank, wt = route(metas, info, experts)

    tall, wide = [tok_rows] + [tok_rows // 2] * (2 * n_owner - 2), tokens.shape[1]
    bits = bits_of(n_dp)
    cross = 1 << bits[-1]
    sent, parts, total = [], [], None
    share = kept = late = None

    def add(c, after):
        k, cuts = 2 * chunks + c, tall if c == chunks - 1 else [sum(tall)]
        outs = down(parts[c], rank, wt, info, given[k], weights, total, of(c), cuts, ahead(k), after)
        outs = fetched(k, outs)
        return outs if c == chunks - 1 else outs[0]

    for c in range(chunks):
        last = c == chunks - 1
        k = 2 * c
        send, rows = fetched(
            k, send_half(feeds, rank, info, given[k], weights, of(c), most, n_dp, ahead(k), sent[-1:])
        )
        k = 2 * c + 1
        (keep,) = fetched(k, keep_half(rows, info, given[k], weights, most, n_dp, ahead(k)))
        before, behind = kept, late
        kept, out = chip_sums(send, keep, bits)
        width = out.shape[2]
        if c > 0:
            share = finish(before, behind[:, :, :width], [])
            out = jnp.concatenate([out, share], axis=2)
        sent.append(out)
        late = flip(out, "dp", cross)
        if c > 0:
            parts.append(everyone_s(share, late, width, bits))
        if last:
            for d in range(min(c - 1, 2)):
                total = add(d, [out] if d == 0 else [])
    share = finish(kept, late[:, :, :width], [] if total is None else [total])
    other = flip(share, "dp", cross)
    for c in range(max(min(chunks - 2, 2), 0), chunks - 1):
        total = add(c, [share])
    if total is not None:
        other = lax.optimization_barrier((other, total))[0]
    parts.append(everyone_s(share, other, 0, bits))
    total = add(chunks - 1, [])
    return returned(total, "expert").astype(jnp.bfloat16)


def gathered_order(n):
    near = [d for s in range(1, n // 2) for d in (-s, s)]
    return [0] + near + ([n // 2] if n > 1 else [])


def ways(n):
    return [(i, (i + 1) % n) for i in range(n)], [(i, (i - 1) % n) for i in range(n)]


def gathered(x, axis):
    n = lax.axis_size(axis)
    up, down_ = [(i, (i + 1) % n) for i in range(n)], [(i, (i - 1) % n) for i in range(n)]
    below = above = x
    found = [x]
    for _ in range(1, n // 2):
        below, above = lax.ppermute(below, axis, up), lax.ppermute(above, axis, down_)
        found += [below, above]
    if n > 1:
        half = x.shape[0] // 2
        found += [lax.ppermute(below[:half], axis, up), lax.ppermute(above[half:], axis, down_)]
    return found


def returned(partials, axis):
    n = lax.axis_size(axis)
    up, down_ = ways(n)
    wide = lambda x: x.astype(jnp.float32)
    mixed = wide(partials[0])
    if n == 1:
        return mixed
    half = mixed.shape[0] // 2

    def hop(there, partial, perm):
        total = partial if there is None else (wide(partial) + wide(there)).astype(jnp.bfloat16)
        return lax.ppermute(total, axis, perm)

    low = [hop(None, partials[-2], down_), None]
    high = [None, hop(None, partials[-1], up)]
    for s in range(n // 2 - 1, 0, -1):
        near = partials[4 * s - 3 : 4 * s + 1]
        low = [hop(low[0], near[0], down_), hop(low[1], near[1], down_)]
        high = [hop(high[0], near[2], up), hop(high[1], near[3], up)]
    halves = []
    for h, own in enumerate((mixed[:half], mixed[half:])):
        for there in (low[h], high[h]):
            own = own if there is None else own + wide(there)
        halves.append(own)
    return jnp.concatenate(halves, axis=0)


def solution(mesh):
    in_specs = (
        P(("groups", "expert"), "dp"),
        P(("groups", "expert"), None),
        P(("groups", "expert"), None),
        P("expert", "dp", None),
        P("expert", "dp", None),
        P("expert", None, "dp"),
    )
    out_specs = P(("groups", "expert"), "dp")
    return jax.shard_map(
        on_device, mesh=mesh, in_specs=in_specs, out_specs=out_specs, check_vma=False
    )
```
